256 devices in a mesh: tok: 8 (over z_lo, y), row: 32 (over x, z_hi, core).
Axes of the slice: x: 4, y: 4, z: 8 (z_hi: 4, z_lo: 2; z = z_hi * 2 + z_lo), core: 2. Of those that a mesh axis runs over, the one named last changes fastest.
Arguments:
- token_ids: int32 [4096], P('tok'), may hold values from 1 to 50271, as said below
- calib_input: bfloat16 [4096, 49152], P('tok', 'row'), may hold values from -6 to 6
- keep_mask: int32 [12288, 256], P('row'), may hold values from 0 to 1, as said below
- weight_window: float32 [12288, 256], P('row'), may hold values from -0.12 to 0.12
- weight_rest: bfloat16 [12288, 48896], P('row', 'tok'), may hold values from -1.5 to 1.5
- factor_window: float32 [256, 256], replicated, as said below
- factor_rest: float32 [256, 48896], P('row', 'tok'), may hold values from -0.72 to 0.72
Outputs:
- pruned_window: float32 [12288, 256], P('row')
- updated_rest: bfloat16 [12288, 48896], P('row', 'tok')
- hessian_rows: float32 [256, 49152], P('tok', 'row')
- window_outputs: bfloat16 [4096, 12288], P(('tok', 'row'))
The draws below stay inside these ranges and needn't reach their ends.
Inputs may be any that keep to these rules, and one draw needn't show every extreme that they name: `token_ids`: tokens form sequences of 128 positions; in each, live ids of 2 or more come first, then at least one padding id 1. `keep_mask`: in every row, each aligned group of 4 consecutive columns holds exactly two ones. `factor_window`: zero below the diagonal; diagonal entries positive.
All inputs are finite; a program needn't handle non-finite values.
Results may differ from the reference program's by a relative error of at most 0.011.
Values may be sent and summed in bfloat16 or wider, within the bound.
A program may use at most 64 MiB of HBM per device.

```python
import jax
import jax.numpy as jnp
import numpy as np
from jax import lax

ROWS = 12288
COLS = 49152
VOCAB = 50272
BLOCK = 128
NBLK = 2
WIN = 256
REST = 48896
TOKENS = 4096
SEQ = 128
N_ROW = 32


def draw_token_ids(key, part):
    key = jax.random.fold_in(key, 11)
    id_key, length_key = jax.random.split(key)
    seq_count = TOKENS // SEQ
    live_ids = jax.random.randint(id_key, (seq_count, SEQ), 2, VOCAB)
    live_ids = live_ids.at[0, 0].set(VOCAB - 1)
    lengths = jax.random.randint(length_key, (seq_count, 1), SEQ // 2, SEQ)
    position = jnp.arange(SEQ)[None, :]
    padded = jnp.where(position < lengths, live_ids, 1)
    return padded.reshape(TOKENS).astype(jnp.int32)


def draw_keep_mask(key, part):
    key = jax.random.fold_in(key, 12)
    patterns = jnp.asarray(np.array([[1, 1, 0, 0], [1, 0, 1, 0], [1, 0, 0, 1], [0, 1, 1, 0], [0, 1, 0, 1], [0, 0, 1, 1]], dtype=np.int32))
    pattern_ids = jax.random.randint(key, (ROWS, WIN // 4), 0, 6)
    return patterns[pattern_ids].reshape(ROWS, WIN).astype(jnp.int32)


def draw_factor_window(key, part):
    key = jax.random.fold_in(key, 13)
    diag_key, off_key = jax.random.split(key)
    diagonal = jnp.exp(jax.random.uniform(diag_key, (WIN,), jnp.float32, jnp.log(0.5), jnp.log(2.0)))
    above = jnp.clip(jax.random.normal(off_key, (WIN, WIN), jnp.float32), -4.0, 4.0)
    row_index = jnp.arange(WIN)[:, None]
    col_index = jnp.arange(WIN)[None, :]
    same_block = row_index // BLOCK == col_index // BLOCK
    spread = jnp.where(same_block, 0.3, 0.03)
    shared_part = jnp.where(same_block, 0.5 * diagonal[None, :], 0.0)
    upper = jnp.where(col_index > row_index, spread * above + shared_part, 0.0)
    return (upper + jnp.diag(diagonal)).astype(jnp.float32)


def block_levels(stream_key, extent, cuts, smallest, largest):
    factor_of, own = 1.0, jax.random.fold_in(stream_key, 6)
    for dim, shards_of in cuts:
        heights = jnp.exp(jax.random.uniform(jax.random.fold_in(own, dim), (shards_of,), jnp.float32, smallest / len(cuts), largest / len(cuts)))
        factor_of = factor_of * jnp.repeat(heights, extent[dim] // shards_of).reshape([-1 if axis == dim else 1 for axis in range(len(extent))])
    return factor_of


def noise(rng, shape, scale, most, cuts=(), kind=jnp.bfloat16):
    values = jax.random.normal(rng, shape, jnp.float32) * scale
    if len(cuts) > 0:
        values = block_levels(rng, shape, cuts, -0.22, 0.18) * values
    return jnp.clip(values, min=-most, max=most).astype(kind)


def setup_inputs(seed: int = 0) -> dict:
    streams_of = jax.random.split(jax.random.key(seed), 8)
    return {
        "token_ids": draw_token_ids(jax.random.fold_in(streams_of[7], 71), 0),
        "calib_input": noise(streams_of[1], (TOKENS, COLS), 1.0, 6.0, ((0, 8), (1, 32))),
        "keep_mask": draw_keep_mask(jax.random.fold_in(streams_of[7], 71), 0),
        "weight_window": noise(streams_of[3], (ROWS, WIN), 0.02, 0.12, ((0, 32),), jnp.float32),
        "weight_rest": noise(streams_of[4], (ROWS, REST), 0.25, 1.5, ((0, 32), (1, 8))),
        "factor_window": draw_factor_window(jax.random.fold_in(streams_of[7], 71), 0),
        "factor_rest": noise(streams_of[6], (WIN, REST), 0.12, 0.72, ((0, 32), (1, 8)), jnp.float32),
    }


def prune_block(weights, keep_float, factor_block):
    def advance(column, state_pair):
        current, errors = state_pair
        values = lax.dynamic_slice_in_dim(current, column, 1, 1)
        kept = lax.dynamic_slice_in_dim(keep_float, column, 1, 1)
        factor_row = lax.dynamic_slice_in_dim(factor_block, column, 1, 0)
        pivot = lax.dynamic_slice_in_dim(factor_row, column, 1, 1)
        error_col = values * (1.0 - kept) / pivot
        current = current - error_col * factor_row
        errors = lax.dynamic_update_slice_in_dim(errors, error_col, column, 1)
        return current, errors

    start_errors = jnp.zeros(weights.shape, jnp.float32)
    return lax.fori_loop(0, weights.shape[1], advance, (weights, start_errors))


def prune_window(weights, keep_float, factor_window):
    pruned_blocks = []
    error_blocks = []
    for block_index in range(NBLK):
        low_col = block_index * BLOCK
        high_col = low_col + BLOCK
        pruned_block, error_block = prune_block(weights[:, low_col:high_col], keep_float[:, low_col:high_col], factor_window[low_col:high_col, low_col:high_col])
        if high_col < weights.shape[1]:
            later = weights[:, high_col:] - jnp.dot(error_block, factor_window[low_col:high_col, high_col:], precision=lax.Precision.HIGHEST, preferred_element_type=jnp.float32)
            weights = jnp.concatenate([weights[:, :high_col], later], axis=1)
        pruned_blocks.append(pruned_block)
        error_blocks.append(error_block)
    return jnp.concatenate(pruned_blocks, axis=1), jnp.concatenate(error_blocks, axis=1)


def reference(token_ids, calib_input, keep_mask, weight_window, weight_rest, factor_window, factor_rest):
    live_mask = (token_ids != 1).astype(jnp.bfloat16)
    window_inputs = calib_input[:, :WIN] * live_mask[:, None]
    gram = lax.dot_general(window_inputs, calib_input, (((0,), (0,)), ((), ())), preferred_element_type=jnp.float32)
    hessian_rows = gram * (2.0 / TOKENS)
    pruned_window, errors = prune_window(weight_window, keep_mask.astype(jnp.float32), factor_window)

    def compensate(pair):
        rest_rows, error_rows = pair
        change = jnp.dot(error_rows, factor_rest, precision=lax.Precision.HIGHEST, preferred_element_type=jnp.float32)
        return (rest_rows.astype(jnp.float32) - change).astype(jnp.bfloat16)

    rest_blocks = weight_rest.reshape(N_ROW, ROWS // N_ROW, REST)
    error_stack = errors.reshape(N_ROW, ROWS // N_ROW, WIN)
    updated_rest = lax.map(compensate, (rest_blocks, error_stack)).reshape(ROWS, REST)
    pruned_half = pruned_window.astype(jnp.bfloat16)
    window_outputs = lax.dot_general(window_inputs, pruned_half, (((1,), (1,)), ((), ())), preferred_element_type=jnp.float32).astype(jnp.bfloat16)
    return (pruned_window, updated_rest, hessian_rows, window_outputs)
```

```python
import functools

import jax
import jax.numpy as jnp
from jax import lax
from jax.experimental import pallas as pl
from jax.experimental.pallas import tpu as pltpu
from jax.sharding import PartitionSpec as P

MESH = pl.DeviceIdType.MESH
F32, BF16 = jnp.float32, jnp.bfloat16

WIN = 256
BLOCK = 128
SUB = 8
LOCAL_ROWS = 384
LOCAL_TOKENS = 512
FEATURES = 1536
REST = 6112
HALF = 3072
N_ROW = 32
N_TOK = 8
CHIPS = 16
TOKENS = LOCAL_TOKENS * N_TOK

PHASES = 2
PHASE_COLS = HALF // PHASES
PIECE = PHASE_COLS // 2

Z_UP, Z_DOWN, Z_UP_PIECE, Z_DOWN_PIECE = 0, 1, 2, 3
X_FIRST = 4
PAIR_FIRST = 20
F_MESSAGES = 36


def prune_prepare(ww, kp, fw, cur, scaled_drop, fw_t):
    factor = fw[...]
    fw_t[...] = factor.T
    row_id = lax.broadcasted_iota(jnp.int32, (WIN, WIN), 0)
    col_id = lax.broadcasted_iota(jnp.int32, (WIN, WIN), 1)
    diagonal = jnp.sum(jnp.where(row_id == col_id, factor, 0.0), axis=1, keepdims=True)
    drop = (1 - kp[...]).astype(F32).T
    scaled_drop[...] = drop * (1.0 / diagonal)
    cur[...] = ww[...].T


def prune_tile(k, cur, scaled_drop, fw_t, err):
    low = k * SUB
    block_end = (low // BLOCK + 1) * BLOCK
    tile = cur[low : low + SUB, :]
    drop = scaled_drop[low : low + SUB, :]
    rows = []
    for s in range(SUB):
        e = tile[s : s + 1, :] * drop[s : s + 1, :]
        rows.append(e)
        tile = tile - fw_t[low : low + SUB, low + s : low + s + 1] * e
    cur[low : low + SUB, :] = tile
    err[low : low + SUB, :] = jnp.concatenate(rows, axis=0)
    start = low + SUB
    while start < block_end:
        end = min(start + 32, block_end)
        part = cur[start:end, :]
        for s in range(SUB):
            part = part - fw_t[start:end, low + s : low + s + 1] * rows[s]
        cur[start:end, :] = part
        start = end
    if block_end == low + SUB and block_end < WIN:
        b = block_end - BLOCK
        cur[block_end:, :] = cur[block_end:, :] - jnp.dot(
            fw_t[block_end:, b:block_end], err[b:block_end, :],
            precision=lax.Precision.HIGHEST, preferred_element_type=F32,
        )


def kernel(
    ids_hbm, calib_hbm, keep_hbm, ww_hbm, rest_hbm, fw_hbm, fr_hbm,
    pruned_out, rest_out, hess_out, outs_out,
    ids, cal, kp, ww, fw, fr, fr_split, fr_pair, fac, xin, x_t, cur, scaled_drop, err, fw_t, err_half, local_outs,
    gram, gram_half, relay_in, relay_out, from_left, from_right, peer_out, peer_in,
    load_sem, pair_sem, f_send, f_recv, scat_send, scat_recv, xz_send, xz_recv, xx_send, xx_recv, xp_sem,
    o_send, o_recv, h_send, h_recv,
):
    tok, row = lax.axis_index("tok"), lax.axis_index("row")
    x, h, c = row // 8, (row // 2) % 4, row % 2
    l, y = tok // 4, tok % 4
    chip = x * 4 + h

    def row_of(px, ph, pc):
        return ((px + 4) % 4) * 8 + ((ph + 4) % 4) * 2 + pc

    def remote(src, dst, ssem, rsem, to_row=None, to_tok=None):
        return pltpu.make_async_remote_copy(
            src_ref=src, dst_ref=dst, send_sem=ssem, recv_sem=rsem,
            device_id=(tok if to_tok is None else to_tok, row if to_row is None else to_row),
            device_id_type=MESH,
        )

    loads = [
        pltpu.make_async_copy(s, d, load_sem.at[i])
        for i, (s, d) in enumerate(
            [(fr_hbm, fr), (calib_hbm, cal), (ww_hbm, ww), (keep_hbm, kp), (fw_hbm, fw), (ids_hbm, ids), (rest_hbm, rest_out)]
        )
    ]
    for load in loads:
        load.start()

    barrier = pltpu.get_barrier_semaphore()

    def greet(d, carry):
        pl.semaphore_signal(barrier, inc=1, device_id=(tok, (row + d) % N_ROW), device_id_type=MESH)
        return carry

    lax.fori_loop(1, N_ROW, greet, 0)
    up_tok, down_tok, other_tok = l * 4 + (y + 1) % 4, l * 4 + (y + 3) % 4, (1 - l) * 4 + y
    for peer in (up_tok, down_tok, other_tok):
        pl.semaphore_signal(barrier, inc=1, device_id=(peer, row), device_id_type=MESH)
    pl.semaphore_wait(barrier, N_ROW - 1 + 3)

    is_source = row == 0
    loads[1].wait()

    def scatter(r):
        first = pl.multiple_of((r % 2) * 256 + (r // 2) * 16, 16)
        return remote(
            cal.at[pl.ds(first, 16), pl.ds(0, WIN)], xin.at[r % 2, r // 2], scat_send.at[r], scat_recv.at[0], to_row=r
        )

    @pl.when(is_source)
    def _():
        def send(r, carry):
            scatter(r).start()
            return carry

        lax.fori_loop(1, N_ROW, send, 0)
        xin[0, 0] = cal[0:16, 0:WIN]

    loads[0].wait()
    fr_split[0] = fr[:, 0:HALF]
    fr_split[1, :, HALF - 128 :] = jnp.zeros((8, 128), F32)
    fr_split[1, :, 0 : REST - HALF] = fr[:, HALF:REST]
    own_rows = pl.ds(pl.multiple_of(c * 8, 8), 8)
    pair_copy = remote(
        fr_split.at[1 - c], fr_pair.at[own_rows], pair_sem.at[0], pair_sem.at[1], to_row=row_of(x, h, 1 - c)
    )
    pair_copy.start()
    fr_pair[own_rows, :] = fr_split[c]

    for i in (2, 3, 4):
        loads[i].wait()
    prune_prepare(ww, kp, fw, cur, scaled_drop, fw_t)

    def f_copy(p, number, slot, to_row, piece=None):
        first, size = p * PHASE_COLS, PHASE_COLS
        if piece is not None:
            first, size = first + piece * PIECE, PIECE
        ref = fac.at[c, slot, :, pl.ds(first, size)]
        return remote(ref, ref, f_send.at[p, number], f_recv.at[p, number], to_row=to_row)

    x_up, x_down = row_of(x + 1, h, c), row_of(x - 1, h, c)
    z_up, z_down = row_of(x, h + 1, c), row_of(x, h - 1, c)
    pair = row_of(x, h, 1 - c)
    z_slots = [h, (h + 3) % 4, (h + 1) % 4, (h + 2) % 4]
    x_slots = [x, (x + 3) % 4, (x + 1) % 4, (x + 2) % 4]
    f_started = []

    def f_start(*args, **kw):
        copy = f_copy(*args, **kw)
        copy.start()
        f_started.append(copy)

    def f_from_z(p, j):
        slot = x * 4 + z_slots[j]
        if j == 1:
            f_start(p, Z_UP_PIECE, slot, z_up, piece=0)
        if j == 2:
            f_start(p, Z_DOWN_PIECE, slot, z_down, piece=1)
        f_start(p, X_FIRST + 4 * j, slot, x_up)
        f_start(p, X_FIRST + 4 * j + 1, slot, x_down)
        f_start(p, PAIR_FIRST + j, slot, pair)

    def f_own(p):
        f_start(p, Z_UP, chip, z_up)
        f_start(p, Z_DOWN, chip, z_down)
        f_from_z(p, 0)

    def f_z_neighbours(p):
        f_copy(p, Z_UP, x * 4 + z_slots[1], z_up).wait_recv()
        f_from_z(p, 1)
        f_copy(p, Z_DOWN, x * 4 + z_slots[2], z_down).wait_recv()
        f_from_z(p, 2)

    def f_z_opposite(p):
        slot = x * 4 + z_slots[3]
        f_copy(p, Z_UP_PIECE, slot, z_up, piece=0).wait_recv()
        f_copy(p, Z_DOWN_PIECE, slot, z_down, piece=1).wait_recv()
        f_from_z(p, 3)

    def f_x_neighbours(p, j):
        n = X_FIRST + 4 * j
        slot = x_slots[1] * 4 + z_slots[j]
        f_copy(p, n, slot, x_up).wait_recv()
        f_start(p, n + 2, slot, x_up, piece=0)
        f_start(p, PAIR_FIRST + 4 + j, slot, pair)
        slot = x_slots[2] * 4 + z_slots[j]
        f_copy(p, n + 1, slot, x_down).wait_recv()
        f_start(p, n + 3, slot, x_down, piece=1)
        f_start(p, PAIR_FIRST + 8 + j, slot, pair)

    def f_x_opposite(p, j):
        n = X_FIRST + 4 * j
        slot = x_slots[3] * 4 + z_slots[j]
        f_copy(p, n + 2, slot, x_up, piece=0).wait_recv()
        f_copy(p, n + 3, slot, x_down, piece=1).wait_recv()
        f_start(p, PAIR_FIRST + 12 + j, slot, pair)

    def f_pair_wait(p):
        for i in range(4):
            for j in range(4):
                slot = x_slots[i] * 4 + z_slots[j]
                ref = fac.at[1 - c, slot, :, pl.ds(p * PHASE_COLS, PHASE_COLS)]
                number = PAIR_FIRST + 4 * i + j
                remote(ref, ref, f_send.at[p, number], f_recv.at[p, number], to_row=pair).wait_recv()

    pair_copy.wait_recv()
    fac[c, chip] = fr_pair[...].astype(BF16)

    def xz_copy(d):
        ref = xin.at[c, chip]
        return remote(ref, ref, xz_send.at[d], xz_recv.at[d], to_row=row_of(x, h + d, c))

    @pl.when(jnp.logical_not(is_source))
    def _():
        remote(xin.at[c, chip], xin.at[c, chip], scat_send.at[0], scat_recv.at[0], to_row=row_of(x, h, 1 - c)).wait_recv()

    for d in (1, 3, 2):
        xz_copy(d).start()
    for p in range(PHASES):
        f_own(p)

    prune = functools.partial(prune_tile, cur=cur, scaled_drop=scaled_drop, fw_t=fw_t, err=err)
    for k in range(0, 8):
        prune(k)

    def xx_copy(d):
        ref = xin.at[c, pl.ds(x * 4, 4)]
        return remote(ref, ref, xx_send.at[d], xx_recv.at[d], to_row=row_of(x + d, h, c))

    for d in (1, 3, 2):
        ref = xin.at[c, x * 4 + (h + 4 - d) % 4]
        remote(ref, ref, xz_send.at[d], xz_recv.at[d], to_row=row_of(x, h + d, c)).wait_recv()
    for d in (1, 3, 2):
        xx_copy(d).start()
    for p in range(PHASES):
        f_z_neighbours(p)

    for k in range(8, 16):
        prune(k)

    for d in (1, 3, 2):
        ref = xin.at[c, pl.ds(((x + 4 - d) % 4) * 4, 4)]
        remote(ref, ref, xx_send.at[d], xx_recv.at[d], to_row=row_of(x + d, h, c)).wait_recv()
    xp_copy = remote(xin.at[c], xin.at[c], xp_sem.at[0], xp_sem.at[1], to_row=pair)
    xp_copy.start()
    for p in range(PHASES):
        f_z_opposite(p)

    for k in range(16, 24):
        prune(k)

    remote(xin.at[1 - c], xin.at[1 - c], xp_sem.at[0], xp_sem.at[1], to_row=pair).wait_recv()

    loads[5].wait()
    live = jnp.where(ids[...] != 1, 1.0, 0.0)
    live_t = jnp.concatenate([live, jnp.zeros((4, 128), F32)], axis=0).T
    x_parts = []
    for s in range(4):
        part = xin[s // 2, (s % 2) * 8 : (s % 2) * 8 + 8].reshape(128, WIN).astype(F32)
        x_parts.append(part * live_t[:, s : s + 1])
    x_all = jnp.concatenate(x_parts, axis=0)
    x_t[...] = x_all.T.astype(BF16)

    @pl.loop(0, FEATURES // 256)
    def _(i):
        cols = pl.ds(pl.multiple_of(i * 256, 256), 256)
        part = jnp.dot(x_t[...], cal[:, cols], preferred_element_type=F32).reshape(N_TOK, 32, 256)
        gram[:, :, cols] = part
        gram_half[:, :, cols] = part.astype(BF16)

    def h_copy(number, src, dst, to_tok):
        return remote(src, dst, h_send.at[number], h_recv.at[number], to_tok=to_tok)

    h_copies = [
        h_copy(0, gram_half.at[(y + 2) % 4], relay_in.at[0], up_tok),
        h_copy(1, gram_half.at[4 + (y + 2) % 4], relay_in.at[1], down_tok),
        h_copy(2, gram_half.at[4 + (y + 1) % 4], from_left.at[1], up_tok),
        h_copy(3, gram_half.at[(y + 3) % 4], from_right.at[0], down_tok),
        h_copy(4, relay_out.at[0], from_left.at[0], up_tok),
        h_copy(5, relay_out.at[1], from_right.at[1], down_tok),
        h_copy(6, peer_out, peer_in, other_tok),
    ]
    for i in range(4):
        h_copies[i].start()

    for k in range(24, 32):
        prune(k)

    pruned_t = cur[...]
    pruned_half = pruned_t.astype(BF16)
    local_outs[...] = jnp.dot(x_all.astype(BF16), pruned_half, preferred_element_type=F32).astype(BF16).reshape(N_ROW, 16, LOCAL_ROWS)

    def out_copy(d, sender, owner):
        cols = pl.ds(pl.multiple_of(sender * LOCAL_ROWS, 128), LOCAL_ROWS)
        return remote(local_outs.at[owner], outs_out.at[:, cols], o_send.at[d], o_recv.at[d], to_row=owner)

    def send_out(d, carry):
        out_copy(d, row, (row + d) % N_ROW).start()
        return carry

    lax.fori_loop(1, N_ROW, send_out, 0)

    h_copies[0].wait_recv()
    relay_out[0] = (relay_in[0].astype(F32) + gram[(y + 1) % 4]).astype(BF16)
    h_copies[4].start()
    h_copies[1].wait_recv()
    relay_out[1] = (relay_in[1].astype(F32) + gram[4 + (y + 3) % 4]).astype(BF16)
    h_copies[5].start()

    for p in range(PHASES):
        for j in range(4):
            f_x_neighbours(p, j)

    outs_out[:, pl.ds(pl.multiple_of(row * LOCAL_ROWS, 128), LOCAL_ROWS)] = local_outs[row]
    pruned_out[...] = pruned_t.T
    err_half[...] = err[...].astype(BF16)

    for i in range(2, 6):
        h_copies[i].wait_recv()
    peer_out[...] = (
        gram[(1 - l) * 4 + y] + from_left[1 - l].astype(F32) + from_right[1 - l].astype(F32)
    ).astype(BF16)
    h_copies[6].start()

    def update(half, first, size):
        factor = fac[half, :, :, pl.ds(first, size)].reshape(WIN, size)
        change = lax.dot_general(
            factor, err_half[...], (((0,), (0,)), ((), ())), preferred_element_type=F32
        )
        count = min(size, REST - (half * HALF + first)) if isinstance(first, int) else size
        start = half * HALF + first
        rows = pl.ds(start if isinstance(first, int) else pl.multiple_of(start, 256), count)
        rest_out[rows, :] = (rest_out[rows, :].astype(F32) - change[:count]).astype(BF16)

    loads[6].wait()
    step = 512
    for p in range(PHASES):
        for j in range(4):
            f_x_opposite(p, j)
        f_pair_wait(p)
        for half in range(2):
            first, count = p * PHASE_COLS, PHASE_COLS // step
            ragged = half == 1 and p == PHASES - 1

            @pl.loop(0, count - 1 if ragged else count)
            def _(i, half=half, first=first):
                update(half, pl.multiple_of(first + i * step, step), step)

            if ragged:
                update(half, HALF - step, step)

    h_copies[6].wait_recv()
    total = gram[l * 4 + y] + from_left[l].astype(F32) + from_right[l].astype(F32) + peer_in[...].astype(F32)
    hess_out[...] = total * (2.0 / TOKENS)


    def take_out(d, carry):
        sender = (row + N_ROW - d) % N_ROW
        cols = pl.ds(pl.multiple_of(sender * LOCAL_ROWS, 128), LOCAL_ROWS)
        remote(local_outs.at[row], outs_out.at[:, cols], o_send.at[d], o_recv.at[d], to_row=sender).wait_recv()
        return carry

    lax.fori_loop(1, N_ROW, take_out, 0)

    def left_out(d, carry):
        out_copy(d, row, (row + d) % N_ROW).wait_send()
        return carry

    lax.fori_loop(1, N_ROW, left_out, 0)

    @pl.when(is_source)
    def _():
        def left(r, carry):
            scatter(r).wait_send()
            return carry

        lax.fori_loop(1, N_ROW, left, 0)

    pair_copy.wait_send()
    for d in (1, 3, 2):
        xz_copy(d).wait_send()
        xx_copy(d).wait_send()
    xp_copy.wait_send()
    for copy in h_copies:
        copy.wait_send()
    for copy in f_started:
        copy.wait_send()


def on_device(token_ids, calib_input, keep_mask, weight_window, weight_rest, factor_window, factor_rest):
    vmem, dma = pltpu.VMEM, pltpu.SemaphoreType.DMA
    slab = (32, FEATURES)
    pruned, rest_t, hess, outs = pl.pallas_call(
        kernel,
        out_shape=(
            jax.ShapeDtypeStruct((LOCAL_ROWS, WIN), F32),
            jax.ShapeDtypeStruct((REST, LOCAL_ROWS), BF16),
            jax.ShapeDtypeStruct(slab, F32),
            jax.ShapeDtypeStruct((16, N_ROW * LOCAL_ROWS), BF16),
        ),
        in_specs=[pl.BlockSpec(memory_space=pltpu.HBM)] * 7,
        out_specs=[pl.BlockSpec(memory_space=vmem)] * 4,
        scratch_shapes=[
            vmem((4, 128), jnp.int32),
            vmem((LOCAL_TOKENS, FEATURES), BF16),
            vmem((LOCAL_ROWS, WIN), jnp.int32),
            vmem((LOCAL_ROWS, WIN), F32),
            vmem((WIN, WIN), F32),
            vmem((8, REST), F32),
            vmem((2, 8, HALF), F32),
            vmem((16, HALF), F32),
            vmem((2, CHIPS, 16, HALF), BF16),
            vmem((2, CHIPS, 16, WIN), BF16),
            vmem((WIN, LOCAL_TOKENS), BF16),
            vmem((WIN, LOCAL_ROWS), F32),
            vmem((WIN, LOCAL_ROWS), F32),
            vmem((WIN, LOCAL_ROWS), F32),
            vmem((WIN, WIN), F32),
            vmem((WIN, LOCAL_ROWS), BF16),
            vmem((N_ROW, 16, LOCAL_ROWS), BF16),
            vmem((N_TOK,) + slab, F32),
            vmem((N_TOK,) + slab, BF16),
            vmem((2,) + slab, BF16),
            vmem((2,) + slab, BF16),
            vmem((2,) + slab, BF16),
            vmem((2,) + slab, BF16),
            vmem(slab, BF16),
            vmem(slab, BF16),
            dma((7,)),
            dma((2,)),
            dma((PHASES, F_MESSAGES)),
            dma((PHASES, F_MESSAGES)),
            dma((N_ROW,)),
            dma((1,)),
            dma((4,)),
            dma((4,)),
            dma((4,)),
            dma((4,)),
            dma((2,)),
            dma((N_ROW,)),
            dma((N_ROW,)),
            dma((7,)),
            dma((7,)),
        ],
        compiler_params=pltpu.CompilerParams(
            collective_id=0, has_side_effects=True, vmem_limit_bytes=52 * 1024 * 1024
        ),
        cost_estimate=pl.CostEstimate(flops=2_000_000_000, bytes_accessed=16_000_000, transcendentals=0),
    )(token_ids.reshape(4, 128), calib_input, keep_mask, weight_window, weight_rest.T, factor_window, factor_rest)
    return pruned, rest_t.T, hess, outs


def solution(mesh):
    return jax.shard_map(
        on_device,
        mesh=mesh,
        in_specs=(
            P("tok"),
            P("tok", "row"),
            P("row", None),
            P("row", None),
            P("row", "tok"),
            P(),
            P("row", "tok"),
        ),
        out_specs=(P("row", None), P("row", "tok"), P("tok", "row"), P(("tok", "row"), None)),
        check_vma=False,
    )
```

```python
import jax
import jax.numpy as jnp
from jax import lax
from jax.experimental import pallas as pl
from jax.experimental.pallas import tpu as pltpu
from jax.sharding import PartitionSpec as P

MESH = pl.DeviceIdType.MESH
F32, BF16 = jnp.float32, jnp.bfloat16

WIN = 256
BLOCK = 128
SUB = 8
LOCAL_ROWS = 384
LOCAL_TOKENS = 512
FEATURES = 1536
REST = 6112
HALF = 3072
N_ROW = 32
N_TOK = 8
CHIPS = 16
TOKENS = LOCAL_TOKENS * N_TOK

PHASES = 2
PHASE_COLS = HALF // PHASES
PIECE = PHASE_COLS // 2
STEP = 512

Z_UP, Z_DOWN, Z_UP_PIECE, Z_DOWN_PIECE = 0, 1, 2, 3
X_FIRST = 4
PAIR_FIRST = 20
F_MESSAGES = 36


def prune_prepare(ww, kp, fw, cur, scaled_drop, fw_t):
    factor = fw[...]
    fw_t[...] = factor.T
    row_id = lax.broadcasted_iota(jnp.int32, (WIN, WIN), 0)
    col_id = lax.broadcasted_iota(jnp.int32, (WIN, WIN), 1)
    diagonal = jnp.sum(jnp.where(row_id == col_id, factor, 0.0), axis=1, keepdims=True)
    drop = (1 - kp[...]).astype(F32).T
    scaled_drop[...] = drop * (1.0 / diagonal)
    cur[...] = ww[...].T


def prune_tile(k, cur, scaled_drop, fw_t, err):
    low = k * SUB
    block_end = (low // BLOCK + 1) * BLOCK
    tile = cur[low : low + SUB, :]
    drop = scaled_drop[low : low + SUB, :]
    rows = []
    for s in range(SUB):
        e = tile[s : s + 1, :] * drop[s : s + 1, :]
        rows.append(e)
        tile = tile - fw_t[low : low + SUB, low + s : low + s + 1] * e
    cur[low : low + SUB, :] = tile
    err[low : low + SUB, :] = jnp.concatenate(rows, axis=0)
    start = low + SUB
    while start < block_end:
        end = min(start + 32, block_end)
        part = cur[start:end, :]
        for s in range(SUB):
            part = part - fw_t[start:end, low + s : low + s + 1] * rows[s]
        cur[start:end, :] = part
        start = end
    if block_end == low + SUB and block_end < WIN:
        b = block_end - BLOCK
        cur[block_end:, :] = cur[block_end:, :] - jnp.dot(
            fw_t[block_end:, b:block_end], err[b:block_end, :],
            precision=lax.Precision.HIGHEST, preferred_element_type=F32,
        )


def compensate(rest, factor, err_half):
    change = lax.dot_general(
        factor.reshape(WIN, -1), err_half, (((0,), (0,)), ((), ())), preferred_element_type=F32
    )
    return (rest.astype(F32) - change[: rest.shape[0]]).astype(BF16)


def kernel(
    ids_hbm, calib_hbm, keep_hbm, ww_hbm, rest_hbm, fw_hbm, fr_hbm,
    pruned_out, rest_out, hess_out, outs_out, fac, err_half,
    ids, cal, kp, ww, fw, fr, fr_split, fr_pair, xin, x_t, cur, scaled_drop, err, fw_t, local_outs,
    gram, gram_half, relay_in, relay_out, from_left, from_right, peer_out, peer_in,
    load_sem, pair_sem, f_send, f_recv, scat_send, scat_recv, xz_send, xz_recv, xx_send, xx_recv, xp_sem,
    o_send, o_recv, h_send, h_recv,
):
    tok, row = lax.axis_index("tok"), lax.axis_index("row")
    x, h, c = row // 8, (row // 2) % 4, row % 2
    l, y = tok // 4, tok % 4
    chip = x * 4 + h

    def row_of(px, ph, pc):
        return ((px + 4) % 4) * 8 + ((ph + 4) % 4) * 2 + pc

    def remote(src, dst, ssem, rsem, to_row=None, to_tok=None):
        return pltpu.make_async_remote_copy(
            src_ref=src, dst_ref=dst, send_sem=ssem, recv_sem=rsem,
            device_id=(tok if to_tok is None else to_tok, row if to_row is None else to_row),
            device_id_type=MESH,
        )

    loads = [
        pltpu.make_async_copy(s, d, load_sem.at[i])
        for i, (s, d) in enumerate(
            [(fr_hbm, fr), (calib_hbm, cal), (ww_hbm, ww), (keep_hbm, kp), (fw_hbm, fw), (ids_hbm, ids), (rest_hbm, rest_out)]
        )
    ]
    for load in loads:
        load.start()

    barrier = pltpu.get_barrier_semaphore()

    def greet(d, carry):
        pl.semaphore_signal(barrier, inc=1, device_id=(tok, (row + d) % N_ROW), device_id_type=MESH)
        return carry

    lax.fori_loop(1, N_ROW, greet, 0)
    up_tok, down_tok, other_tok = l * 4 + (y + 1) % 4, l * 4 + (y + 3) % 4, (1 - l) * 4 + y
    for peer in (up_tok, down_tok, other_tok):
        pl.semaphore_signal(barrier, inc=1, device_id=(peer, row), device_id_type=MESH)
    pl.semaphore_wait(barrier, N_ROW - 1 + 3)

    is_source = row == 0
    loads[1].wait()

    def scatter(r):
        first = pl.multiple_of((r % 2) * 256 + (r // 2) * 16, 16)
        return remote(
            cal.at[pl.ds(first, 16), pl.ds(0, WIN)], xin.at[r % 2, r // 2], scat_send.at[r], scat_recv.at[0], to_row=r
        )

    @pl.when(is_source)
    def _():
        def send(r, carry):
            scatter(r).start()
            return carry

        lax.fori_loop(1, N_ROW, send, 0)
        xin[0, 0] = cal[0:16, 0:WIN]

    loads[0].wait()
    fr_split[0] = fr[:, 0:HALF]
    fr_split[1, :, HALF - 128 :] = jnp.zeros((8, 128), F32)
    fr_split[1, :, 0 : REST - HALF] = fr[:, HALF:REST]
    own_rows = pl.ds(pl.multiple_of(c * 8, 8), 8)
    pair_copy = remote(
        fr_split.at[1 - c], fr_pair.at[own_rows], pair_sem.at[0], pair_sem.at[1], to_row=row_of(x, h, 1 - c)
    )
    pair_copy.start()
    fr_pair[own_rows, :] = fr_split[c]

    for i in (2, 3, 4):
        loads[i].wait()
    prune_prepare(ww, kp, fw, cur, scaled_drop, fw_t)

    def f_copy(p, number, slot, to_row, piece=None):
        first, size = p * PHASE_COLS, PHASE_COLS
        if piece is not None:
            first, size = first + piece * PIECE, PIECE
        ref = fac.at[c, slot, :, pl.ds(first, size)]
        return remote(ref, ref, f_send.at[p, number], f_recv.at[p, number], to_row=to_row)

    x_up, x_down = row_of(x + 1, h, c), row_of(x - 1, h, c)
    z_up, z_down = row_of(x, h + 1, c), row_of(x, h - 1, c)
    pair = row_of(x, h, 1 - c)
    z_slots = [h, (h + 3) % 4, (h + 1) % 4, (h + 2) % 4]
    x_slots = [x, (x + 3) % 4, (x + 1) % 4, (x + 2) % 4]
    f_started = []

    def f_start(*args, **kw):
        copy = f_copy(*args, **kw)
        copy.start()
        f_started.append(copy)

    def f_from_z(p, j):
        slot = x * 4 + z_slots[j]
        if j == 1:
            f_start(p, Z_UP_PIECE, slot, z_up, piece=0)
        if j == 2:
            f_start(p, Z_DOWN_PIECE, slot, z_down, piece=1)
        f_start(p, X_FIRST + 4 * j, slot, x_up)
        f_start(p, X_FIRST + 4 * j + 1, slot, x_down)
        f_start(p, PAIR_FIRST + j, slot, pair)

    def f_own(p):
        f_start(p, Z_UP, chip, z_up)
        f_start(p, Z_DOWN, chip, z_down)
        f_from_z(p, 0)

    def f_z_neighbours(p):
        f_copy(p, Z_UP, x * 4 + z_slots[1], z_up).wait_recv()
        f_from_z(p, 1)
        f_copy(p, Z_DOWN, x * 4 + z_slots[2], z_down).wait_recv()
        f_from_z(p, 2)

    def f_z_opposite(p):
        slot = x * 4 + z_slots[3]
        f_copy(p, Z_UP_PIECE, slot, z_up, piece=0).wait_recv()
        f_copy(p, Z_DOWN_PIECE, slot, z_down, piece=1).wait_recv()
        f_from_z(p, 3)

    def f_x_neighbours(p, j):
        n = X_FIRST + 4 * j
        slot = x_slots[1] * 4 + z_slots[j]
        f_copy(p, n, slot, x_up).wait_recv()
        f_start(p, n + 2, slot, x_up, piece=0)
        f_start(p, PAIR_FIRST + 4 + j, slot, pair)
        slot = x_slots[2] * 4 + z_slots[j]
        f_copy(p, n + 1, slot, x_down).wait_recv()
        f_start(p, n + 3, slot, x_down, piece=1)
        f_start(p, PAIR_FIRST + 8 + j, slot, pair)

    def f_x_opposite(p, j):
        n = X_FIRST + 4 * j
        slot = x_slots[3] * 4 + z_slots[j]
        f_copy(p, n + 2, slot, x_up, piece=0).wait_recv()
        f_copy(p, n + 3, slot, x_down, piece=1).wait_recv()
        f_start(p, PAIR_FIRST + 12 + j, slot, pair)

    def f_pair_wait(p):
        for i in range(4):
            for j in range(4):
                slot = x_slots[i] * 4 + z_slots[j]
                ref = fac.at[1 - c, slot, :, pl.ds(p * PHASE_COLS, PHASE_COLS)]
                number = PAIR_FIRST + 4 * i + j
                remote(ref, ref, f_send.at[p, number], f_recv.at[p, number], to_row=pair).wait_recv()

    pair_copy.wait_recv()
    fac[c, chip] = fr_pair[...].astype(BF16)

    def xz_copy(d):
        ref = xin.at[c, chip]
        return remote(ref, ref, xz_send.at[d], xz_recv.at[d], to_row=row_of(x, h + d, c))

    @pl.when(jnp.logical_not(is_source))
    def _():
        remote(xin.at[c, chip], xin.at[c, chip], scat_send.at[0], scat_recv.at[0], to_row=row_of(x, h, 1 - c)).wait_recv()

    for d in (1, 3, 2):
        xz_copy(d).start()
    for p in range(PHASES):
        f_own(p)

    def prune(first, last):
        for k in range(first, last):
            prune_tile(k, cur, scaled_drop, fw_t, err)

    prune(0, 6)

    def xx_copy(d):
        ref = xin.at[c, pl.ds(x * 4, 4)]
        return remote(ref, ref, xx_send.at[d], xx_recv.at[d], to_row=row_of(x + d, h, c))

    for d in (1, 3, 2):
        ref = xin.at[c, x * 4 + (h + 4 - d) % 4]
        remote(ref, ref, xz_send.at[d], xz_recv.at[d], to_row=row_of(x, h + d, c)).wait_recv()
    for d in (1, 3, 2):
        xx_copy(d).start()

    prune(6, 9)
    f_z_neighbours(0)
    prune(9, 12)
    f_x_neighbours(0, 0)

    for d in (1, 3, 2):
        ref = xin.at[c, pl.ds(((x + 4 - d) % 4) * 4, 4)]
        remote(ref, ref, xx_send.at[d], xx_recv.at[d], to_row=row_of(x + d, h, c)).wait_recv()
    xp_copy = remote(xin.at[c], xin.at[c], xp_sem.at[0], xp_sem.at[1], to_row=pair)
    xp_copy.start()

    prune(12, 15)
    f_z_neighbours(1)
    f_x_neighbours(1, 0)
    prune(15, 18)

    remote(xin.at[1 - c], xin.at[1 - c], xp_sem.at[0], xp_sem.at[1], to_row=pair).wait_recv()

    loads[5].wait()
    live = jnp.where(ids[...] != 1, 1.0, 0.0)
    live_t = jnp.concatenate([live, jnp.zeros((4, 128), F32)], axis=0).T
    x_parts = []
    for s in range(4):
        part = xin[s // 2, (s % 2) * 8 : (s % 2) * 8 + 8].reshape(128, WIN).astype(F32)
        x_parts.append(part * live_t[:, s : s + 1])
    x_all = jnp.concatenate(x_parts, axis=0)
    x_t[...] = x_all.T.astype(BF16)

    @pl.loop(0, FEATURES // 256)
    def _(i):
        cols = pl.ds(pl.multiple_of(i * 256, 256), 256)
        part = jnp.dot(x_t[...], cal[:, cols], preferred_element_type=F32).reshape(N_TOK, 32, 256)
        gram[:, :, cols] = part
        gram_half[:, :, cols] = part.astype(BF16)

    def h_copy(number, src, dst, to_tok):
        return remote(src, dst, h_send.at[number], h_recv.at[number], to_tok=to_tok)

    h_copies = [
        h_copy(0, gram_half.at[(y + 2) % 4], relay_in.at[0], up_tok),
        h_copy(1, gram_half.at[4 + (y + 2) % 4], relay_in.at[1], down_tok),
        h_copy(2, gram_half.at[4 + (y + 1) % 4], from_left.at[1], up_tok),
        h_copy(3, gram_half.at[(y + 3) % 4], from_right.at[0], down_tok),
        h_copy(4, relay_out.at[0], from_left.at[0], up_tok),
        h_copy(5, relay_out.at[1], from_right.at[1], down_tok),
        h_copy(6, peer_out, peer_in, other_tok),
    ]
    for i in range(4):
        h_copies[i].start()

    f_z_opposite(0)
    f_x_neighbours(0, 1)
    prune(18, 23)
    f_z_opposite(1)
    f_x_neighbours(1, 1)
    prune(23, 28)
    f_x_neighbours(0, 2)
    prune(28, 32)

    pruned_t = cur[...]
    pruned_half = pruned_t.astype(BF16)
    local_outs[...] = jnp.dot(
        x_all.astype(BF16), pruned_half, preferred_element_type=F32
    ).astype(BF16).reshape(N_ROW, 16, LOCAL_ROWS)

    def out_copy(d, sender, owner):
        cols = pl.ds(pl.multiple_of(sender * LOCAL_ROWS, 128), LOCAL_ROWS)
        return remote(local_outs.at[owner], outs_out.at[:, cols], o_send.at[d], o_recv.at[d], to_row=owner)

    def send_out(d, carry):
        out_copy(d, row, (row + d) % N_ROW).start()
        return carry

    lax.fori_loop(1, N_ROW, send_out, 0)

    h_copies[0].wait_recv()
    relay_out[0] = (relay_in[0].astype(F32) + gram[(y + 1) % 4]).astype(BF16)
    h_copies[4].start()
    h_copies[1].wait_recv()
    relay_out[1] = (relay_in[1].astype(F32) + gram[4 + (y + 3) % 4]).astype(BF16)
    h_copies[5].start()

    f_x_neighbours(1, 2)
    f_x_neighbours(0, 3)
    f_x_opposite(0, 0)
    f_x_opposite(0, 1)
    f_x_neighbours(1, 3)
    f_x_opposite(0, 2)
    f_x_opposite(0, 3)

    outs_out[:, pl.ds(pl.multiple_of(row * LOCAL_ROWS, 128), LOCAL_ROWS)] = local_outs[row]
    pruned_out[...] = pruned_t.T
    err_half[...] = err[...].astype(BF16)

    for i in range(2, 6):
        h_copies[i].wait_recv()
    peer_out[...] = (
        gram[(1 - l) * 4 + y] + from_left[1 - l].astype(F32) + from_right[1 - l].astype(F32)
    ).astype(BF16)
    h_copies[6].start()

    f_x_opposite(1, 0)
    f_x_opposite(1, 1)

    loads[6].wait()
    for p in range(PHASES - 1):
        f_pair_wait(p)
        for half in range(2):

            @pl.loop(0, PHASE_COLS // STEP)
            def _(i, half=half, p=p):
                first = pl.multiple_of(p * PHASE_COLS + i * STEP, STEP)
                rows = pl.ds(pl.multiple_of(half * HALF + first, STEP), STEP)
                factor = fac[half, :, :, pl.ds(first, STEP)]
                rest_out[rows, :] = compensate(rest_out[rows, :], factor, err_half[...])

    f_x_opposite(1, 2)
    f_x_opposite(1, 3)

    h_copies[6].wait_recv()
    total = gram[l * 4 + y] + from_left[l].astype(F32) + from_right[l].astype(F32) + peer_in[...].astype(F32)
    hess_out[...] = total * (2.0 / TOKENS)

    def take_out(d, carry):
        sender = (row + N_ROW - d) % N_ROW
        cols = pl.ds(pl.multiple_of(sender * LOCAL_ROWS, 128), LOCAL_ROWS)
        remote(local_outs.at[row], outs_out.at[:, cols], o_send.at[d], o_recv.at[d], to_row=sender).wait_recv()
        return carry

    lax.fori_loop(1, N_ROW, take_out, 0)
    f_pair_wait(PHASES - 1)

    def left_out(d, carry):
        out_copy(d, row, (row + d) % N_ROW).wait_send()
        return carry

    lax.fori_loop(1, N_ROW, left_out, 0)

    @pl.when(is_source)
    def _():
        def left(r, carry):
            scatter(r).wait_send()
            return carry

        lax.fori_loop(1, N_ROW, left, 0)

    pair_copy.wait_send()
    for d in (1, 3, 2):
        xz_copy(d).wait_send()
        xx_copy(d).wait_send()
    xp_copy.wait_send()
    for copy in h_copies:
        copy.wait_send()
    for copy in f_started:
        copy.wait_send()


def finish_kernel(
    pruned, rest, hess, outs, fac, err_half,
    pruned_hbm, rest_hbm, hess_hbm, outs_hbm,
    updated, sem,
):
    copies = [
        pltpu.make_async_copy(pruned, pruned_hbm, sem.at[0]),
        pltpu.make_async_copy(hess, hess_hbm, sem.at[1]),
        pltpu.make_async_copy(outs, outs_hbm, sem.at[2]),
    ]
    last = HALF - PHASE_COLS
    for half in range(2):
        rows = pl.ds(half * HALF, last)
        copies.append(pltpu.make_async_copy(rest.at[rows], rest_hbm.at[rows], sem.at[3 + half]))
    for copy in copies:
        copy.start()
    for half in range(2):
        for i in range(PHASE_COLS // STEP):
            first = last + i * STEP
            start = half * HALF + first
            count = min(STEP, REST - start)
            part = rest[start : start + count, :]
            at = half * PHASE_COLS + i * STEP
            updated[at : at + count, :] = compensate(part, fac[half, :, :, first : first + STEP], err_half[...])
            copy = pltpu.make_async_copy(
                updated.at[pl.ds(at, count)], rest_hbm.at[pl.ds(start, count)], sem.at[5 + half * (PHASE_COLS // STEP) + i]
            )
            copy.start()
            copies.append(copy)
    for copy in copies:
        copy.wait()


def on_device(token_ids, calib_input, keep_mask, weight_window, weight_rest, factor_window, factor_rest):
    vmem, dma = pltpu.VMEM, pltpu.SemaphoreType.DMA
    slab = (32, FEATURES)
    in_hbm = [
        pltpu.with_memory_space_constraint(a, pltpu.HBM)
        for a in (
            token_ids.reshape(4, 128), calib_input, keep_mask, weight_window, weight_rest.T, factor_window, factor_rest
        )
    ]
    shapes = [
        ((LOCAL_ROWS, WIN), F32),
        ((REST, LOCAL_ROWS), BF16),
        (slab, F32),
        ((16, N_ROW * LOCAL_ROWS), BF16),
    ]
    held = pl.pallas_call(
        kernel,
        out_shape=tuple(
            vmem(*s) for s in shapes + [((2, CHIPS, 16, HALF), BF16), ((WIN, LOCAL_ROWS), BF16)]
        ),
        in_specs=[pl.BlockSpec(memory_space=pltpu.HBM)] * 7,
        out_specs=[pl.BlockSpec(memory_space=vmem)] * 6,
        scratch_shapes=[
            vmem((4, 128), jnp.int32),
            vmem((LOCAL_TOKENS, FEATURES), BF16),
            vmem((LOCAL_ROWS, WIN), jnp.int32),
            vmem((LOCAL_ROWS, WIN), F32),
            vmem((WIN, WIN), F32),
            vmem((8, REST), F32),
            vmem((2, 8, HALF), F32),
            vmem((16, HALF), F32),
            vmem((2, CHIPS, 16, WIN), BF16),
            vmem((WIN, LOCAL_TOKENS), BF16),
            vmem((WIN, LOCAL_ROWS), F32),
            vmem((WIN, LOCAL_ROWS), F32),
            vmem((WIN, LOCAL_ROWS), F32),
            vmem((WIN, WIN), F32),
            vmem((N_ROW, 16, LOCAL_ROWS), BF16),
            vmem((N_TOK,) + slab, F32),
            vmem((N_TOK,) + slab, BF16),
            vmem((2,) + slab, BF16),
            vmem((2,) + slab, BF16),
            vmem((2,) + slab, BF16),
            vmem((2,) + slab, BF16),
            vmem(slab, BF16),
            vmem(slab, BF16),
            dma((7,)),
            dma((2,)),
            dma((PHASES, F_MESSAGES)),
            dma((PHASES, F_MESSAGES)),
            dma((N_ROW,)),
            dma((1,)),
            dma((4,)),
            dma((4,)),
            dma((4,)),
            dma((4,)),
            dma((2,)),
            dma((N_ROW,)),
            dma((N_ROW,)),
            dma((7,)),
            dma((7,)),
        ],
        compiler_params=pltpu.CompilerParams(
            collective_id=0, has_side_effects=True, vmem_limit_bytes=32 * 1024 * 1024
        ),
        cost_estimate=pl.CostEstimate(flops=2_000_000_000, bytes_accessed=16_000_000, transcendentals=0),
    )(*in_hbm)
    pruned, rest_t, hess, outs = pl.pallas_call(
        finish_kernel,
        out_shape=tuple(jax.ShapeDtypeStruct(*s) for s in shapes),
        in_specs=[pl.BlockSpec(memory_space=vmem)] * 6,
        out_specs=[pl.BlockSpec(memory_space=pltpu.HBM)] * 4,
        scratch_shapes=[
            vmem((2 * PHASE_COLS, LOCAL_ROWS), BF16),
            dma((5 + 2 * (PHASE_COLS // STEP),)),
        ],
        compiler_params=pltpu.CompilerParams(vmem_limit_bytes=32 * 1024 * 1024),
        cost_estimate=pl.CostEstimate(flops=600_000_000, bytes_accessed=12_000_000, transcendentals=0),
    )(*[pltpu.with_memory_space_constraint(a, vmem) for a in held])
    return pruned, rest_t.T, hess, outs


def solution(mesh):
    return jax.shard_map(
        on_device,
        mesh=mesh,
        in_specs=(
            P("tok"),
            P("tok", "row"),
            P("row", None),
            P("row", None),
            P("row", "tok"),
            P(),
            P("row", "tok"),
        ),
        out_specs=(P("row", None), P("row", "tok"), P("tok", "row"), P(("tok", "row"), None)),
        check_vma=False,
    )
```

```python
import jax
import jax.numpy as jnp
from jax import lax
from jax.experimental import pallas as pl
from jax.experimental.pallas import tpu as pltpu
from jax.sharding import PartitionSpec as P

MESH = pl.DeviceIdType.MESH
F32, BF16 = jnp.float32, jnp.bfloat16

WIN = 256
BLOCK = 128
SUB = 8
LOCAL_ROWS = 384
LOCAL_TOKENS = 512
FEATURES = 1536
REST = 6112
HALF = 3072
N_ROW = 32
N_TOK = 8
CHIPS = 16
TOKENS = LOCAL_TOKENS * N_TOK

PHASES = 2
PHASE_COLS = HALF // PHASES
PIECE = PHASE_COLS // 2
STEP = 512

Z_UP, Z_DOWN, Z_UP_PIECE, Z_DOWN_PIECE = 0, 1, 2, 3
X_FIRST = 4
PAIR_FIRST = 20
F_MESSAGES = 20


def prune_prepare(ww, kp, fw, cur, scaled_drop, fw_t):
    factor = fw[...]
    fw_t[...] = factor.T
    row_id = lax.broadcasted_iota(jnp.int32, (WIN, WIN), 0)
    col_id = lax.broadcasted_iota(jnp.int32, (WIN, WIN), 1)
    diagonal = jnp.sum(jnp.where(row_id == col_id, factor, 0.0), axis=1, keepdims=True)
    drop = (1 - kp[...]).astype(F32).T
    scaled_drop[...] = drop * (1.0 / diagonal)
    cur[...] = ww[...].T


def prune_tile(k, cur, scaled_drop, fw_t, err):
    low = k * SUB
    block_end = (low // BLOCK + 1) * BLOCK
    tile = cur[low : low + SUB, :]
    drop = scaled_drop[low : low + SUB, :]
    rows = []
    for s in range(SUB):
        e = tile[s : s + 1, :] * drop[s : s + 1, :]
        rows.append(e)
        tile = tile - fw_t[low : low + SUB, low + s : low + s + 1] * e
    cur[low : low + SUB, :] = tile
    err[low : low + SUB, :] = jnp.concatenate(rows, axis=0)
    start = low + SUB
    while start < block_end:
        end = min(start + 32, block_end)
        part = cur[start:end, :]
        for s in range(SUB):
            part = part - fw_t[start:end, low + s : low + s + 1] * rows[s]
        cur[start:end, :] = part
        start = end
    if block_end == low + SUB and block_end < WIN:
        b = block_end - BLOCK
        cur[block_end:, :] = cur[block_end:, :] - jnp.dot(
            fw_t[block_end:, b:block_end], err[b:block_end, :],
            precision=lax.Precision.HIGHEST, preferred_element_type=F32,
        )


def compensate(rest, factor, err_half):
    change = lax.dot_general(
        factor.reshape(WIN, -1), err_half, (((0,), (0,)), ((), ())), preferred_element_type=F32
    )
    return (rest.astype(F32) - change[: rest.shape[0]]).astype(BF16)


def kernel(
    ids_hbm, calib_hbm, keep_hbm, ww_hbm, rest_hbm, fw_hbm, fr_hbm,
    pruned_out, rest_out, hess_out, outs_out, fac, err_half,
    ids, cal, kp, ww, fw, fr, fr_split, fr_pair, xin, x_t, cur, scaled_drop, err, fw_t, x_half, local_outs, out_relay,
    gram, gram_half, relay_in, relay_out, from_left, from_right, peer_out, peer_in,
    load_sem, pair_sem, f_send, f_recv, pair_recv, scat_send, scat_recv, xz_send, xz_recv, xx_send, xx_recv, xp_sem,
    o_send, o_recv, relay_recv, h_send, h_recv,
):
    tok, row = lax.axis_index("tok"), lax.axis_index("row")
    x, h, c = row // 8, (row // 2) % 4, row % 2
    l, y = tok // 4, tok % 4
    chip = x * 4 + h

    def row_of(px, ph, pc):
        return ((px + 4) % 4) * 8 + ((ph + 4) % 4) * 2 + pc

    def remote(src, dst, ssem, rsem, to_row=None, to_tok=None):
        return pltpu.make_async_remote_copy(
            src_ref=src, dst_ref=dst, send_sem=ssem, recv_sem=rsem,
            device_id=(tok if to_tok is None else to_tok, row if to_row is None else to_row),
            device_id_type=MESH,
        )

    loads = [
        pltpu.make_async_copy(s, d, load_sem.at[i])
        for i, (s, d) in enumerate(
            [(fr_hbm, fr), (calib_hbm, cal), (ww_hbm, ww), (keep_hbm, kp), (fw_hbm, fw), (ids_hbm, ids), (rest_hbm, rest_out)]
        )
    ]
    for load in loads[:6]:
        load.start()

    barrier = pltpu.get_barrier_semaphore()

    def greet(d, carry):
        pl.semaphore_signal(barrier, inc=1, device_id=(tok, (row + d) % N_ROW), device_id_type=MESH)
        return carry

    lax.fori_loop(1, N_ROW, greet, 0)
    up_tok, down_tok, other_tok = l * 4 + (y + 1) % 4, l * 4 + (y + 3) % 4, (1 - l) * 4 + y
    for peer in (up_tok, down_tok, other_tok):
        pl.semaphore_signal(barrier, inc=1, device_id=(peer, row), device_id_type=MESH)
    pl.semaphore_wait(barrier, N_ROW - 1 + 3)

    is_source = row == 0

    def scatter(r):
        first = pl.multiple_of((r % 2) * 256 + (r // 2) * 16, 16)
        return remote(
            cal.at[pl.ds(first, 16), pl.ds(0, WIN)], xin.at[r % 2, r // 2], scat_send.at[r], scat_recv.at[0], to_row=r
        )

    loads[0].wait()
    fr_split[0] = fr[:, 0:HALF]
    fr_split[1, :, HALF - 128 :] = jnp.zeros((8, 128), F32)
    fr_split[1, :, 0 : REST - HALF] = fr[:, HALF:REST]
    own_rows = pl.ds(pl.multiple_of(c * 8, 8), 8)
    pair_copy = remote(
        fr_split.at[1 - c], fr_pair.at[own_rows], pair_sem.at[0], pair_sem.at[1], to_row=row_of(x, h, 1 - c)
    )
    pair_copy.start()
    fr_pair[own_rows, :] = fr_split[c]

    loads[1].wait()

    @pl.when(is_source)
    def _():
        def send(r, carry):
            scatter(r).start()
            return carry

        lax.fori_loop(1, N_ROW, send, 0)
        xin[0, 0] = cal[0:16, 0:WIN]

    for i in (2, 3, 4):
        loads[i].wait()
    prune_prepare(ww, kp, fw, cur, scaled_drop, fw_t)

    def f_copy(p, number, slot, to_row, piece=None):
        first, size = p * PHASE_COLS, PHASE_COLS
        if piece is not None:
            first, size = first + piece * PIECE, PIECE
        ref = fac.at[c * CHIPS + slot, :, pl.ds(first, size)]
        rsem = pair_recv.at[p] if number >= PAIR_FIRST else f_recv.at[p, number]
        return remote(ref, ref, f_send.at[0], rsem, to_row=to_row)

    x_up, x_down = row_of(x + 1, h, c), row_of(x - 1, h, c)
    z_up, z_down = row_of(x, h + 1, c), row_of(x, h - 1, c)
    pair = row_of(x, h, 1 - c)
    z_slots = [h, (h + 3) % 4, (h + 1) % 4, (h + 2) % 4]
    x_slots = [x, (x + 3) % 4, (x + 1) % 4, (x + 2) % 4]

    def f_start(*args, **kw):
        f_copy(*args, **kw).start()

    def f_from_z(p, j):
        slot = x * 4 + z_slots[j]
        if j == 1:
            f_start(p, Z_UP_PIECE, slot, z_up, piece=0)
        if j == 2:
            f_start(p, Z_DOWN_PIECE, slot, z_down, piece=1)
        f_start(p, X_FIRST + 4 * j, slot, x_up)
        f_start(p, X_FIRST + 4 * j + 1, slot, x_down)
        f_start(p, PAIR_FIRST + j, slot, pair)

    def f_own(p):
        f_start(p, Z_UP, chip, z_up)
        f_start(p, Z_DOWN, chip, z_down)
        f_from_z(p, 0)

    def f_z_neighbours(p):
        f_copy(p, Z_UP, x * 4 + z_slots[1], z_up).wait_recv()
        f_from_z(p, 1)
        f_copy(p, Z_DOWN, x * 4 + z_slots[2], z_down).wait_recv()
        f_from_z(p, 2)

    def f_z_opposite(p):
        slot = x * 4 + z_slots[3]
        f_copy(p, Z_UP_PIECE, slot, z_up, piece=0).wait_recv()
        f_copy(p, Z_DOWN_PIECE, slot, z_down, piece=1).wait_recv()
        f_from_z(p, 3)

    def f_x_neighbours(p, j):
        n = X_FIRST + 4 * j
        slot = x_slots[1] * 4 + z_slots[j]
        f_copy(p, n, slot, x_up).wait_recv()
        f_start(p, n + 2, slot, x_up, piece=0)
        f_start(p, PAIR_FIRST + 4 + j, slot, pair)
        slot = x_slots[2] * 4 + z_slots[j]
        f_copy(p, n + 1, slot, x_down).wait_recv()
        f_start(p, n + 3, slot, x_down, piece=1)
        f_start(p, PAIR_FIRST + 8 + j, slot, pair)

    def f_x_opposite(p, j):
        n = X_FIRST + 4 * j
        slot = x_slots[3] * 4 + z_slots[j]
        f_copy(p, n + 2, slot, x_up, piece=0).wait_recv()
        f_copy(p, n + 3, slot, x_down, piece=1).wait_recv()
        f_start(p, PAIR_FIRST + 12 + j, slot, pair)

    def f_pair_wait(p):
        ref = fac.at[pl.ds((1 - c) * CHIPS, CHIPS), :, pl.ds(p * PHASE_COLS, PHASE_COLS)]
        remote(ref, ref, f_send.at[0], pair_recv.at[p], to_row=pair).wait_recv()

    pair_copy.wait_recv()
    fac[c * CHIPS + chip] = fr_pair[...].astype(BF16)

    for p in range(PHASES):
        f_own(p)

    def xz_copy(d):
        ref = xin.at[c, chip]
        return remote(ref, ref, xz_send.at[d], xz_recv.at[d], to_row=row_of(x, h + d, c))

    @pl.when(jnp.logical_not(is_source))
    def _():
        remote(xin.at[c, chip], xin.at[c, chip], scat_send.at[0], scat_recv.at[0], to_row=pair).wait_recv()

    for d in (1, 3, 2):
        xz_copy(d).start()
    loads[6].start()

    def prune(first, last):
        for k in range(first, last):
            prune_tile(k, cur, scaled_drop, fw_t, err)

    prune(0, 8)
    f_x_neighbours(0, 0)

    def xx_copy(d):
        ref = xin.at[c, pl.ds(x * 4, 4)]
        return remote(ref, ref, xx_send.at[d], xx_recv.at[d], to_row=row_of(x + d, h, c))

    for d in (1, 3, 2):
        ref = xin.at[c, x * 4 + (h + 4 - d) % 4]
        remote(ref, ref, xz_send.at[d], xz_recv.at[d], to_row=row_of(x, h + d, c)).wait_recv()
    for d in (1, 3, 2):
        xx_copy(d).start()

    prune(8, 16)
    f_z_neighbours(0)
    f_x_neighbours(1, 0)

    for d in (1, 3, 2):
        ref = xin.at[c, pl.ds(((x + 4 - d) % 4) * 4, 4)]
        remote(ref, ref, xx_send.at[d], xx_recv.at[d], to_row=row_of(x + d, h, c)).wait_recv()
    xp_copy = remote(xin.at[c], xin.at[c], xp_sem.at[0], xp_sem.at[1], to_row=pair)
    xp_copy.start()

    prune(16, 22)
    f_z_neighbours(1)
    f_x_neighbours(0, 1)

    remote(xin.at[1 - c], xin.at[1 - c], xp_sem.at[0], xp_sem.at[1], to_row=pair).wait_recv()

    loads[5].wait()
    live = jnp.where(ids[...] != 1, 1.0, 0.0)
    live_t = jnp.concatenate([live, jnp.zeros((4, 128), F32)], axis=0).T
    x_parts = []
    for s in range(4):
        part = xin[s // 2, (s % 2) * 8 : (s % 2) * 8 + 8].reshape(128, WIN).astype(F32)
        x_parts.append(part * live_t[:, s : s + 1])
    x_all = jnp.concatenate(x_parts, axis=0)
    x_t[...] = x_all.T.astype(BF16)
    x_half[...] = x_all.astype(BF16)

    @pl.loop(0, FEATURES // 256)
    def _(i):
        cols = pl.ds(pl.multiple_of(i * 256, 256), 256)
        part = jnp.dot(x_t[...], cal[:, cols], preferred_element_type=F32).reshape(N_TOK, 32, 256)
        gram[:, :, cols] = part
        gram_half[:, :, cols] = part.astype(BF16)

    def h_copy(number, src, dst, to_tok):
        return remote(src, dst, h_send.at[number], h_recv.at[number], to_tok=to_tok)

    h_copies = [
        h_copy(0, gram_half.at[(y + 2) % 4], relay_in.at[0], up_tok),
        h_copy(1, gram_half.at[4 + (y + 2) % 4], relay_in.at[1], down_tok),
        h_copy(2, gram_half.at[4 + (y + 1) % 4], from_left.at[1], up_tok),
        h_copy(3, gram_half.at[(y + 3) % 4], from_right.at[0], down_tok),
        h_copy(4, relay_out.at[0], from_left.at[0], up_tok),
        h_copy(5, relay_out.at[1], from_right.at[1], down_tok),
        h_copy(6, peer_out, peer_in, other_tok),
    ]
    for i in range(4):
        h_copies[i].start()

    prune(22, 27)
    f_z_opposite(0)
    f_x_neighbours(0, 2)
    prune(27, 32)

    pruned_t = cur[...]
    local_outs[...] = jnp.dot(
        x_half[...], pruned_t.astype(BF16), preferred_element_type=F32
    ).astype(BF16).reshape(4, 4, 2, 16, LOCAL_ROWS)

    def out_cols(sender):
        return pl.ds(pl.multiple_of(sender * LOCAL_ROWS, 128), LOCAL_ROWS)

    opposite = (h + 2) % 4
    relays = [
        remote(local_outs.at[:, opposite, 0], out_relay.at[0], o_send.at[0], relay_recv.at[0], to_row=z_up),
        remote(local_outs.at[:, opposite, 1], out_relay.at[1], o_send.at[0], relay_recv.at[1], to_row=z_down),
    ]
    for relay in relays:
        relay.start()
    my_cols = out_cols(row)
    for dx in (2, 1, 3, 0):
        for dh in (1, 3, 0):
            for dc in (0, 1):
                if (dx, dh, dc) != (0, 0, 0):
                    ox, oh, oc = (x + dx) % 4, (h + dh) % 4, (c + dc) % 2
                    remote(
                        local_outs.at[ox, oh, oc], outs_out.at[:, my_cols], o_send.at[0], o_recv.at[0],
                        to_row=row_of(ox, oh, oc),
                    ).start()

    def pass_on(way):
        relays[way].wait_recv()
        sender = row_of(x, h + (3 if way == 0 else 1), c)
        for px in range(4):
            remote(
                out_relay.at[way, px], outs_out.at[:, out_cols(sender)], o_send.at[1], o_recv.at[0],
                to_row=row_of(px, h + (1 if way == 0 else 3), way),
            ).start()

    f_z_opposite(1)
    f_x_neighbours(1, 1)

    h_copies[0].wait_recv()
    relay_out[0] = (relay_in[0].astype(F32) + gram[(y + 1) % 4]).astype(BF16)
    h_copies[4].start()
    h_copies[1].wait_recv()
    relay_out[1] = (relay_in[1].astype(F32) + gram[4 + (y + 3) % 4]).astype(BF16)
    h_copies[5].start()

    f_x_neighbours(1, 2)
    f_x_neighbours(0, 3)
    pass_on(0)
    pass_on(1)
    f_x_opposite(0, 0)
    f_x_opposite(0, 1)
    f_x_neighbours(1, 3)
    f_x_opposite(0, 2)
    f_x_opposite(1, 0)

    outs_out[:, my_cols] = local_outs[x, h, c]
    pruned_out[...] = pruned_t.T
    err_half[...] = err[...].astype(BF16)

    for i in range(2, 6):
        h_copies[i].wait_recv()
    peer_out[...] = (
        gram[(1 - l) * 4 + y] + from_left[1 - l].astype(F32) + from_right[1 - l].astype(F32)
    ).astype(BF16)
    h_copies[6].start()

    f_x_opposite(0, 3)
    f_x_opposite(1, 1)

    loads[6].wait()
    for p in range(PHASES - 1):
        f_pair_wait(p)
        for half in range(2):

            @pl.loop(0, PHASE_COLS // STEP)
            def _(i, half=half, p=p):
                first = pl.multiple_of(p * PHASE_COLS + i * STEP, STEP)
                rows = pl.ds(pl.multiple_of(half * HALF + first, STEP), STEP)
                factor = fac[half * CHIPS : (half + 1) * CHIPS, :, pl.ds(first, STEP)]
                rest_out[rows, :] = compensate(rest_out[rows, :], factor, err_half[...])

    f_x_opposite(1, 2)
    f_x_opposite(1, 3)

    h_copies[6].wait_recv()
    total = gram[l * 4 + y] + from_left[l].astype(F32) + from_right[l].astype(F32) + peer_in[...].astype(F32)
    hess_out[...] = total * (2.0 / TOKENS)

    arrived = outs_out.at[:, pl.ds(0, (N_ROW - 1) * LOCAL_ROWS)]
    remote(arrived, arrived, o_send.at[0], o_recv.at[0], to_row=pair).wait_recv()
    f_pair_wait(PHASES - 1)

    remote(arrived, arrived, o_send.at[0], o_recv.at[0], to_row=pair).wait_send()
    remote(out_relay, out_relay, o_send.at[1], o_recv.at[0], to_row=pair).wait_send()

    @pl.when(is_source)
    def _():
        def left(r, carry):
            scatter(r).wait_send()
            return carry

        lax.fori_loop(1, N_ROW, left, 0)

    pair_copy.wait_send()
    for d in (1, 3, 2):
        xz_copy(d).wait_send()
        xx_copy(d).wait_send()
    xp_copy.wait_send()
    for copy in h_copies:
        copy.wait_send()
    sent = fac.at[pl.ds(0, 31)]
    remote(sent, sent, f_send.at[0], pair_recv.at[0], to_row=pair).wait_send()


def finish_kernel(
    pruned, rest, hess, outs, fac, err_half,
    pruned_hbm, rest_hbm, hess_hbm, outs_hbm,
    updated, sem,
):
    copies = [
        pltpu.make_async_copy(pruned, pruned_hbm, sem.at[0]),
        pltpu.make_async_copy(hess, hess_hbm, sem.at[1]),
        pltpu.make_async_copy(outs, outs_hbm, sem.at[2]),
    ]
    last = HALF - PHASE_COLS
    for half in range(2):
        rows = pl.ds(half * HALF, last)
        copies.append(pltpu.make_async_copy(rest.at[rows], rest_hbm.at[rows], sem.at[3 + half]))
    for copy in copies:
        copy.start()
    for half in range(2):
        for i in range(PHASE_COLS // STEP):
            first = last + i * STEP
            start = half * HALF + first
            count = min(STEP, REST - start)
            part = rest[start : start + count, :]
            at = half * PHASE_COLS + i * STEP
            updated[at : at + count, :] = compensate(
                part, fac[half * CHIPS : (half + 1) * CHIPS, :, first : first + STEP], err_half[...]
            )
            copy = pltpu.make_async_copy(
                updated.at[pl.ds(at, count)], rest_hbm.at[pl.ds(start, count)], sem.at[5 + half * (PHASE_COLS // STEP) + i]
            )
            copy.start()
            copies.append(copy)
    for copy in copies:
        copy.wait()


def on_device(token_ids, calib_input, keep_mask, weight_window, weight_rest, factor_window, factor_rest):
    vmem, dma = pltpu.VMEM, pltpu.SemaphoreType.DMA
    slab = (32, FEATURES)
    in_hbm = [
        pltpu.with_memory_space_constraint(a, pltpu.HBM)
        for a in (
            token_ids.reshape(4, 128), calib_input, keep_mask, weight_window, weight_rest.T, factor_window, factor_rest
        )
    ]
    shapes = [
        ((LOCAL_ROWS, WIN), F32),
        ((REST, LOCAL_ROWS), BF16),
        (slab, F32),
        ((16, N_ROW * LOCAL_ROWS), BF16),
    ]
    held = pl.pallas_call(
        kernel,
        out_shape=tuple(
            vmem(*s) for s in shapes + [((2 * CHIPS, 16, HALF), BF16), ((WIN, LOCAL_ROWS), BF16)]
        ),
        in_specs=[pl.BlockSpec(memory_space=pltpu.HBM)] * 7,
        out_specs=[pl.BlockSpec(memory_space=vmem)] * 6,
        scratch_shapes=[
            vmem((4, 128), jnp.int32),
            vmem((LOCAL_TOKENS, FEATURES), BF16),
            vmem((LOCAL_ROWS, WIN), jnp.int32),
            vmem((LOCAL_ROWS, WIN), F32),
            vmem((WIN, WIN), F32),
            vmem((8, REST), F32),
            vmem((2, 8, HALF), F32),
            vmem((16, HALF), F32),
            vmem((2, CHIPS, 16, WIN), BF16),
            vmem((WIN, LOCAL_TOKENS), BF16),
            vmem((WIN, LOCAL_ROWS), F32),
            vmem((WIN, LOCAL_ROWS), F32),
            vmem((WIN, LOCAL_ROWS), F32),
            vmem((WIN, WIN), F32),
            vmem((LOCAL_TOKENS, WIN), BF16),
            vmem((4, 4, 2, 16, LOCAL_ROWS), BF16),
            vmem((2, 4, 16, LOCAL_ROWS), BF16),
            vmem((N_TOK,) + slab, F32),
            vmem((N_TOK,) + slab, BF16),
            vmem((2,) + slab, BF16),
            vmem((2,) + slab, BF16),
            vmem((2,) + slab, BF16),
            vmem((2,) + slab, BF16),
            vmem(slab, BF16),
            vmem(slab, BF16),
            dma((7,)),
            dma((2,)),
            dma((1,)),
            dma((PHASES, F_MESSAGES)),
            dma((PHASES,)),
            dma((N_ROW,)),
            dma((1,)),
            dma((4,)),
            dma((4,)),
            dma((4,)),
            dma((4,)),
            dma((2,)),
            dma((2,)),
            dma((1,)),
            dma((2,)),
            dma((7,)),
            dma((7,)),
        ],
        compiler_params=pltpu.CompilerParams(
            collective_id=0, has_side_effects=True, vmem_limit_bytes=32 * 1024 * 1024
        ),
        cost_estimate=pl.CostEstimate(flops=2_000_000_000, bytes_accessed=16_000_000, transcendentals=0),
    )(*in_hbm)
    pruned, rest_t, hess, outs = pl.pallas_call(
        finish_kernel,
        out_shape=tuple(jax.ShapeDtypeStruct(*s) for s in shapes),
        in_specs=[pl.BlockSpec(memory_space=vmem)] * 6,
        out_specs=[pl.BlockSpec(memory_space=pltpu.HBM)] * 4,
        scratch_shapes=[
            vmem((2 * PHASE_COLS, LOCAL_ROWS), BF16),
            dma((5 + 2 * (PHASE_COLS // STEP),)),
        ],
        compiler_params=pltpu.CompilerParams(vmem_limit_bytes=32 * 1024 * 1024),
        cost_estimate=pl.CostEstimate(flops=600_000_000, bytes_accessed=12_000_000, transcendentals=0),
    )(*[pltpu.with_memory_space_constraint(a, vmem) for a in held])
    return pruned, rest_t.T, hess, outs


def solution(mesh):
    return jax.shard_map(
        on_device,
        mesh=mesh,
        in_specs=(
            P("tok"),
            P("tok", "row"),
            P("row", None),
            P("row", None),
            P("row", "tok"),
            P(),
            P("row", "tok"),
        ),
        out_specs=(P("row", None), P("row", "tok"), P("tok", "row"), P(("tok", "row"), None)),
        check_vma=False,
    )
```

```python
import jax
import jax.numpy as jnp
from jax import lax
from jax.experimental import pallas as pl
from jax.experimental.pallas import tpu as pltpu
from jax.sharding import PartitionSpec as P

MESH = pl.DeviceIdType.MESH
F32, BF16 = jnp.float32, jnp.bfloat16

WIN = 256
BLOCK = 128
SUB = 8
LOCAL_ROWS = 384
LOCAL_TOKENS = 512
FEATURES = 1536
REST = 6112
HALF = 3072
N_ROW = 32
N_TOK = 8
CHIPS = 16
TOKENS = LOCAL_TOKENS * N_TOK

PHASES = 2
PHASE_COLS = HALF // PHASES
PIECE = PHASE_COLS // 2
STEP = 512

Z_UP, Z_DOWN, Z_UP_PIECE, Z_DOWN_PIECE = 0, 1, 2, 3
X_FIRST = 4
PAIR_FIRST = 20
F_MESSAGES = 20


def prune_prepare(ww, kp, fw, cur, scaled_drop, fw_t):
    factor = fw[...]
    fw_t[...] = factor.T
    row_id = lax.broadcasted_iota(jnp.int32, (WIN, WIN), 0)
    col_id = lax.broadcasted_iota(jnp.int32, (WIN, WIN), 1)
    diagonal = jnp.sum(jnp.where(row_id == col_id, factor, 0.0), axis=1, keepdims=True)
    drop = (1 - kp[...]).astype(F32).T
    scaled_drop[...] = drop * (1.0 / diagonal)
    cur[...] = ww[...].T


def prune_tile(k, cur, scaled_drop, fw_t, fw_s, err):
    low = k * SUB
    block_end = (low // BLOCK + 1) * BLOCK
    shape = (SUB, LOCAL_ROWS)
    tile = cur[low : low + SUB, :]
    drop = scaled_drop[low : low + SUB, :]
    place = lax.broadcasted_iota(jnp.int32, shape, 0)
    values = [jnp.broadcast_to(tile[s : s + 1, :], shape) for s in range(SUB)]
    errors = []
    tile_err = jnp.zeros(shape, F32)
    tile_out = jnp.zeros(shape, F32)
    for s in range(SUB):
        e = values[s] * jnp.broadcast_to(drop[s : s + 1, :], shape)
        for t in range(s + 1, SUB):
            values[t] = values[t] - fw_s[low + s, low + t] * e
        errors.append(e)
        tile_err = jnp.where(place == s, e, tile_err)
        tile_out = jnp.where(place == s, values[s] - fw_s[low + s, low + s] * e, tile_out)
    cur[low : low + SUB, :] = tile_out
    err[low : low + SUB, :] = tile_err
    start = low + SUB
    while start < block_end:
        end = min(start + 32, block_end)
        n = (end - start) // SUB
        part = cur[start:end, :].reshape(n, SUB, LOCAL_ROWS)
        for s in range(SUB):
            part = part - fw_t[start:end, low + s : low + s + 1].reshape(n, SUB, 1) * errors[s][None]
        cur[start:end, :] = part.reshape(n * SUB, LOCAL_ROWS)
        start = end
    if block_end == low + SUB and block_end < WIN:
        b = block_end - BLOCK
        cur[block_end:, :] = cur[block_end:, :] - jnp.dot(
            fw_t[block_end:, b:block_end], err[b:block_end, :],
            precision=lax.Precision.HIGHEST, preferred_element_type=F32,
        )


def compensate(rest, factor, err_half):
    change = lax.dot_general(
        factor.reshape(WIN, -1), err_half, (((0,), (0,)), ((), ())), preferred_element_type=F32
    )
    return (rest.astype(F32) - change[: rest.shape[0]]).astype(BF16)


def kernel(
    ids_hbm, calib_hbm, keep_hbm, ww_hbm, rest_hbm, fw_hbm, fr_hbm,
    pruned_out, rest_out, hess_out, outs_out, fac, err_half,
    ids, cal, kp, ww, fw, fw_s, fr, fr_split, fr_pair, xin, x_t, cur, scaled_drop, err, fw_t, x_half, local_outs, out_relay,
    gram, gram_half, relay_in, relay_out, from_left, from_right, peer_out, peer_in,
    load_sem, pair_sem, f_send, f_recv, pair_recv, scat_send, scat_recv, xz_send, xz_recv, xx_send, xx_recv, xp_sem,
    o_send, o_recv, relay_recv, h_send, h_recv,
):
    tok, row = lax.axis_index("tok"), lax.axis_index("row")
    x, h, c = row // 8, (row // 2) % 4, row % 2
    l, y = tok // 4, tok % 4
    chip = x * 4 + h

    def row_of(px, ph, pc):
        return ((px + 4) % 4) * 8 + ((ph + 4) % 4) * 2 + pc

    def remote(src, dst, ssem, rsem, to_row=None, to_tok=None):
        return pltpu.make_async_remote_copy(
            src_ref=src, dst_ref=dst, send_sem=ssem, recv_sem=rsem,
            device_id=(tok if to_tok is None else to_tok, row if to_row is None else to_row),
            device_id_type=MESH,
        )

    loads = [
        pltpu.make_async_copy(s, d, load_sem.at[i])
        for i, (s, d) in enumerate(
            [(fr_hbm, fr), (calib_hbm, cal), (ww_hbm, ww), (keep_hbm, kp), (fw_hbm, fw), (ids_hbm, ids), (rest_hbm, rest_out), (fw_hbm, fw_s)]
        )
    ]
    for load in loads[:6] + loads[7:]:
        load.start()

    barrier = pltpu.get_barrier_semaphore()

    def greet(d, carry):
        pl.semaphore_signal(barrier, inc=1, device_id=(tok, (row + d) % N_ROW), device_id_type=MESH)
        return carry

    lax.fori_loop(1, N_ROW, greet, 0)
    up_tok, down_tok, other_tok = l * 4 + (y + 1) % 4, l * 4 + (y + 3) % 4, (1 - l) * 4 + y
    for peer in (up_tok, down_tok, other_tok):
        pl.semaphore_signal(barrier, inc=1, device_id=(peer, row), device_id_type=MESH)
    pl.semaphore_wait(barrier, N_ROW - 1 + 3)

    is_source = row == 0

    def scatter(r):
        first = pl.multiple_of((r % 2) * 256 + (r // 2) * 16, 16)
        return remote(
            cal.at[pl.ds(first, 16), pl.ds(0, WIN)], xin.at[r % 2, r // 2], scat_send.at[r], scat_recv.at[0], to_row=r
        )

    loads[0].wait()
    fr_split[0] = fr[:, 0:HALF]
    fr_split[1, :, HALF - 128 :] = jnp.zeros((8, 128), F32)
    fr_split[1, :, 0 : REST - HALF] = fr[:, HALF:REST]
    own_rows = pl.ds(pl.multiple_of(c * 8, 8), 8)
    pair_copy = remote(
        fr_split.at[1 - c], fr_pair.at[own_rows], pair_sem.at[0], pair_sem.at[1], to_row=row_of(x, h, 1 - c)
    )
    pair_copy.start()
    fr_pair[own_rows, :] = fr_split[c]

    loads[1].wait()

    @pl.when(is_source)
    def _():
        def send(r, carry):
            scatter(r).start()
            return carry

        lax.fori_loop(1, N_ROW, send, 0)
        xin[0, 0] = cal[0:16, 0:WIN]

    for i in (2, 3, 4, 7):
        loads[i].wait()
    prune_prepare(ww, kp, fw, cur, scaled_drop, fw_t)

    def f_copy(p, number, slot, to_row, piece=None):
        first, size = p * PHASE_COLS, PHASE_COLS
        if piece is not None:
            first, size = first + piece * PIECE, PIECE
        ref = fac.at[c * CHIPS + slot, :, pl.ds(first, size)]
        rsem = pair_recv.at[p] if number >= PAIR_FIRST else f_recv.at[p, number]
        return remote(ref, ref, f_send.at[0], rsem, to_row=to_row)

    x_up, x_down = row_of(x + 1, h, c), row_of(x - 1, h, c)
    z_up, z_down = row_of(x, h + 1, c), row_of(x, h - 1, c)
    pair = row_of(x, h, 1 - c)
    z_slots = [h, (h + 3) % 4, (h + 1) % 4, (h + 2) % 4]
    x_slots = [x, (x + 3) % 4, (x + 1) % 4, (x + 2) % 4]

    def f_start(*args, **kw):
        f_copy(*args, **kw).start()

    def f_from_z(p, j):
        slot = x * 4 + z_slots[j]
        if j == 1:
            f_start(p, Z_UP_PIECE, slot, z_up, piece=0)
        if j == 2:
            f_start(p, Z_DOWN_PIECE, slot, z_down, piece=1)
        f_start(p, X_FIRST + 4 * j, slot, x_up)
        f_start(p, X_FIRST + 4 * j + 1, slot, x_down)
        f_start(p, PAIR_FIRST + j, slot, pair)

    def f_own(p):
        f_start(p, Z_UP, chip, z_up)
        f_start(p, Z_DOWN, chip, z_down)
        f_from_z(p, 0)

    def f_z_neighbours(p):
        f_copy(p, Z_UP, x * 4 + z_slots[1], z_up).wait_recv()
        f_from_z(p, 1)
        f_copy(p, Z_DOWN, x * 4 + z_slots[2], z_down).wait_recv()
        f_from_z(p, 2)

    def f_z_opposite(p):
        slot = x * 4 + z_slots[3]
        f_copy(p, Z_UP_PIECE, slot, z_up, piece=0).wait_recv()
        f_copy(p, Z_DOWN_PIECE, slot, z_down, piece=1).wait_recv()
        f_from_z(p, 3)

    def f_x_neighbours(p, j):
        n = X_FIRST + 4 * j
        slot = x_slots[1] * 4 + z_slots[j]
        f_copy(p, n, slot, x_up).wait_recv()
        f_start(p, n + 2, slot, x_up, piece=0)
        f_start(p, PAIR_FIRST + 4 + j, slot, pair)
        slot = x_slots[2] * 4 + z_slots[j]
        f_copy(p, n + 1, slot, x_down).wait_recv()
        f_start(p, n + 3, slot, x_down, piece=1)
        f_start(p, PAIR_FIRST + 8 + j, slot, pair)

    def f_x_opposite(p, j):
        n = X_FIRST + 4 * j
        slot = x_slots[3] * 4 + z_slots[j]
        f_copy(p, n + 2, slot, x_up, piece=0).wait_recv()
        f_copy(p, n + 3, slot, x_down, piece=1).wait_recv()
        f_start(p, PAIR_FIRST + 12 + j, slot, pair)

    def f_pair_wait(p):
        ref = fac.at[pl.ds((1 - c) * CHIPS, CHIPS), :, pl.ds(p * PHASE_COLS, PHASE_COLS)]
        remote(ref, ref, f_send.at[0], pair_recv.at[p], to_row=pair).wait_recv()

    pair_copy.wait_recv()
    fac[c * CHIPS + chip] = fr_pair[...].astype(BF16)

    for p in range(PHASES):
        f_own(p)

    def xz_copy(d):
        ref = xin.at[c, chip]
        return remote(ref, ref, xz_send.at[d], xz_recv.at[d], to_row=row_of(x, h + d, c))

    @pl.when(jnp.logical_not(is_source))
    def _():
        remote(xin.at[c, chip], xin.at[c, chip], scat_send.at[0], scat_recv.at[0], to_row=pair).wait_recv()

    for d in (1, 3, 2):
        xz_copy(d).start()
    loads[6].start()

    def prune(first, last):
        for k in range(first, last):
            prune_tile(k, cur, scaled_drop, fw_t, fw_s, err)

    prune(0, 8)
    f_x_neighbours(0, 0)

    def xx_copy(d):
        ref = xin.at[c, pl.ds(x * 4, 4)]
        return remote(ref, ref, xx_send.at[d], xx_recv.at[d], to_row=row_of(x + d, h, c))

    for d in (1, 3, 2):
        ref = xin.at[c, x * 4 + (h + 4 - d) % 4]
        remote(ref, ref, xz_send.at[d], xz_recv.at[d], to_row=row_of(x, h + d, c)).wait_recv()
    for d in (1, 3, 2):
        xx_copy(d).start()

    prune(8, 16)
    f_z_neighbours(0)
    f_x_neighbours(1, 0)

    for d in (1, 3, 2):
        ref = xin.at[c, pl.ds(((x + 4 - d) % 4) * 4, 4)]
        remote(ref, ref, xx_send.at[d], xx_recv.at[d], to_row=row_of(x + d, h, c)).wait_recv()
    xp_copy = remote(xin.at[c], xin.at[c], xp_sem.at[0], xp_sem.at[1], to_row=pair)
    xp_copy.start()

    prune(16, 22)
    f_z_neighbours(1)
    f_x_neighbours(0, 1)

    remote(xin.at[1 - c], xin.at[1 - c], xp_sem.at[0], xp_sem.at[1], to_row=pair).wait_recv()

    loads[5].wait()
    live = jnp.where(ids[...] != 1, 1.0, 0.0)
    live_t = jnp.concatenate([live, jnp.zeros((4, 128), F32)], axis=0).T
    x_parts = []
    for s in range(4):
        part = xin[s // 2, (s % 2) * 8 : (s % 2) * 8 + 8].reshape(128, WIN).astype(F32)
        x_parts.append(part * live_t[:, s : s + 1])
    x_all = jnp.concatenate(x_parts, axis=0)
    x_t[...] = x_all.T.astype(BF16)
    x_half[...] = x_all.astype(BF16)

    @pl.loop(0, FEATURES // 256)
    def _(i):
        cols = pl.ds(pl.multiple_of(i * 256, 256), 256)
        part = jnp.dot(x_t[...], cal[:, cols], preferred_element_type=F32).reshape(N_TOK, 32, 256)
        gram[:, :, cols] = part
        gram_half[:, :, cols] = part.astype(BF16)

    def h_copy(number, src, dst, to_tok):
        return remote(src, dst, h_send.at[number], h_recv.at[number], to_tok=to_tok)

    h_copies = [
        h_copy(0, gram_half.at[(y + 2) % 4], relay_in.at[0], up_tok),
        h_copy(1, gram_half.at[4 + (y + 2) % 4], relay_in.at[1], down_tok),
        h_copy(2, gram_half.at[4 + (y + 1) % 4], from_left.at[1], up_tok),
        h_copy(3, gram_half.at[(y + 3) % 4], from_right.at[0], down_tok),
        h_copy(4, relay_out.at[0], from_left.at[0], up_tok),
        h_copy(5, relay_out.at[1], from_right.at[1], down_tok),
        h_copy(6, peer_out, peer_in, other_tok),
    ]
    for i in range(4):
        h_copies[i].start()

    prune(22, 27)
    f_z_opposite(0)
    f_x_neighbours(0, 2)
    prune(27, 32)

    pruned_t = cur[...]
    local_outs[...] = jnp.dot(
        x_half[...], pruned_t.astype(BF16), preferred_element_type=F32
    ).astype(BF16).reshape(4, 4, 2, 16, LOCAL_ROWS)

    def out_cols(sender):
        return pl.ds(pl.multiple_of(sender * LOCAL_ROWS, 128), LOCAL_ROWS)

    opposite = (h + 2) % 4
    relays = [
        remote(local_outs.at[:, opposite, 0], out_relay.at[0], o_send.at[0], relay_recv.at[0], to_row=z_up),
        remote(local_outs.at[:, opposite, 1], out_relay.at[1], o_send.at[0], relay_recv.at[1], to_row=z_down),
    ]
    for relay in relays:
        relay.start()
    my_cols = out_cols(row)
    for dx in (2, 1, 3, 0):
        for dh in (1, 3, 0):
            for dc in (0, 1):
                if (dx, dh, dc) != (0, 0, 0):
                    ox, oh, oc = (x + dx) % 4, (h + dh) % 4, (c + dc) % 2
                    remote(
                        local_outs.at[ox, oh, oc], outs_out.at[:, my_cols], o_send.at[0], o_recv.at[0],
                        to_row=row_of(ox, oh, oc),
                    ).start()

    def pass_on(way):
        relays[way].wait_recv()
        sender = row_of(x, h + (3 if way == 0 else 1), c)
        for px in range(4):
            remote(
                out_relay.at[way, px], outs_out.at[:, out_cols(sender)], o_send.at[1], o_recv.at[0],
                to_row=row_of(px, h + (1 if way == 0 else 3), way),
            ).start()

    f_z_opposite(1)
    f_x_neighbours(1, 1)

    h_copies[0].wait_recv()
    relay_out[0] = (relay_in[0].astype(F32) + gram[(y + 1) % 4]).astype(BF16)
    h_copies[4].start()
    h_copies[1].wait_recv()
    relay_out[1] = (relay_in[1].astype(F32) + gram[4 + (y + 3) % 4]).astype(BF16)
    h_copies[5].start()

    f_x_neighbours(1, 2)
    f_x_neighbours(0, 3)
    pass_on(0)
    pass_on(1)
    f_x_opposite(0, 0)
    f_x_opposite(0, 1)
    f_x_neighbours(1, 3)
    f_x_opposite(0, 2)
    f_x_opposite(1, 0)

    outs_out[:, my_cols] = local_outs[x, h, c]
    pruned_out[...] = pruned_t.T
    err_half[...] = err[...].astype(BF16)

    for i in range(2, 6):
        h_copies[i].wait_recv()
    peer_out[...] = (
        gram[(1 - l) * 4 + y] + from_left[1 - l].astype(F32) + from_right[1 - l].astype(F32)
    ).astype(BF16)
    h_copies[6].start()

    f_x_opposite(0, 3)
    f_x_opposite(1, 1)

    loads[6].wait()
    for p in range(PHASES - 1):
        f_pair_wait(p)
        for half in range(2):

            @pl.loop(0, PHASE_COLS // STEP)
            def _(i, half=half, p=p):
                first = pl.multiple_of(p * PHASE_COLS + i * STEP, STEP)
                rows = pl.ds(pl.multiple_of(half * HALF + first, STEP), STEP)
                factor = fac[half * CHIPS : (half + 1) * CHIPS, :, pl.ds(first, STEP)]
                rest_out[rows, :] = compensate(rest_out[rows, :], factor, err_half[...])

    f_x_opposite(1, 2)
    f_x_opposite(1, 3)

    h_copies[6].wait_recv()
    total = gram[l * 4 + y] + from_left[l].astype(F32) + from_right[l].astype(F32) + peer_in[...].astype(F32)
    hess_out[...] = total * (2.0 / TOKENS)

    arrived = outs_out.at[:, pl.ds(0, (N_ROW - 1) * LOCAL_ROWS)]
    remote(arrived, arrived, o_send.at[0], o_recv.at[0], to_row=pair).wait_recv()
    f_pair_wait(PHASES - 1)

    remote(arrived, arrived, o_send.at[0], o_recv.at[0], to_row=pair).wait_send()
    remote(out_relay, out_relay, o_send.at[1], o_recv.at[0], to_row=pair).wait_send()

    @pl.when(is_source)
    def _():
        def left(r, carry):
            scatter(r).wait_send()
            return carry

        lax.fori_loop(1, N_ROW, left, 0)

    pair_copy.wait_send()
    for d in (1, 3, 2):
        xz_copy(d).wait_send()
        xx_copy(d).wait_send()
    xp_copy.wait_send()
    for copy in h_copies:
        copy.wait_send()
    sent = fac.at[pl.ds(0, 31)]
    remote(sent, sent, f_send.at[0], pair_recv.at[0], to_row=pair).wait_send()


def finish_kernel(
    pruned, rest, hess, outs, fac, err_half,
    pruned_hbm, rest_hbm, hess_hbm, outs_hbm,
    updated, sem,
):
    copies = [
        pltpu.make_async_copy(pruned, pruned_hbm, sem.at[0]),
        pltpu.make_async_copy(hess, hess_hbm, sem.at[1]),
        pltpu.make_async_copy(outs, outs_hbm, sem.at[2]),
    ]
    last = HALF - PHASE_COLS
    for half in range(2):
        rows = pl.ds(half * HALF, last)
        copies.append(pltpu.make_async_copy(rest.at[rows], rest_hbm.at[rows], sem.at[3 + half]))
    for copy in copies:
        copy.start()
    for half in range(2):
        for i in range(PHASE_COLS // STEP):
            first = last + i * STEP
            start = half * HALF + first
            count = min(STEP, REST - start)
            part = rest[start : start + count, :]
            at = half * PHASE_COLS + i * STEP
            updated[at : at + count, :] = compensate(
                part, fac[half * CHIPS : (half + 1) * CHIPS, :, first : first + STEP], err_half[...]
            )
            copy = pltpu.make_async_copy(
                updated.at[pl.ds(at, count)], rest_hbm.at[pl.ds(start, count)], sem.at[5 + half * (PHASE_COLS // STEP) + i]
            )
            copy.start()
            copies.append(copy)
    for copy in copies:
        copy.wait()


def on_device(token_ids, calib_input, keep_mask, weight_window, weight_rest, factor_window, factor_rest):
    vmem, dma = pltpu.VMEM, pltpu.SemaphoreType.DMA
    slab = (32, FEATURES)
    in_hbm = [
        pltpu.with_memory_space_constraint(a, pltpu.HBM)
        for a in (
            token_ids.reshape(4, 128), calib_input, keep_mask, weight_window, weight_rest.T, factor_window, factor_rest
        )
    ]
    shapes = [
        ((LOCAL_ROWS, WIN), F32),
        ((REST, LOCAL_ROWS), BF16),
        (slab, F32),
        ((16, N_ROW * LOCAL_ROWS), BF16),
    ]
    held = pl.pallas_call(
        kernel,
        out_shape=tuple(
            vmem(*s) for s in shapes + [((2 * CHIPS, 16, HALF), BF16), ((WIN, LOCAL_ROWS), BF16)]
        ),
        in_specs=[pl.BlockSpec(memory_space=pltpu.HBM)] * 7,
        out_specs=[pl.BlockSpec(memory_space=vmem)] * 6,
        scratch_shapes=[
            vmem((4, 128), jnp.int32),
            vmem((LOCAL_TOKENS, FEATURES), BF16),
            vmem((LOCAL_ROWS, WIN), jnp.int32),
            vmem((LOCAL_ROWS, WIN), F32),
            vmem((WIN, WIN), F32),
            pltpu.SMEM((WIN, WIN), F32),
            vmem((8, REST), F32),
            vmem((2, 8, HALF), F32),
            vmem((16, HALF), F32),
            vmem((2, CHIPS, 16, WIN), BF16),
            vmem((WIN, LOCAL_TOKENS), BF16),
            vmem((WIN, LOCAL_ROWS), F32),
            vmem((WIN, LOCAL_ROWS), F32),
            vmem((WIN, LOCAL_ROWS), F32),
            vmem((WIN, WIN), F32),
            vmem((LOCAL_TOKENS, WIN), BF16),
            vmem((4, 4, 2, 16, LOCAL_ROWS), BF16),
            vmem((2, 4, 16, LOCAL_ROWS), BF16),
            vmem((N_TOK,) + slab, F32),
            vmem((N_TOK,) + slab, BF16),
            vmem((2,) + slab, BF16),
            vmem((2,) + slab, BF16),
            vmem((2,) + slab, BF16),
            vmem((2,) + slab, BF16),
            vmem(slab, BF16),
            vmem(slab, BF16),
            dma((8,)),
            dma((2,)),
            dma((1,)),
            dma((PHASES, F_MESSAGES)),
            dma((PHASES,)),
            dma((N_ROW,)),
            dma((1,)),
            dma((4,)),
            dma((4,)),
            dma((4,)),
            dma((4,)),
            dma((2,)),
            dma((2,)),
            dma((1,)),
            dma((2,)),
            dma((7,)),
            dma((7,)),
        ],
        compiler_params=pltpu.CompilerParams(
            collective_id=0, has_side_effects=True, vmem_limit_bytes=32 * 1024 * 1024
        ),
        cost_estimate=pl.CostEstimate(flops=2_000_000_000, bytes_accessed=16_000_000, transcendentals=0),
    )(*in_hbm)
    pruned, rest_t, hess, outs = pl.pallas_call(
        finish_kernel,
        out_shape=tuple(jax.ShapeDtypeStruct(*s) for s in shapes),
        in_specs=[pl.BlockSpec(memory_space=vmem)] * 6,
        out_specs=[pl.BlockSpec(memory_space=pltpu.HBM)] * 4,
        scratch_shapes=[
            vmem((2 * PHASE_COLS, LOCAL_ROWS), BF16),
            dma((5 + 2 * (PHASE_COLS // STEP),)),
        ],
        compiler_params=pltpu.CompilerParams(vmem_limit_bytes=32 * 1024 * 1024),
        cost_estimate=pl.CostEstimate(flops=600_000_000, bytes_accessed=12_000_000, transcendentals=0),
    )(*[pltpu.with_memory_space_constraint(a, vmem) for a in held])
    return pruned, rest_t.T, hess, outs


def solution(mesh):
    return jax.shard_map(
        on_device,
        mesh=mesh,
        in_specs=(
            P("tok"),
            P("tok", "row"),
            P("row", None),
            P("row", None),
            P("row", "tok"),
            P(),
            P("row", "tok"),
        ),
        out_specs=(P("row", None), P("row", "tok"), P("tok", "row"), P(("tok", "row"), None)),
        check_vma=False,
    )
```

```python
import jax
import jax.numpy as jnp
from jax import lax
from jax.experimental import pallas as pl
from jax.experimental.pallas import tpu as pltpu
from jax.sharding import PartitionSpec as P

MESH = pl.DeviceIdType.MESH
F32, BF16 = jnp.float32, jnp.bfloat16

WIN = 256
BLOCK = 128
SUB = 8
LOCAL_ROWS = 384
LOCAL_TOKENS = 512
FEATURES = 1536
REST = 6112
HALF = 3072
N_ROW = 32
N_TOK = 8
CHIPS = 16
TOKENS = LOCAL_TOKENS * N_TOK

PHASES = 2
PHASE_COLS = HALF // PHASES
PIECE = PHASE_COLS // 2
STEP = 512

Z_UP, Z_DOWN, Z_UP_PIECE, Z_DOWN_PIECE = 0, 1, 2, 3
X_FIRST = 4
PAIR_FIRST = 20
F_MESSAGES = 20


def prune_prepare(ww, kp, fw, cur, scaled_drop, fw_t):
    factor = fw[...]
    fw_t[...] = factor.T
    row_id = lax.broadcasted_iota(jnp.int32, (WIN, WIN), 0)
    col_id = lax.broadcasted_iota(jnp.int32, (WIN, WIN), 1)
    diagonal = jnp.sum(jnp.where(row_id == col_id, factor, 0.0), axis=1, keepdims=True)
    drop = (1 - kp[...]).astype(F32).T
    scaled_drop[...] = drop * (1.0 / diagonal)
    cur[...] = ww[...].T


def prune_tile(k, cur, scaled_drop, fw_t, fw_s, err):
    low = k * SUB
    block_end = (low // BLOCK + 1) * BLOCK
    shape = (SUB, LOCAL_ROWS)
    tile = cur[low : low + SUB, :]
    drop = scaled_drop[low : low + SUB, :]
    place = lax.broadcasted_iota(jnp.int32, shape, 0)
    values = [jnp.broadcast_to(tile[s : s + 1, :], shape) for s in range(SUB)]
    errors = []
    tile_err = jnp.zeros(shape, F32)
    tile_out = jnp.zeros(shape, F32)
    for s in range(SUB):
        e = values[s] * jnp.broadcast_to(drop[s : s + 1, :], shape)
        for t in range(s + 1, SUB):
            values[t] = values[t] - fw_s[low + s, low + t] * e
        errors.append(e)
        tile_err = jnp.where(place == s, e, tile_err)
        tile_out = jnp.where(place == s, values[s] - fw_s[low + s, low + s] * e, tile_out)
    cur[low : low + SUB, :] = tile_out
    err[low : low + SUB, :] = tile_err
    start = low + SUB
    while start < block_end:
        end = min(start + 32, block_end)
        n = (end - start) // SUB
        part = cur[start:end, :].reshape(n, SUB, LOCAL_ROWS)
        for s in range(SUB):
            part = part - fw_t[start:end, low + s : low + s + 1].reshape(n, SUB, 1) * errors[s][None]
        cur[start:end, :] = part.reshape(n * SUB, LOCAL_ROWS)
        start = end
    if block_end == low + SUB and block_end < WIN:
        b = block_end - BLOCK
        cur[block_end:, :] = cur[block_end:, :] - jnp.dot(
            fw_t[block_end:, b:block_end], err[b:block_end, :],
            precision=lax.Precision.HIGHEST, preferred_element_type=F32,
        )


def compensate(rest, factor, err_half):
    change = lax.dot_general(
        factor.reshape(WIN, -1), err_half, (((0,), (0,)), ((), ())), preferred_element_type=F32
    )
    return (rest.astype(F32) - change[: rest.shape[0]]).astype(BF16)


def kernel(
    ids_hbm, calib_hbm, keep_hbm, ww_hbm, rest_hbm, fw_hbm, fr_hbm,
    pruned_out, rest_out, hess_out, outs_out, fac, err_half,
    ids, cal, kp, ww, fw, fw_s, fr, fr_split, fr_pair, xin, x_t, cur, scaled_drop, err, fw_t, x_half, local_outs, out_relay,
    gram, gram_half, relay_in, relay_out, from_left, from_right, peer_out, peer_in,
    load_sem, pair_sem, f_send, f_recv, pair_recv, scat_send, scat_recv, xz_send, xz_recv, xx_send, xx_recv, xp_sem,
    o_send, o_recv, relay_recv, h_send, h_recv,
):
    tok, row = lax.axis_index("tok"), lax.axis_index("row")
    x, h, c = row // 8, (row // 2) % 4, row % 2
    l, y = tok // 4, tok % 4
    chip = x * 4 + h

    def row_of(px, ph, pc):
        return ((px + 4) % 4) * 8 + ((ph + 4) % 4) * 2 + pc

    def remote(src, dst, ssem, rsem, to_row=None, to_tok=None):
        return pltpu.make_async_remote_copy(
            src_ref=src, dst_ref=dst, send_sem=ssem, recv_sem=rsem,
            device_id=(tok if to_tok is None else to_tok, row if to_row is None else to_row),
            device_id_type=MESH,
        )

    loads = [
        pltpu.make_async_copy(s, d, load_sem.at[i])
        for i, (s, d) in enumerate(
            [(fr_hbm, fr), (calib_hbm, cal), (ww_hbm, ww), (keep_hbm, kp), (fw_hbm, fw), (ids_hbm, ids), (rest_hbm, rest_out), (fw_hbm, fw_s)]
        )
    ]
    for load in loads[:6] + loads[7:]:
        load.start()

    barrier = pltpu.get_barrier_semaphore()

    def greet(d, carry):
        pl.semaphore_signal(barrier, inc=1, device_id=(tok, (row + d) % N_ROW), device_id_type=MESH)
        return carry

    lax.fori_loop(1, N_ROW, greet, 0)
    up_tok, down_tok, other_tok = l * 4 + (y + 1) % 4, l * 4 + (y + 3) % 4, (1 - l) * 4 + y
    for peer in (up_tok, down_tok, other_tok):
        pl.semaphore_signal(barrier, inc=1, device_id=(peer, row), device_id_type=MESH)
    pl.semaphore_wait(barrier, N_ROW - 1 + 3)

    is_source = row == 0

    def scatter(r):
        first = pl.multiple_of((r % 2) * 256 + (r // 2) * 16, 16)
        return remote(
            cal.at[pl.ds(first, 16), pl.ds(0, WIN)], xin.at[r % 2, r // 2], scat_send.at[r], scat_recv.at[0], to_row=r
        )

    loads[0].wait()
    fr_split[0] = fr[:, 0:HALF]
    fr_split[1, :, HALF - 128 :] = jnp.zeros((8, 128), F32)
    fr_split[1, :, 0 : REST - HALF] = fr[:, HALF:REST]
    own_rows = pl.ds(pl.multiple_of(c * 8, 8), 8)
    pair_copy = remote(
        fr_split.at[1 - c], fr_pair.at[own_rows], pair_sem.at[0], pair_sem.at[1], to_row=row_of(x, h, 1 - c)
    )
    pair_copy.start()
    fr_pair[own_rows, :] = fr_split[c]

    loads[1].wait()

    @pl.when(is_source)
    def _():
        def send(r, carry):
            scatter(r).start()
            return carry

        lax.fori_loop(1, N_ROW, send, 0)
        xin[0, 0] = cal[0:16, 0:WIN]

    for i in (2, 3, 4, 7):
        loads[i].wait()
    prune_prepare(ww, kp, fw, cur, scaled_drop, fw_t)

    def f_copy(p, number, slot, to_row, piece=None):
        first, size = p * PHASE_COLS, PHASE_COLS
        if piece is not None:
            first, size = first + piece * PIECE, PIECE
        ref = fac.at[c * CHIPS + slot, :, pl.ds(first, size)]
        rsem = pair_recv.at[p] if number >= PAIR_FIRST else f_recv.at[p, number]
        return remote(ref, ref, f_send.at[0], rsem, to_row=to_row)

    x_up, x_down = row_of(x + 1, h, c), row_of(x - 1, h, c)
    z_up, z_down = row_of(x, h + 1, c), row_of(x, h - 1, c)
    pair = row_of(x, h, 1 - c)
    z_slots = [h, (h + 3) % 4, (h + 1) % 4, (h + 2) % 4]
    x_slots = [x, (x + 3) % 4, (x + 1) % 4, (x + 2) % 4]

    def f_start(*args, **kw):
        f_copy(*args, **kw).start()

    def f_from_z(p, j):
        slot = x * 4 + z_slots[j]
        if j == 1:
            f_start(p, Z_UP_PIECE, slot, z_up, piece=0)
        if j == 2:
            f_start(p, Z_DOWN_PIECE, slot, z_down, piece=1)
        f_start(p, X_FIRST + 4 * j, slot, x_up)
        f_start(p, X_FIRST + 4 * j + 1, slot, x_down)
        f_start(p, PAIR_FIRST + j, slot, pair)

    def f_own(p):
        f_start(p, Z_UP, chip, z_up)
        f_start(p, Z_DOWN, chip, z_down)
        f_from_z(p, 0)

    def f_z_neighbours(p):
        f_copy(p, Z_UP, x * 4 + z_slots[1], z_up).wait_recv()
        f_from_z(p, 1)
        f_copy(p, Z_DOWN, x * 4 + z_slots[2], z_down).wait_recv()
        f_from_z(p, 2)

    def f_z_opposite(p):
        slot = x * 4 + z_slots[3]
        f_copy(p, Z_UP_PIECE, slot, z_up, piece=0).wait_recv()
        f_copy(p, Z_DOWN_PIECE, slot, z_down, piece=1).wait_recv()
        f_from_z(p, 3)

    def f_x_neighbours(p, j):
        n = X_FIRST + 4 * j
        slot = x_slots[1] * 4 + z_slots[j]
        f_copy(p, n, slot, x_up).wait_recv()
        f_start(p, n + 2, slot, x_up, piece=0)
        f_start(p, PAIR_FIRST + 4 + j, slot, pair)
        slot = x_slots[2] * 4 + z_slots[j]
        f_copy(p, n + 1, slot, x_down).wait_recv()
        f_start(p, n + 3, slot, x_down, piece=1)
        f_start(p, PAIR_FIRST + 8 + j, slot, pair)

    def f_x_opposite(p, j):
        n = X_FIRST + 4 * j
        slot = x_slots[3] * 4 + z_slots[j]
        f_copy(p, n + 2, slot, x_up, piece=0).wait_recv()
        f_copy(p, n + 3, slot, x_down, piece=1).wait_recv()
        f_start(p, PAIR_FIRST + 12 + j, slot, pair)

    def f_pair_wait(p):
        ref = fac.at[pl.ds((1 - c) * CHIPS, CHIPS), :, pl.ds(p * PHASE_COLS, PHASE_COLS)]
        remote(ref, ref, f_send.at[0], pair_recv.at[p], to_row=pair).wait_recv()

    pair_copy.wait_recv()
    fac[c * CHIPS + chip] = fr_pair[...].astype(BF16)

    def xz_copy(d):
        ref = xin.at[c, chip]
        return remote(ref, ref, xz_send.at[d], xz_recv.at[d], to_row=row_of(x, h + d, c))

    def xx_copy(d):
        ref = xin.at[c, pl.ds(x * 4, 4)]
        return remote(ref, ref, xx_send.at[d], xx_recv.at[d], to_row=row_of(x + d, h, c))

    xp_copy = remote(xin.at[c], xin.at[c], xp_sem.at[0], xp_sem.at[1], to_row=pair)

    def inputs_along_z():
        @pl.when(jnp.logical_not(is_source))
        def _():
            ref = xin.at[c, chip]
            remote(ref, ref, scat_send.at[0], scat_recv.at[0], to_row=pair).wait_recv()

        for d in (1, 3, 2):
            xz_copy(d).start()

    def inputs_along_x():
        for d in (1, 3, 2):
            ref = xin.at[c, x * 4 + (h + 4 - d) % 4]
            remote(ref, ref, xz_send.at[d], xz_recv.at[d], to_row=row_of(x, h + d, c)).wait_recv()
        for d in (1, 3, 2):
            xx_copy(d).start()

    def inputs_to_pair():
        for d in (1, 3, 2):
            ref = xin.at[c, pl.ds(((x + 4 - d) % 4) * 4, 4)]
            remote(ref, ref, xx_send.at[d], xx_recv.at[d], to_row=row_of(x + d, h, c)).wait_recv()
        xp_copy.start()

    def inputs_complete():
        remote(xin.at[1 - c], xin.at[1 - c], xp_sem.at[0], xp_sem.at[1], to_row=pair).wait_recv()
        loads[5].wait()
        live = jnp.where(ids[...] != 1, 1.0, 0.0)
        live_t = jnp.concatenate([live, jnp.zeros((4, 128), F32)], axis=0).T
        x_parts = []
        for s in range(4):
            part = xin[s // 2, (s % 2) * 8 : (s % 2) * 8 + 8].reshape(128, WIN).astype(F32)
            x_parts.append(part * live_t[:, s : s + 1])
        x_all = jnp.concatenate(x_parts, axis=0)
        x_t[...] = x_all.T.astype(BF16)
        x_half[...] = x_all.astype(BF16)

    def h_copy(number, src, dst, to_tok):
        return remote(src, dst, h_send.at[number], h_recv.at[number], to_tok=to_tok)

    h_copies = [
        h_copy(0, gram_half.at[(y + 2) % 4], relay_in.at[0], up_tok),
        h_copy(1, gram_half.at[4 + (y + 2) % 4], relay_in.at[1], down_tok),
        h_copy(2, gram_half.at[4 + (y + 1) % 4], from_left.at[1], up_tok),
        h_copy(3, gram_half.at[(y + 3) % 4], from_right.at[0], down_tok),
        h_copy(4, relay_out.at[0], from_left.at[0], up_tok),
        h_copy(5, relay_out.at[1], from_right.at[1], down_tok),
        h_copy(6, peer_out, peer_in, other_tok),
    ]

    def hessian_begin():
        @pl.loop(0, FEATURES // 256)
        def _(i):
            cols = pl.ds(pl.multiple_of(i * 256, 256), 256)
            part = jnp.dot(x_t[...], cal[:, cols], preferred_element_type=F32).reshape(N_TOK, 32, 256)
            gram[:, :, cols] = part
            gram_half[:, :, cols] = part.astype(BF16)

        for i in range(4):
            h_copies[i].start()

    def hessian_relay():
        h_copies[0].wait_recv()
        relay_out[0] = (relay_in[0].astype(F32) + gram[(y + 1) % 4]).astype(BF16)
        h_copies[4].start()
        h_copies[1].wait_recv()
        relay_out[1] = (relay_in[1].astype(F32) + gram[4 + (y + 3) % 4]).astype(BF16)
        h_copies[5].start()

    def hessian_peer():
        for i in range(2, 6):
            h_copies[i].wait_recv()
        peer_out[...] = (
            gram[(1 - l) * 4 + y] + from_left[1 - l].astype(F32) + from_right[1 - l].astype(F32)
        ).astype(BF16)
        h_copies[6].start()

    def hessian_end():
        h_copies[6].wait_recv()
        total = gram[l * 4 + y] + from_left[l].astype(F32) + from_right[l].astype(F32) + peer_in[...].astype(F32)
        hess_out[...] = total * (2.0 / TOKENS)

    def out_cols(sender):
        return pl.ds(pl.multiple_of(sender * LOCAL_ROWS, 128), LOCAL_ROWS)

    my_cols = out_cols(row)
    opposite = (h + 2) % 4
    relays = [
        remote(local_outs.at[:, opposite, 0], out_relay.at[0], o_send.at[0], relay_recv.at[0], to_row=z_up),
        remote(local_outs.at[:, opposite, 1], out_relay.at[1], o_send.at[0], relay_recv.at[1], to_row=z_down),
    ]

    def send_outputs():
        local_outs[...] = jnp.dot(
            x_half[...], cur[...].astype(BF16), preferred_element_type=F32
        ).astype(BF16).reshape(4, 4, 2, 16, LOCAL_ROWS)
        for relay in relays:
            relay.start()
        for dx in (2, 1, 3, 0):
            for dh in (1, 3, 0):
                for dc in (0, 1):
                    if (dx, dh, dc) != (0, 0, 0):
                        ox, oh, oc = (x + dx) % 4, (h + dh) % 4, (c + dc) % 2
                        remote(
                            local_outs.at[ox, oh, oc], outs_out.at[:, my_cols], o_send.at[0], o_recv.at[0],
                            to_row=row_of(ox, oh, oc),
                        ).start()

    def pass_on(way):
        relays[way].wait_recv()
        sender = row_of(x, h + (3 if way == 0 else 1), c)
        for px in range(4):
            remote(
                out_relay.at[way, px], outs_out.at[:, out_cols(sender)], o_send.at[1], o_recv.at[0],
                to_row=row_of(px, h + (1 if way == 0 else 3), way),
            ).start()

    arrived = outs_out.at[:, pl.ds(0, (N_ROW - 1) * LOCAL_ROWS)]

    def outputs_complete():
        remote(arrived, arrived, o_send.at[0], o_recv.at[0], to_row=pair).wait_recv()

    def prune(first, last):
        for k in range(first, last):
            prune_tile(k, cur, scaled_drop, fw_t, fw_s, err)

    def pruned_results():
        outs_out[:, my_cols] = local_outs[x, h, c]
        pruned_out[...] = cur[...].T
        err_half[...] = err[...].astype(BF16)

    def update(p):
        for half in range(2):

            @pl.loop(0, PHASE_COLS // STEP)
            def _(i, half=half, p=p):
                first = pl.multiple_of(p * PHASE_COLS + i * STEP, STEP)
                rows = pl.ds(pl.multiple_of(half * HALF + first, STEP), STEP)
                factor = fac[half * CHIPS : (half + 1) * CHIPS, :, pl.ds(first, STEP)]
                rest_out[rows, :] = compensate(rest_out[rows, :], factor, err_half[...])

    f_own(0)
    loads[6].start()
    prune(0, 12)
    inputs_along_z()
    f_own(1)
    prune(12, 16)
    f_z_neighbours(0)
    prune(16, 20)
    inputs_along_x()
    prune(20, 28)
    f_z_neighbours(1)
    f_z_opposite(0)
    inputs_to_pair()
    prune(28, 32)
    f_x_neighbours(0, 1)
    f_x_neighbours(1, 0)
    f_z_opposite(1)
    inputs_complete()
    hessian_begin()
    send_outputs()
    f_x_neighbours(0, 2)
    f_x_neighbours(0, 0)
    f_x_neighbours(0, 3)
    hessian_relay()
    pruned_results()
    f_x_neighbours(1, 2)
    f_x_neighbours(1, 3)
    f_x_neighbours(1, 1)
    f_x_opposite(1, 0)
    pass_on(0)
    pass_on(1)
    for j in (1, 2, 3, 0):
        f_x_opposite(0, j)
    hessian_peer()
    f_x_opposite(1, 1)
    f_x_opposite(1, 3)
    f_pair_wait(0)
    f_x_opposite(1, 2)
    loads[6].wait()
    update(0)
    outputs_complete()
    f_pair_wait(1)
    hessian_end()

    remote(arrived, arrived, o_send.at[0], o_recv.at[0], to_row=pair).wait_send()
    remote(out_relay, out_relay, o_send.at[1], o_recv.at[0], to_row=pair).wait_send()

    @pl.when(is_source)
    def _():
        def left(r, carry):
            scatter(r).wait_send()
            return carry

        lax.fori_loop(1, N_ROW, left, 0)

    pair_copy.wait_send()
    for d in (1, 3, 2):
        xz_copy(d).wait_send()
        xx_copy(d).wait_send()
    xp_copy.wait_send()
    for copy in h_copies:
        copy.wait_send()
    sent = fac.at[pl.ds(0, 31)]
    remote(sent, sent, f_send.at[0], pair_recv.at[0], to_row=pair).wait_send()


def finish_kernel(
    pruned, rest, hess, outs, fac, err_half,
    pruned_hbm, rest_hbm, hess_hbm, outs_hbm,
    updated, sem,
):
    copies = [
        pltpu.make_async_copy(pruned, pruned_hbm, sem.at[0]),
        pltpu.make_async_copy(hess, hess_hbm, sem.at[1]),
        pltpu.make_async_copy(outs, outs_hbm, sem.at[2]),
    ]
    last = HALF - PHASE_COLS
    for half in range(2):
        rows = pl.ds(half * HALF, last)
        copies.append(pltpu.make_async_copy(rest.at[rows], rest_hbm.at[rows], sem.at[3 + half]))
    for copy in copies:
        copy.start()
    for half in range(2):
        for i in range(PHASE_COLS // STEP):
            first = last + i * STEP
            start = half * HALF + first
            count = min(STEP, REST - start)
            part = rest[start : start + count, :]
            at = half * PHASE_COLS + i * STEP
            updated[at : at + count, :] = compensate(
                part, fac[half * CHIPS : (half + 1) * CHIPS, :, first : first + STEP], err_half[...]
            )
            copy = pltpu.make_async_copy(
                updated.at[pl.ds(at, count)], rest_hbm.at[pl.ds(start, count)], sem.at[5 + half * (PHASE_COLS // STEP) + i]
            )
            copy.start()
            copies.append(copy)
    for copy in copies:
        copy.wait()


def on_device(token_ids, calib_input, keep_mask, weight_window, weight_rest, factor_window, factor_rest):
    vmem, dma = pltpu.VMEM, pltpu.SemaphoreType.DMA
    slab = (32, FEATURES)
    in_hbm = [
        pltpu.with_memory_space_constraint(a, pltpu.HBM)
        for a in (
            token_ids.reshape(4, 128), calib_input, keep_mask, weight_window, weight_rest.T, factor_window, factor_rest
        )
    ]
    shapes = [
        ((LOCAL_ROWS, WIN), F32),
        ((REST, LOCAL_ROWS), BF16),
        (slab, F32),
        ((16, N_ROW * LOCAL_ROWS), BF16),
    ]
    held = pl.pallas_call(
        kernel,
        out_shape=tuple(
            vmem(*s) for s in shapes + [((2 * CHIPS, 16, HALF), BF16), ((WIN, LOCAL_ROWS), BF16)]
        ),
        in_specs=[pl.BlockSpec(memory_space=pltpu.HBM)] * 7,
        out_specs=[pl.BlockSpec(memory_space=vmem)] * 6,
        scratch_shapes=[
            vmem((4, 128), jnp.int32),
            vmem((LOCAL_TOKENS, FEATURES), BF16),
            vmem((LOCAL_ROWS, WIN), jnp.int32),
            vmem((LOCAL_ROWS, WIN), F32),
            vmem((WIN, WIN), F32),
            pltpu.SMEM((WIN, WIN), F32),
            vmem((8, REST), F32),
            vmem((2, 8, HALF), F32),
            vmem((16, HALF), F32),
            vmem((2, CHIPS, 16, WIN), BF16),
            vmem((WIN, LOCAL_TOKENS), BF16),
            vmem((WIN, LOCAL_ROWS), F32),
            vmem((WIN, LOCAL_ROWS), F32),
            vmem((WIN, LOCAL_ROWS), F32),
            vmem((WIN, WIN), F32),
            vmem((LOCAL_TOKENS, WIN), BF16),
            vmem((4, 4, 2, 16, LOCAL_ROWS), BF16),
            vmem((2, 4, 16, LOCAL_ROWS), BF16),
            vmem((N_TOK,) + slab, F32),
            vmem((N_TOK,) + slab, BF16),
            vmem((2,) + slab, BF16),
            vmem((2,) + slab, BF16),
            vmem((2,) + slab, BF16),
            vmem((2,) + slab, BF16),
            vmem(slab, BF16),
            vmem(slab, BF16),
            dma((8,)),
            dma((2,)),
            dma((1,)),
            dma((PHASES, F_MESSAGES)),
            dma((PHASES,)),
            dma((N_ROW,)),
            dma((1,)),
            dma((4,)),
            dma((4,)),
            dma((4,)),
            dma((4,)),
            dma((2,)),
            dma((2,)),
            dma((1,)),
            dma((2,)),
            dma((7,)),
            dma((7,)),
        ],
        compiler_params=pltpu.CompilerParams(
            collective_id=0, has_side_effects=True, vmem_limit_bytes=32 * 1024 * 1024
        ),
        cost_estimate=pl.CostEstimate(flops=2_000_000_000, bytes_accessed=16_000_000, transcendentals=0),
    )(*in_hbm)
    pruned, rest_t, hess, outs = pl.pallas_call(
        finish_kernel,
        out_shape=tuple(jax.ShapeDtypeStruct(*s) for s in shapes),
        in_specs=[pl.BlockSpec(memory_space=vmem)] * 6,
        out_specs=[pl.BlockSpec(memory_space=pltpu.HBM)] * 4,
        scratch_shapes=[
            vmem((2 * PHASE_COLS, LOCAL_ROWS), BF16),
            dma((5 + 2 * (PHASE_COLS // STEP),)),
        ],
        compiler_params=pltpu.CompilerParams(vmem_limit_bytes=32 * 1024 * 1024),
        cost_estimate=pl.CostEstimate(flops=600_000_000, bytes_accessed=12_000_000, transcendentals=0),
    )(*[pltpu.with_memory_space_constraint(a, vmem) for a in held])
    return pruned, rest_t.T, hess, outs


def solution(mesh):
    return jax.shard_map(
        on_device,
        mesh=mesh,
        in_specs=(
            P("tok"),
            P("tok", "row"),
            P("row", None),
            P("row", None),
            P("row", "tok"),
            P(),
            P("row", "tok"),
        ),
        out_specs=(P("row", None), P("row", "tok"), P("tok", "row"), P(("tok", "row"), None)),
        check_vma=False,
    )
```

```python
import jax
import jax.numpy as jnp
from jax import lax
from jax.experimental import pallas as pl
from jax.experimental.pallas import tpu as pltpu
from jax.sharding import PartitionSpec as P

MESH = pl.DeviceIdType.MESH
F32, BF16 = jnp.float32, jnp.bfloat16

WIN = 256
BLOCK = 128
SUB = 8
LOCAL_ROWS = 384
LOCAL_TOKENS = 512
FEATURES = 1536
REST = 6112
HALF = 3072
N_ROW = 32
N_TOK = 8
CHIPS = 16
TOKENS = LOCAL_TOKENS * N_TOK

PHASES = 2
PHASE_COLS = HALF // PHASES
PIECE = PHASE_COLS // 2
STEP = 512

Z_UP, Z_DOWN, Z_UP_PIECE, Z_DOWN_PIECE = 0, 1, 2, 3
X_FIRST = 4
PAIR_FIRST = 20
F_MESSAGES = 20


def prune_prepare(ww, kp, fw, cur, scaled_drop, fw_t):
    factor = fw[...]
    fw_t[...] = factor.T
    row_id = lax.broadcasted_iota(jnp.int32, (WIN, WIN), 0)
    col_id = lax.broadcasted_iota(jnp.int32, (WIN, WIN), 1)
    diagonal = jnp.sum(jnp.where(row_id == col_id, factor, 0.0), axis=1, keepdims=True)
    drop = (1 - kp[...]).astype(F32).T
    scaled_drop[...] = drop * (1.0 / diagonal)
    cur[...] = ww[...].T


def prune_tile(k, cur, scaled_drop, fw_t, fw_s, err, err_blocks):
    low = k * SUB
    block_end = (low // BLOCK + 1) * BLOCK
    shape = (SUB, LOCAL_ROWS)
    tile = cur[low : low + SUB, :]
    drop = scaled_drop[low : low + SUB, :]
    place = lax.broadcasted_iota(jnp.int32, shape, 0)
    values = [jnp.broadcast_to(tile[s : s + 1, :], shape) for s in range(SUB)]
    errors = []
    tile_err = jnp.zeros(shape, F32)
    tile_out = jnp.zeros(shape, F32)
    for s in range(SUB):
        e = values[s] * jnp.broadcast_to(drop[s : s + 1, :], shape)
        for t in range(s + 1, SUB):
            values[t] = values[t] - fw_s[low + s, low + t] * e
        errors.append(e)
        tile_err = jnp.where(place == s, e, tile_err)
        tile_out = jnp.where(place == s, values[s] - fw_s[low + s, low + s] * e, tile_out)
    cur[low : low + SUB, :] = tile_out
    err[low : low + SUB, :] = tile_err
    at = ((k % 2) * CHIPS + k // 2) * SUB
    err_blocks[at : at + SUB, :] = tile_err
    start = low + SUB
    while start < block_end:
        end = min(start + 32, block_end)
        n = (end - start) // SUB
        part = cur[start:end, :].reshape(n, SUB, LOCAL_ROWS)
        for s in range(SUB):
            part = part - fw_t[start:end, low + s : low + s + 1].reshape(n, SUB, 1) * errors[s][None]
        cur[start:end, :] = part.reshape(n * SUB, LOCAL_ROWS)
        start = end
    if block_end == low + SUB and block_end < WIN:
        b = block_end - BLOCK
        cur[block_end:, :] = cur[block_end:, :] - jnp.dot(
            fw_t[block_end:, b:block_end], err[b:block_end, :],
            precision=lax.Precision.HIGHEST, preferred_element_type=F32,
        )


def compensate(rest, blocks, half, err_half):
    factor = blocks[:, half * 8 : half * 8 + 8, :].reshape(WIN, blocks.shape[2])
    change = lax.dot_general(
        factor, err_half, (((0,), (0,)), ((), ())), preferred_element_type=F32
    )
    return (rest.astype(F32) - change[: rest.shape[0]]).astype(BF16)


def kernel(
    ids_hbm, calib_hbm, keep_hbm, ww_hbm, rest_hbm, fw_hbm, fr_hbm,
    pruned_out, rest_out, hess_out, outs_out, fac, err_half,
    ids, cal, kp, ww, fw, fw_s, fr, fr_block, xin, x_t, cur, scaled_drop, err, err_blocks, fw_t, x_half, local_outs, z_relay, x_relay,
    gram, gram_half, relay_in, relay_out, from_left, from_right, peer_out, peer_in,
    load_sem, f_send, f_recv, pair_recv, scat_send, scat_recv, xz_send, xz_recv, xx_send, xx_recv, xp_sem,
    o_send, o_recv, relay_recv, h_send, h_recv,
):
    tok, row = lax.axis_index("tok"), lax.axis_index("row")
    x, h, c = row // 8, (row // 2) % 4, row % 2
    l, y = tok // 4, tok % 4
    chip = x * 4 + h

    def row_of(px, ph, pc):
        return ((px + 4) % 4) * 8 + ((ph + 4) % 4) * 2 + pc

    def remote(src, dst, ssem, rsem, to_row=None, to_tok=None):
        return pltpu.make_async_remote_copy(
            src_ref=src, dst_ref=dst, send_sem=ssem, recv_sem=rsem,
            device_id=(tok if to_tok is None else to_tok, row if to_row is None else to_row),
            device_id_type=MESH,
        )

    loads = [
        pltpu.make_async_copy(s, d, load_sem.at[i])
        for i, (s, d) in enumerate(
            [(fr_hbm, fr), (calib_hbm, cal), (ww_hbm, ww), (keep_hbm, kp), (fw_hbm, fw), (ids_hbm, ids), (rest_hbm, rest_out), (fw_hbm, fw_s)]
        )
    ]
    for load in loads[:6] + loads[7:]:
        load.start()

    barrier = pltpu.get_barrier_semaphore()

    def greet(d, carry):
        pl.semaphore_signal(barrier, inc=1, device_id=(tok, (row + d) % N_ROW), device_id_type=MESH)
        return carry

    lax.fori_loop(1, N_ROW, greet, 0)
    up_tok, down_tok, other_tok = l * 4 + (y + 1) % 4, l * 4 + (y + 3) % 4, (1 - l) * 4 + y
    for peer in (up_tok, down_tok, other_tok):
        pl.semaphore_signal(barrier, inc=1, device_id=(peer, row), device_id_type=MESH)
    pl.semaphore_wait(barrier, N_ROW - 1 + 3)

    is_source = row == 0

    def scatter(r):
        first = pl.multiple_of((r % 2) * 256 + (r // 2) * 16, 16)
        return remote(
            cal.at[pl.ds(first, 16), pl.ds(0, WIN)], xin.at[r % 2, r // 2], scat_send.at[r], scat_recv.at[0], to_row=r
        )

    loads[0].wait()
    fr_block[0:8, :] = fr[:, 0:HALF]
    fr_block[8:16, HALF - 128 :] = jnp.zeros((8, 128), F32)
    fr_block[8:16, 0 : REST - HALF] = fr[:, HALF:REST]
    fac[c * CHIPS + chip] = fr_block[...].astype(BF16)

    def f_copy(p, number, slot, to_row, piece=None):
        first, size = p * PHASE_COLS, PHASE_COLS
        if piece is not None:
            first, size = first + piece * PIECE, PIECE
        ref = fac.at[c * CHIPS + slot, :, pl.ds(first, size)]
        rsem = pair_recv.at[p] if number >= PAIR_FIRST else f_recv.at[p, number]
        return remote(ref, ref, f_send.at[0], rsem, to_row=to_row)

    x_up, x_down = row_of(x + 1, h, c), row_of(x - 1, h, c)
    z_up, z_down = row_of(x, h + 1, c), row_of(x, h - 1, c)
    pair = row_of(x, h, 1 - c)
    z_slots = [h, (h + 3) % 4, (h + 1) % 4, (h + 2) % 4]
    x_slots = [x, (x + 3) % 4, (x + 1) % 4, (x + 2) % 4]

    def f_start(*args, **kw):
        f_copy(*args, **kw).start()

    def f_from_z(p, j):
        slot = x * 4 + z_slots[j]
        if j == 1:
            f_start(p, Z_UP_PIECE, slot, z_up, piece=0)
        if j == 2:
            f_start(p, Z_DOWN_PIECE, slot, z_down, piece=1)
        f_start(p, X_FIRST + 4 * j, slot, x_up)
        f_start(p, X_FIRST + 4 * j + 1, slot, x_down)
        f_start(p, PAIR_FIRST + j, slot, pair)

    def f_own(p):
        f_start(p, Z_UP, chip, z_up)
        f_start(p, Z_DOWN, chip, z_down)
        f_from_z(p, 0)

    def f_z_neighbours(p):
        f_copy(p, Z_UP, x * 4 + z_slots[1], z_up).wait_recv()
        f_from_z(p, 1)
        f_copy(p, Z_DOWN, x * 4 + z_slots[2], z_down).wait_recv()
        f_from_z(p, 2)

    def f_z_opposite(p):
        slot = x * 4 + z_slots[3]
        f_copy(p, Z_UP_PIECE, slot, z_up, piece=0).wait_recv()
        f_copy(p, Z_DOWN_PIECE, slot, z_down, piece=1).wait_recv()
        f_from_z(p, 3)

    def f_x_neighbours(p, j):
        n = X_FIRST + 4 * j
        slot = x_slots[1] * 4 + z_slots[j]
        f_copy(p, n, slot, x_up).wait_recv()
        f_start(p, n + 2, slot, x_up, piece=0)
        f_start(p, PAIR_FIRST + 4 + j, slot, pair)
        slot = x_slots[2] * 4 + z_slots[j]
        f_copy(p, n + 1, slot, x_down).wait_recv()
        f_start(p, n + 3, slot, x_down, piece=1)
        f_start(p, PAIR_FIRST + 8 + j, slot, pair)

    def f_x_opposite(p, j):
        n = X_FIRST + 4 * j
        slot = x_slots[3] * 4 + z_slots[j]
        f_copy(p, n + 2, slot, x_up, piece=0).wait_recv()
        f_copy(p, n + 3, slot, x_down, piece=1).wait_recv()
        f_start(p, PAIR_FIRST + 12 + j, slot, pair)

    def f_pair_wait(p):
        ref = fac.at[pl.ds((1 - c) * CHIPS, CHIPS), :, pl.ds(p * PHASE_COLS, PHASE_COLS)]
        remote(ref, ref, f_send.at[0], pair_recv.at[p], to_row=pair).wait_recv()

    loads[1].wait()

    @pl.when(is_source)
    def _():
        def send(r, carry):
            scatter(r).start()
            return carry

        lax.fori_loop(1, N_ROW, send, 0)
        xin[0, 0] = cal[0:16, 0:WIN]

    def xz_copy(d):
        ref = xin.at[c, chip]
        return remote(ref, ref, xz_send.at[d], xz_recv.at[d], to_row=row_of(x, h + d, c))

    def xx_copy(d):
        ref = xin.at[c, pl.ds(x * 4, 4)]
        return remote(ref, ref, xx_send.at[d], xx_recv.at[d], to_row=row_of(x + d, h, c))

    xp_copy = remote(xin.at[c], xin.at[c], xp_sem.at[0], xp_sem.at[1], to_row=pair)

    def inputs_along_z():
        @pl.when(jnp.logical_not(is_source))
        def _():
            ref = xin.at[c, chip]
            remote(ref, ref, scat_send.at[0], scat_recv.at[0], to_row=pair).wait_recv()

        for d in (1, 3, 2):
            xz_copy(d).start()

    def inputs_along_x():
        for d in (1, 3, 2):
            ref = xin.at[c, x * 4 + (h + 4 - d) % 4]
            remote(ref, ref, xz_send.at[d], xz_recv.at[d], to_row=row_of(x, h + d, c)).wait_recv()
        for d in (1, 3, 2):
            xx_copy(d).start()

    def inputs_to_pair():
        for d in (1, 3, 2):
            ref = xin.at[c, pl.ds(((x + 4 - d) % 4) * 4, 4)]
            remote(ref, ref, xx_send.at[d], xx_recv.at[d], to_row=row_of(x + d, h, c)).wait_recv()
        xp_copy.start()

    def inputs_complete():
        remote(xin.at[1 - c], xin.at[1 - c], xp_sem.at[0], xp_sem.at[1], to_row=pair).wait_recv()
        loads[5].wait()
        live = jnp.where(ids[...] != 1, 1.0, 0.0)
        live_t = jnp.concatenate([live, jnp.zeros((4, 128), F32)], axis=0).T
        x_parts = []
        for s in range(4):
            part = xin[s // 2, (s % 2) * 8 : (s % 2) * 8 + 8].reshape(128, WIN).astype(F32)
            x_parts.append(part * live_t[:, s : s + 1])
        x_all = jnp.concatenate(x_parts, axis=0)
        x_t[...] = x_all.T.astype(BF16)
        x_half[...] = x_all.astype(BF16)

    def h_copy(number, src, dst, to_tok):
        return remote(src, dst, h_send.at[number], h_recv.at[number], to_tok=to_tok)

    h_copies = [
        h_copy(0, gram_half.at[(y + 2) % 4], relay_in.at[0], up_tok),
        h_copy(1, gram_half.at[4 + (y + 2) % 4], relay_in.at[1], down_tok),
        h_copy(2, gram_half.at[4 + (y + 1) % 4], from_left.at[1], up_tok),
        h_copy(3, gram_half.at[(y + 3) % 4], from_right.at[0], down_tok),
        h_copy(4, relay_out.at[0], from_left.at[0], up_tok),
        h_copy(5, relay_out.at[1], from_right.at[1], down_tok),
        h_copy(6, peer_out, peer_in, other_tok),
    ]

    def hessian_begin():
        @pl.loop(0, FEATURES // 256)
        def _(i):
            cols = pl.ds(pl.multiple_of(i * 256, 256), 256)
            part = jnp.dot(x_t[...], cal[:, cols], preferred_element_type=F32).reshape(N_TOK, 32, 256)
            gram[:, :, cols] = part
            gram_half[:, :, cols] = part.astype(BF16)

        for i in range(4):
            h_copies[i].start()

    def hessian_relay():
        h_copies[0].wait_recv()
        relay_out[0] = (relay_in[0].astype(F32) + gram[(y + 1) % 4]).astype(BF16)
        h_copies[4].start()
        h_copies[1].wait_recv()
        relay_out[1] = (relay_in[1].astype(F32) + gram[4 + (y + 3) % 4]).astype(BF16)
        h_copies[5].start()

    def hessian_peer():
        for i in range(2, 6):
            h_copies[i].wait_recv()
        peer_out[...] = (
            gram[(1 - l) * 4 + y] + from_left[1 - l].astype(F32) + from_right[1 - l].astype(F32)
        ).astype(BF16)
        h_copies[6].start()

    def hessian_end():
        h_copies[6].wait_recv()
        total = gram[l * 4 + y] + from_left[l].astype(F32) + from_right[l].astype(F32) + peer_in[...].astype(F32)
        hess_out[...] = total * (2.0 / TOKENS)

    def out_cols(sender):
        return pl.ds(pl.multiple_of(sender * LOCAL_ROWS, 128), LOCAL_ROWS)

    my_cols = out_cols(row)
    relays = [
        remote(local_outs.at[:, 3, 0], z_relay.at[0], o_send.at[0], relay_recv.at[0], to_row=z_up),
        remote(local_outs.at[:, 3, 1], z_relay.at[1], o_send.at[0], relay_recv.at[1], to_row=z_down),
        remote(local_outs.at[2, pl.ds(0, 3), 0], x_relay.at[0], o_send.at[0], relay_recv.at[2], to_row=x_up),
        remote(local_outs.at[2, pl.ds(0, 3), 1], x_relay.at[1], o_send.at[0], relay_recv.at[3], to_row=x_down),
    ]

    def send_outputs():
        found = jnp.dot(
            x_half[...], cur[...].astype(BF16), preferred_element_type=F32
        ).astype(BF16).reshape(N_ROW, 16, LOCAL_ROWS)
        for r in range(N_ROW):
            local_outs[(r // 8 - x + 4) % 4, ((r // 2) % 4 - h + 5) % 4, r % 2] = found[r]
        for relay in relays:
            relay.start()
        for dx in (1, 3, 0):
            for dh in (1, -1, 0):
                for dc in (0, 1):
                    if (dx, dh, dc) != (0, 0, 0):
                        oc = (c + dc) % 2
                        remote(
                            local_outs.at[dx, dh + 1, oc], outs_out.at[:, my_cols], o_send.at[0], o_recv.at[0],
                            to_row=row_of(x + dx, h + dh, oc),
                        ).start()

    def pass_on_z(way):
        relays[way].wait_recv()
        step = 1 if way == 0 else -1
        sender = row_of(x, h - step, c)
        for dx in range(4):
            remote(
                z_relay.at[way, dx], outs_out.at[:, out_cols(sender)], o_send.at[1], o_recv.at[0],
                to_row=row_of(x + dx, h + step, way),
            ).start()

    def pass_on_x(way):
        relays[2 + way].wait_recv()
        step = 1 if way == 0 else -1
        sender = row_of(x - step, h, c)
        for dh in (-1, 0, 1):
            remote(
                x_relay.at[way, dh + 1], outs_out.at[:, out_cols(sender)], o_send.at[2], o_recv.at[0],
                to_row=row_of(x + step, h + dh, way),
            ).start()

    arrived = outs_out.at[:, pl.ds(0, (N_ROW - 1) * LOCAL_ROWS)]

    def outputs_complete():
        remote(arrived, arrived, o_send.at[0], o_recv.at[0], to_row=pair).wait_recv()

    def prune(first, last):
        for k in range(first, last):
            prune_tile(k, cur, scaled_drop, fw_t, fw_s, err, err_blocks)

    def pruned_results():
        outs_out[:, my_cols] = local_outs[0, 1, c]
        pruned_out[...] = cur[...].T
        err_half[...] = err_blocks[...].astype(BF16)

    def update(p):
        for half in range(2):

            @pl.loop(0, PHASE_COLS // STEP)
            def _(i, half=half, p=p):
                first = pl.multiple_of(p * PHASE_COLS + i * STEP, STEP)
                rows = pl.ds(pl.multiple_of(half * HALF + first, STEP), STEP)
                rest_out[rows, :] = compensate(rest_out[rows, :], fac[:, :, pl.ds(first, STEP)], half, err_half[...])

    f_own(0)
    loads[6].start()
    for i in (2, 3, 4, 7):
        loads[i].wait()
    prune_prepare(ww, kp, fw, cur, scaled_drop, fw_t)
    prune(0, 4)
    inputs_along_z()
    prune(4, 8)
    f_own(1)
    prune(8, 12)
    f_z_neighbours(0)
    prune(12, 16)
    inputs_along_x()
    prune(16, 24)
    f_z_neighbours(1)
    prune(24, 28)
    inputs_to_pair()
    prune(28, 32)
    f_x_neighbours(0, 0)
    f_z_opposite(0)
    f_x_neighbours(0, 2)
    inputs_complete()
    hessian_begin()
    send_outputs()
    f_x_neighbours(1, 1)
    f_x_neighbours(0, 3)
    pruned_results()
    f_x_neighbours(0, 1)
    f_z_opposite(1)
    hessian_relay()
    f_x_neighbours(1, 0)
    pass_on_x(0)
    pass_on_x(1)
    f_x_opposite(1, 1)
    f_x_opposite(0, 2)
    f_x_neighbours(1, 2)
    f_x_neighbours(1, 3)
    pass_on_z(0)
    pass_on_z(1)
    f_x_opposite(0, 0)
    f_x_opposite(0, 1)
    f_x_opposite(1, 0)
    f_x_opposite(0, 3)
    hessian_peer()
    f_pair_wait(0)
    f_x_opposite(1, 3)
    f_x_opposite(1, 2)
    loads[6].wait()
    update(0)
    outputs_complete()
    f_pair_wait(1)
    hessian_end()

    remote(arrived, arrived, o_send.at[0], o_recv.at[0], to_row=pair).wait_send()
    remote(z_relay, z_relay, o_send.at[1], o_recv.at[0], to_row=pair).wait_send()
    remote(x_relay, x_relay, o_send.at[2], o_recv.at[0], to_row=pair).wait_send()

    @pl.when(is_source)
    def _():
        def left(r, carry):
            scatter(r).wait_send()
            return carry

        lax.fori_loop(1, N_ROW, left, 0)

    for d in (1, 3, 2):
        xz_copy(d).wait_send()
        xx_copy(d).wait_send()
    xp_copy.wait_send()
    for copy in h_copies:
        copy.wait_send()
    sent = fac.at[pl.ds(0, 31)]
    remote(sent, sent, f_send.at[0], pair_recv.at[0], to_row=pair).wait_send()


def finish_kernel(
    pruned, rest, hess, outs, fac, err_half,
    pruned_hbm, rest_hbm, hess_hbm, outs_hbm,
    updated, sem,
):
    copies = [
        pltpu.make_async_copy(pruned, pruned_hbm, sem.at[0]),
        pltpu.make_async_copy(hess, hess_hbm, sem.at[1]),
        pltpu.make_async_copy(outs, outs_hbm, sem.at[2]),
    ]
    last = HALF - PHASE_COLS
    for half in range(2):
        rows = pl.ds(half * HALF, last)
        copies.append(pltpu.make_async_copy(rest.at[rows], rest_hbm.at[rows], sem.at[3 + half]))
    for copy in copies:
        copy.start()
    for half in range(2):
        for i in range(PHASE_COLS // STEP):
            first = last + i * STEP
            start = half * HALF + first
            count = min(STEP, REST - start)
            part = rest[start : start + count, :]
            at = half * PHASE_COLS + i * STEP
            updated[at : at + count, :] = compensate(part, fac[:, :, first : first + STEP], half, err_half[...])
            copy = pltpu.make_async_copy(
                updated.at[pl.ds(at, count)], rest_hbm.at[pl.ds(start, count)], sem.at[5 + half * (PHASE_COLS // STEP) + i]
            )
            copy.start()
            copies.append(copy)
    for copy in copies:
        copy.wait()


def on_device(token_ids, calib_input, keep_mask, weight_window, weight_rest, factor_window, factor_rest):
    vmem, dma = pltpu.VMEM, pltpu.SemaphoreType.DMA
    slab = (32, FEATURES)
    in_hbm = [
        pltpu.with_memory_space_constraint(a, pltpu.HBM)
        for a in (
            token_ids.reshape(4, 128), calib_input, keep_mask, weight_window, weight_rest.T, factor_window, factor_rest
        )
    ]
    shapes = [
        ((LOCAL_ROWS, WIN), F32),
        ((REST, LOCAL_ROWS), BF16),
        (slab, F32),
        ((16, N_ROW * LOCAL_ROWS), BF16),
    ]
    held = pl.pallas_call(
        kernel,
        out_shape=tuple(
            vmem(*s) for s in shapes + [((2 * CHIPS, 16, HALF), BF16), ((WIN, LOCAL_ROWS), BF16)]
        ),
        in_specs=[pl.BlockSpec(memory_space=pltpu.HBM)] * 7,
        out_specs=[pl.BlockSpec(memory_space=vmem)] * 6,
        scratch_shapes=[
            vmem((4, 128), jnp.int32),
            vmem((LOCAL_TOKENS, FEATURES), BF16),
            vmem((LOCAL_ROWS, WIN), jnp.int32),
            vmem((LOCAL_ROWS, WIN), F32),
            vmem((WIN, WIN), F32),
            pltpu.SMEM((WIN, WIN), F32),
            vmem((8, REST), F32),
            vmem((16, HALF), F32),
            vmem((2, CHIPS, 16, WIN), BF16),
            vmem((WIN, LOCAL_TOKENS), BF16),
            vmem((WIN, LOCAL_ROWS), F32),
            vmem((WIN, LOCAL_ROWS), F32),
            vmem((WIN, LOCAL_ROWS), F32),
            vmem((WIN, LOCAL_ROWS), F32),
            vmem((WIN, WIN), F32),
            vmem((LOCAL_TOKENS, WIN), BF16),
            vmem((4, 4, 2, 16, LOCAL_ROWS), BF16),
            vmem((2, 4, 16, LOCAL_ROWS), BF16),
            vmem((2, 3, 16, LOCAL_ROWS), BF16),
            vmem((N_TOK,) + slab, F32),
            vmem((N_TOK,) + slab, BF16),
            vmem((2,) + slab, BF16),
            vmem((2,) + slab, BF16),
            vmem((2,) + slab, BF16),
            vmem((2,) + slab, BF16),
            vmem(slab, BF16),
            vmem(slab, BF16),
            dma((8,)),
            dma((1,)),
            dma((PHASES, F_MESSAGES)),
            dma((PHASES,)),
            dma((N_ROW,)),
            dma((1,)),
            dma((4,)),
            dma((4,)),
            dma((4,)),
            dma((4,)),
            dma((2,)),
            dma((3,)),
            dma((1,)),
            dma((4,)),
            dma((7,)),
            dma((7,)),
        ],
        compiler_params=pltpu.CompilerParams(
            collective_id=0, has_side_effects=True, vmem_limit_bytes=32 * 1024 * 1024
        ),
        cost_estimate=pl.CostEstimate(flops=2_000_000_000, bytes_accessed=16_000_000, transcendentals=0),
    )(*in_hbm)
    pruned, rest_t, hess, outs = pl.pallas_call(
        finish_kernel,
        out_shape=tuple(jax.ShapeDtypeStruct(*s) for s in shapes),
        in_specs=[pl.BlockSpec(memory_space=vmem)] * 6,
        out_specs=[pl.BlockSpec(memory_space=pltpu.HBM)] * 4,
        scratch_shapes=[
            vmem((2 * PHASE_COLS, LOCAL_ROWS), BF16),
            dma((5 + 2 * (PHASE_COLS // STEP),)),
        ],
        compiler_params=pltpu.CompilerParams(vmem_limit_bytes=32 * 1024 * 1024),
        cost_estimate=pl.CostEstimate(flops=600_000_000, bytes_accessed=12_000_000, transcendentals=0),
    )(*[pltpu.with_memory_space_constraint(a, vmem) for a in held])
    return pruned, rest_t.T, hess, outs


def solution(mesh):
    return jax.shard_map(
        on_device,
        mesh=mesh,
        in_specs=(
            P("tok"),
            P("tok", "row"),
            P("row", None),
            P("row", None),
            P("row", "tok"),
            P(),
            P("row", "tok"),
        ),
        out_specs=(P("row", None), P("row", "tok"), P("tok", "row"), P(("tok", "row"), None)),
        check_vma=False,
    )
```

```python
import jax
import jax.numpy as jnp
from jax import lax
from jax.experimental import pallas as pl
from jax.experimental.pallas import tpu as pltpu
from jax.sharding import PartitionSpec as P

MESH = pl.DeviceIdType.MESH
F32, BF16 = jnp.float32, jnp.bfloat16

WIN = 256
BLOCK = 128
SUB = 8
LOCAL_ROWS = 384
LOCAL_TOKENS = 512
FEATURES = 1536
REST = 6112
HALF = 3072
N_ROW = 32
N_TOK = 8
CHIPS = 16
TOKENS = LOCAL_TOKENS * N_TOK

PHASES = 1
PHASE_COLS = HALF // PHASES
PIECE = PHASE_COLS // 2
STEP = 512

Z_UP, Z_DOWN, Z_UP_PIECE, Z_DOWN_PIECE = 0, 1, 2, 3
X_FIRST = 4
PAIR_FIRST = 20
F_MESSAGES = 20


def prune_prepare(ww, kp, fw, cur, scaled_drop, fw_t):
    factor = fw[...]
    fw_t[...] = factor.T
    row_id = lax.broadcasted_iota(jnp.int32, (WIN, WIN), 0)
    col_id = lax.broadcasted_iota(jnp.int32, (WIN, WIN), 1)
    diagonal = jnp.sum(jnp.where(row_id == col_id, factor, 0.0), axis=1, keepdims=True)
    drop = (1 - kp[...]).astype(F32).T
    scaled_drop[...] = drop * (1.0 / diagonal)
    cur[...] = ww[...].T


def prune_tile(k, cur, scaled_drop, fw_t, fw_s, err, err_blocks):
    low = k * SUB
    block_end = (low // BLOCK + 1) * BLOCK
    shape = (SUB, LOCAL_ROWS)
    tile = cur[low : low + SUB, :]
    drop = scaled_drop[low : low + SUB, :]
    place = lax.broadcasted_iota(jnp.int32, shape, 0)
    values = [jnp.broadcast_to(tile[s : s + 1, :], shape) for s in range(SUB)]
    errors = []
    tile_err = jnp.zeros(shape, F32)
    tile_out = jnp.zeros(shape, F32)
    for s in range(SUB):
        e = values[s] * jnp.broadcast_to(drop[s : s + 1, :], shape)
        for t in range(s + 1, SUB):
            values[t] = values[t] - fw_s[low + s, low + t] * e
        errors.append(e)
        tile_err = jnp.where(place == s, e, tile_err)
        tile_out = jnp.where(place == s, values[s] - fw_s[low + s, low + s] * e, tile_out)
    cur[low : low + SUB, :] = tile_out
    err[low : low + SUB, :] = tile_err
    at = ((k % 2) * CHIPS + k // 2) * SUB
    err_blocks[at : at + SUB, :] = tile_err
    start = low + SUB
    while start < block_end:
        end = min(start + 32, block_end)
        n = (end - start) // SUB
        part = cur[start:end, :].reshape(n, SUB, LOCAL_ROWS)
        for s in range(SUB):
            part = part - fw_t[start:end, low + s : low + s + 1].reshape(n, SUB, 1) * errors[s][None]
        cur[start:end, :] = part.reshape(n * SUB, LOCAL_ROWS)
        start = end
    if block_end == low + SUB and block_end < WIN:
        b = block_end - BLOCK
        cur[block_end:, :] = cur[block_end:, :] - jnp.dot(
            fw_t[block_end:, b:block_end], err[b:block_end, :],
            precision=lax.Precision.HIGHEST, preferred_element_type=F32,
        )


def compensate(rest, blocks, half, err_half):
    factor = blocks[:, half * 8 : half * 8 + 8, :].reshape(WIN, blocks.shape[2])
    change = lax.dot_general(
        factor, err_half, (((0,), (0,)), ((), ())), preferred_element_type=F32
    )
    return (rest.astype(F32) - change[: rest.shape[0]]).astype(BF16)


def kernel(
    ids_hbm, calib_hbm, keep_hbm, ww_hbm, rest_hbm, fw_hbm, fr_hbm,
    pruned_out, rest_out, hess_out, outs_out, fac, err_half,
    ids, cal, kp, ww, fw, fw_s, fr, fr_block, xin, x_t, cur, scaled_drop, err, err_blocks, fw_t, x_half, local_outs, z_relay, x_relay,
    gram, gram_half, relay_in, relay_out, from_left, from_right, peer_out, peer_in,
    load_sem, f_send, f_recv, pair_recv, scat_send, scat_recv, xz_send, xz_recv, xx_send, xx_recv, xp_sem,
    o_send, o_recv, relay_recv, h_send, h_recv,
):
    tok, row = lax.axis_index("tok"), lax.axis_index("row")
    x, h, c = row // 8, (row // 2) % 4, row % 2
    l, y = tok // 4, tok % 4
    chip = x * 4 + h

    def row_of(px, ph, pc):
        return ((px + 4) % 4) * 8 + ((ph + 4) % 4) * 2 + pc

    def remote(src, dst, ssem, rsem, to_row=None, to_tok=None):
        return pltpu.make_async_remote_copy(
            src_ref=src, dst_ref=dst, send_sem=ssem, recv_sem=rsem,
            device_id=(tok if to_tok is None else to_tok, row if to_row is None else to_row),
            device_id_type=MESH,
        )

    loads = [
        pltpu.make_async_copy(s, d, load_sem.at[i])
        for i, (s, d) in enumerate(
            [(fr_hbm, fr), (calib_hbm, cal), (ww_hbm, ww), (keep_hbm, kp), (fw_hbm, fw), (ids_hbm, ids), (rest_hbm, rest_out), (fw_hbm, fw_s)]
        )
    ]
    for load in loads[:6] + loads[7:]:
        load.start()

    barrier = pltpu.get_barrier_semaphore()

    def greet(d, carry):
        pl.semaphore_signal(barrier, inc=1, device_id=(tok, (row + d) % N_ROW), device_id_type=MESH)
        return carry

    lax.fori_loop(1, N_ROW, greet, 0)
    up_tok, down_tok, other_tok = l * 4 + (y + 1) % 4, l * 4 + (y + 3) % 4, (1 - l) * 4 + y
    for peer in (up_tok, down_tok, other_tok):
        pl.semaphore_signal(barrier, inc=1, device_id=(peer, row), device_id_type=MESH)
    pl.semaphore_wait(barrier, N_ROW - 1 + 3)

    is_source = row == 0

    def scatter(r):
        first = pl.multiple_of((r % 2) * 256 + (r // 2) * 16, 16)
        return remote(
            cal.at[pl.ds(first, 16), pl.ds(0, WIN)], xin.at[r % 2, r // 2], scat_send.at[r], scat_recv.at[0], to_row=r
        )

    loads[0].wait()
    fr_block[0:8, :] = fr[:, 0:HALF]
    fr_block[8:16, HALF - 128 :] = jnp.zeros((8, 128), F32)
    fr_block[8:16, 0 : REST - HALF] = fr[:, HALF:REST]
    fac[c * CHIPS + chip] = fr_block[...].astype(BF16)

    def f_copy(p, number, slot, to_row, piece=None):
        first, size = p * PHASE_COLS, PHASE_COLS
        if piece is not None:
            first, size = first + piece * PIECE, PIECE
        ref = fac.at[c * CHIPS + slot, :, pl.ds(first, size)]
        rsem = pair_recv.at[p] if number >= PAIR_FIRST else f_recv.at[p, number]
        return remote(ref, ref, f_send.at[0], rsem, to_row=to_row)

    x_up, x_down = row_of(x + 1, h, c), row_of(x - 1, h, c)
    z_up, z_down = row_of(x, h + 1, c), row_of(x, h - 1, c)
    pair = row_of(x, h, 1 - c)
    z_slots = [h, (h + 3) % 4, (h + 1) % 4, (h + 2) % 4]
    x_slots = [x, (x + 3) % 4, (x + 1) % 4, (x + 2) % 4]

    def f_start(*args, **kw):
        f_copy(*args, **kw).start()

    def f_from_z(p, j):
        slot = x * 4 + z_slots[j]
        if j == 1:
            f_start(p, Z_UP_PIECE, slot, z_up, piece=0)
        if j == 2:
            f_start(p, Z_DOWN_PIECE, slot, z_down, piece=1)
        f_start(p, X_FIRST + 4 * j, slot, x_up)
        f_start(p, X_FIRST + 4 * j + 1, slot, x_down)
        f_start(p, PAIR_FIRST + j, slot, pair)

    def f_own(p):
        f_start(p, Z_UP, chip, z_up)
        f_start(p, Z_DOWN, chip, z_down)
        f_from_z(p, 0)

    def f_z_neighbours(p):
        f_copy(p, Z_UP, x * 4 + z_slots[1], z_up).wait_recv()
        f_from_z(p, 1)
        f_copy(p, Z_DOWN, x * 4 + z_slots[2], z_down).wait_recv()
        f_from_z(p, 2)

    def f_z_opposite(p):
        slot = x * 4 + z_slots[3]
        f_copy(p, Z_UP_PIECE, slot, z_up, piece=0).wait_recv()
        f_copy(p, Z_DOWN_PIECE, slot, z_down, piece=1).wait_recv()
        f_from_z(p, 3)

    def f_x_neighbours(p, j):
        n = X_FIRST + 4 * j
        slot = x_slots[1] * 4 + z_slots[j]
        f_copy(p, n, slot, x_up).wait_recv()
        f_start(p, n + 2, slot, x_up, piece=0)
        f_start(p, PAIR_FIRST + 4 + j, slot, pair)
        slot = x_slots[2] * 4 + z_slots[j]
        f_copy(p, n + 1, slot, x_down).wait_recv()
        f_start(p, n + 3, slot, x_down, piece=1)
        f_start(p, PAIR_FIRST + 8 + j, slot, pair)

    def f_x_opposite(p, j):
        n = X_FIRST + 4 * j
        slot = x_slots[3] * 4 + z_slots[j]
        f_copy(p, n + 2, slot, x_up, piece=0).wait_recv()
        f_copy(p, n + 3, slot, x_down, piece=1).wait_recv()
        f_start(p, PAIR_FIRST + 12 + j, slot, pair)

    def f_pair_wait(p):
        ref = fac.at[pl.ds((1 - c) * CHIPS, CHIPS), :, pl.ds(p * PHASE_COLS, PHASE_COLS)]
        remote(ref, ref, f_send.at[0], pair_recv.at[p], to_row=pair).wait_recv()

    loads[1].wait()

    @pl.when(is_source)
    def _():
        def send(r, carry):
            scatter(r).start()
            return carry

        lax.fori_loop(1, N_ROW, send, 0)
        xin[0, 0] = cal[0:16, 0:WIN]

    def xz_copy(d):
        ref = xin.at[c, chip]
        return remote(ref, ref, xz_send.at[d], xz_recv.at[d], to_row=row_of(x, h + d, c))

    def xx_copy(d):
        ref = xin.at[c, pl.ds(x * 4, 4)]
        return remote(ref, ref, xx_send.at[d], xx_recv.at[d], to_row=row_of(x + d, h, c))

    xp_copy = remote(xin.at[c], xin.at[c], xp_sem.at[0], xp_sem.at[1], to_row=pair)

    def inputs_along_z():
        @pl.when(jnp.logical_not(is_source))
        def _():
            ref = xin.at[c, chip]
            remote(ref, ref, scat_send.at[0], scat_recv.at[0], to_row=pair).wait_recv()

        for d in (1, 3, 2):
            xz_copy(d).start()

    def inputs_along_x():
        for d in (1, 3, 2):
            ref = xin.at[c, x * 4 + (h + 4 - d) % 4]
            remote(ref, ref, xz_send.at[d], xz_recv.at[d], to_row=row_of(x, h + d, c)).wait_recv()
        for d in (1, 3, 2):
            xx_copy(d).start()

    def inputs_to_pair():
        for d in (1, 3, 2):
            ref = xin.at[c, pl.ds(((x + 4 - d) % 4) * 4, 4)]
            remote(ref, ref, xx_send.at[d], xx_recv.at[d], to_row=row_of(x + d, h, c)).wait_recv()
        xp_copy.start()

    def inputs_complete():
        remote(xin.at[1 - c], xin.at[1 - c], xp_sem.at[0], xp_sem.at[1], to_row=pair).wait_recv()
        loads[5].wait()
        live = jnp.where(ids[...] != 1, 1.0, 0.0)
        live_t = jnp.concatenate([live, jnp.zeros((4, 128), F32)], axis=0).T
        x_parts = []
        for s in range(4):
            part = xin[s // 2, (s % 2) * 8 : (s % 2) * 8 + 8].reshape(128, WIN).astype(F32)
            x_parts.append(part * live_t[:, s : s + 1])
        x_all = jnp.concatenate(x_parts, axis=0)
        x_t[...] = x_all.T.astype(BF16)
        x_half[...] = x_all.astype(BF16)

    def h_copy(number, src, dst, to_tok):
        return remote(src, dst, h_send.at[number], h_recv.at[number], to_tok=to_tok)

    h_copies = [
        h_copy(0, gram_half.at[(y + 2) % 4], relay_in.at[0], up_tok),
        h_copy(1, gram_half.at[4 + (y + 2) % 4], relay_in.at[1], down_tok),
        h_copy(2, gram_half.at[4 + (y + 1) % 4], from_left.at[1], up_tok),
        h_copy(3, gram_half.at[(y + 3) % 4], from_right.at[0], down_tok),
        h_copy(4, relay_out.at[0], from_left.at[0], up_tok),
        h_copy(5, relay_out.at[1], from_right.at[1], down_tok),
        h_copy(6, peer_out, peer_in, other_tok),
    ]

    def hessian_begin():
        @pl.loop(0, FEATURES // 256)
        def _(i):
            cols = pl.ds(pl.multiple_of(i * 256, 256), 256)
            part = jnp.dot(x_t[...], cal[:, cols], preferred_element_type=F32).reshape(N_TOK, 32, 256)
            gram[:, :, cols] = part
            gram_half[:, :, cols] = part.astype(BF16)

        for i in range(4):
            h_copies[i].start()

    def hessian_relay():
        h_copies[0].wait_recv()
        relay_out[0] = (relay_in[0].astype(F32) + gram[(y + 1) % 4]).astype(BF16)
        h_copies[4].start()
        h_copies[1].wait_recv()
        relay_out[1] = (relay_in[1].astype(F32) + gram[4 + (y + 3) % 4]).astype(BF16)
        h_copies[5].start()

    def hessian_peer():
        for i in range(2, 6):
            h_copies[i].wait_recv()
        peer_out[...] = (
            gram[(1 - l) * 4 + y] + from_left[1 - l].astype(F32) + from_right[1 - l].astype(F32)
        ).astype(BF16)
        h_copies[6].start()

    def hessian_end():
        h_copies[6].wait_recv()
        total = gram[l * 4 + y] + from_left[l].astype(F32) + from_right[l].astype(F32) + peer_in[...].astype(F32)
        hess_out[...] = total * (2.0 / TOKENS)

    def out_cols(sender):
        return pl.ds(pl.multiple_of(sender * LOCAL_ROWS, 128), LOCAL_ROWS)

    my_cols = out_cols(row)
    relays = [
        remote(local_outs.at[:, 3, 0], z_relay.at[0], o_send.at[0], relay_recv.at[0], to_row=z_up),
        remote(local_outs.at[:, 3, 1], z_relay.at[1], o_send.at[0], relay_recv.at[1], to_row=z_down),
        remote(local_outs.at[2, pl.ds(0, 3), 0], x_relay.at[0], o_send.at[0], relay_recv.at[2], to_row=x_up),
        remote(local_outs.at[2, pl.ds(0, 3), 1], x_relay.at[1], o_send.at[0], relay_recv.at[3], to_row=x_down),
    ]

    def send_outputs():
        found = jnp.dot(
            x_half[...], cur[...].astype(BF16), preferred_element_type=F32
        ).astype(BF16).reshape(N_ROW, 16, LOCAL_ROWS)
        for r in range(N_ROW):
            local_outs[(r // 8 - x + 4) % 4, ((r // 2) % 4 - h + 5) % 4, r % 2] = found[r]
        for relay in relays:
            relay.start()
        for dx in (1, 3, 0):
            for dh in (1, -1, 0):
                for dc in (0, 1):
                    if (dx, dh, dc) != (0, 0, 0):
                        oc = (c + dc) % 2
                        remote(
                            local_outs.at[dx, dh + 1, oc], outs_out.at[:, my_cols], o_send.at[0], o_recv.at[0],
                            to_row=row_of(x + dx, h + dh, oc),
                        ).start()

    def pass_on_z(way):
        relays[way].wait_recv()
        step = 1 if way == 0 else -1
        sender = row_of(x, h - step, c)
        for dx in range(4):
            remote(
                z_relay.at[way, dx], outs_out.at[:, out_cols(sender)], o_send.at[1], o_recv.at[0],
                to_row=row_of(x + dx, h + step, way),
            ).start()

    def pass_on_x(way):
        relays[2 + way].wait_recv()
        step = 1 if way == 0 else -1
        sender = row_of(x - step, h, c)
        for dh in (-1, 0, 1):
            remote(
                x_relay.at[way, dh + 1], outs_out.at[:, out_cols(sender)], o_send.at[2], o_recv.at[0],
                to_row=row_of(x + step, h + dh, way),
            ).start()

    arrived = outs_out.at[:, pl.ds(0, (N_ROW - 1) * LOCAL_ROWS)]

    def outputs_complete():
        remote(arrived, arrived, o_send.at[0], o_recv.at[0], to_row=pair).wait_recv()

    def prune(first, last):
        for k in range(first, last):
            prune_tile(k, cur, scaled_drop, fw_t, fw_s, err, err_blocks)

    def pruned_results():
        outs_out[:, my_cols] = local_outs[0, 1, c]
        pruned_out[...] = cur[...].T
        err_half[...] = err_blocks[...].astype(BF16)

    def update(p):
        for half in range(2):

            @pl.loop(0, PHASE_COLS // STEP)
            def _(i, half=half, p=p):
                first = pl.multiple_of(p * PHASE_COLS + i * STEP, STEP)
                rows = pl.ds(pl.multiple_of(half * HALF + first, STEP), STEP)
                rest_out[rows, :] = compensate(rest_out[rows, :], fac[:, :, pl.ds(first, STEP)], half, err_half[...])

    f_own(0)
    loads[6].start()
    for i in (2, 3, 4, 7):
        loads[i].wait()
    prune_prepare(ww, kp, fw, cur, scaled_drop, fw_t)
    prune(0, 4)
    inputs_along_z()
    prune(4, 12)
    f_x_neighbours(0, 0)
    prune(12, 16)
    inputs_along_x()
    prune(16, 24)
    f_z_neighbours(0)
    prune(24, 28)
    inputs_to_pair()
    prune(28, 32)
    inputs_complete()
    send_outputs()
    hessian_begin()
    f_z_opposite(0)
    f_x_opposite(0, 0)
    f_x_neighbours(0, 1)
    pruned_results()
    pass_on_z(1)
    f_x_neighbours(0, 2)
    pass_on_z(0)
    hessian_relay()
    f_x_neighbours(0, 3)
    pass_on_x(1)
    pass_on_x(0)
    hessian_peer()
    f_x_opposite(0, 1)
    f_x_opposite(0, 2)
    f_x_opposite(0, 3)
    outputs_complete()
    hessian_end()
    f_pair_wait(0)
    loads[6].wait()

    remote(arrived, arrived, o_send.at[0], o_recv.at[0], to_row=pair).wait_send()
    remote(z_relay, z_relay, o_send.at[1], o_recv.at[0], to_row=pair).wait_send()
    remote(x_relay, x_relay, o_send.at[2], o_recv.at[0], to_row=pair).wait_send()

    @pl.when(is_source)
    def _():
        def left(r, carry):
            scatter(r).wait_send()
            return carry

        lax.fori_loop(1, N_ROW, left, 0)

    for d in (1, 3, 2):
        xz_copy(d).wait_send()
        xx_copy(d).wait_send()
    xp_copy.wait_send()
    for copy in h_copies:
        copy.wait_send()
    sent = fac.at[pl.ds(0, 31)]
    remote(sent, sent, f_send.at[0], pair_recv.at[0], to_row=pair).wait_send()


def finish_kernel(
    pruned, rest, hess, outs, fac, err_half,
    pruned_hbm, rest_hbm, hess_hbm, outs_hbm,
    updated, sem,
):
    copies = [
        pltpu.make_async_copy(pruned, pruned_hbm, sem.at[0]),
        pltpu.make_async_copy(hess, hess_hbm, sem.at[1]),
        pltpu.make_async_copy(outs, outs_hbm, sem.at[2]),
    ]
    last = HALF - PHASE_COLS
    if last > 0:
        for half in range(2):
            rows = pl.ds(half * HALF, last)
            copies.append(pltpu.make_async_copy(rest.at[rows], rest_hbm.at[rows], sem.at[3 + half]))
    for copy in copies:
        copy.start()
    for half in range(2):
        for i in range(PHASE_COLS // STEP):
            first = last + i * STEP
            start = half * HALF + first
            count = min(STEP, REST - start)
            part = rest[start : start + count, :]
            at = half * PHASE_COLS + i * STEP
            updated[at : at + count, :] = compensate(part, fac[:, :, first : first + STEP], half, err_half[...])
            copy = pltpu.make_async_copy(
                updated.at[pl.ds(at, count)], rest_hbm.at[pl.ds(start, count)], sem.at[5 + half * (PHASE_COLS // STEP) + i]
            )
            copy.start()
            copies.append(copy)
    for copy in copies:
        copy.wait()


def on_device(token_ids, calib_input, keep_mask, weight_window, weight_rest, factor_window, factor_rest):
    vmem, dma = pltpu.VMEM, pltpu.SemaphoreType.DMA
    slab = (32, FEATURES)
    in_hbm = [
        pltpu.with_memory_space_constraint(a, pltpu.HBM)
        for a in (
            token_ids.reshape(4, 128), calib_input, keep_mask, weight_window, weight_rest.T, factor_window, factor_rest
        )
    ]
    shapes = [
        ((LOCAL_ROWS, WIN), F32),
        ((REST, LOCAL_ROWS), BF16),
        (slab, F32),
        ((16, N_ROW * LOCAL_ROWS), BF16),
    ]
    held = pl.pallas_call(
        kernel,
        out_shape=tuple(
            vmem(*s) for s in shapes + [((2 * CHIPS, 16, HALF), BF16), ((WIN, LOCAL_ROWS), BF16)]
        ),
        in_specs=[pl.BlockSpec(memory_space=pltpu.HBM)] * 7,
        out_specs=[pl.BlockSpec(memory_space=vmem)] * 6,
        scratch_shapes=[
            vmem((4, 128), jnp.int32),
            vmem((LOCAL_TOKENS, FEATURES), BF16),
            vmem((LOCAL_ROWS, WIN), jnp.int32),
            vmem((LOCAL_ROWS, WIN), F32),
            vmem((WIN, WIN), F32),
            pltpu.SMEM((WIN, WIN), F32),
            vmem((8, REST), F32),
            vmem((16, HALF), F32),
            vmem((2, CHIPS, 16, WIN), BF16),
            vmem((WIN, LOCAL_TOKENS), BF16),
            vmem((WIN, LOCAL_ROWS), F32),
            vmem((WIN, LOCAL_ROWS), F32),
            vmem((WIN, LOCAL_ROWS), F32),
            vmem((WIN, LOCAL_ROWS), F32),
            vmem((WIN, WIN), F32),
            vmem((LOCAL_TOKENS, WIN), BF16),
            vmem((4, 4, 2, 16, LOCAL_ROWS), BF16),
            vmem((2, 4, 16, LOCAL_ROWS), BF16),
            vmem((2, 3, 16, LOCAL_ROWS), BF16),
            vmem((N_TOK,) + slab, F32),
            vmem((N_TOK,) + slab, BF16),
            vmem((2,) + slab, BF16),
            vmem((2,) + slab, BF16),
            vmem((2,) + slab, BF16),
            vmem((2,) + slab, BF16),
            vmem(slab, BF16),
            vmem(slab, BF16),
            dma((8,)),
            dma((1,)),
            dma((PHASES, F_MESSAGES)),
            dma((PHASES,)),
            dma((N_ROW,)),
            dma((1,)),
            dma((4,)),
            dma((4,)),
            dma((4,)),
            dma((4,)),
            dma((2,)),
            dma((3,)),
            dma((1,)),
            dma((4,)),
            dma((7,)),
            dma((7,)),
        ],
        compiler_params=pltpu.CompilerParams(
            collective_id=0, has_side_effects=True, vmem_limit_bytes=32 * 1024 * 1024
        ),
        cost_estimate=pl.CostEstimate(flops=2_000_000_000, bytes_accessed=16_000_000, transcendentals=0),
    )(*in_hbm)
    pruned, rest_t, hess, outs = pl.pallas_call(
        finish_kernel,
        out_shape=tuple(jax.ShapeDtypeStruct(*s) for s in shapes),
        in_specs=[pl.BlockSpec(memory_space=vmem)] * 6,
        out_specs=[pl.BlockSpec(memory_space=pltpu.HBM)] * 4,
        scratch_shapes=[
            vmem((2 * PHASE_COLS, LOCAL_ROWS), BF16),
            dma((5 + 2 * (PHASE_COLS // STEP),)),
        ],
        compiler_params=pltpu.CompilerParams(vmem_limit_bytes=32 * 1024 * 1024),
        cost_estimate=pl.CostEstimate(flops=600_000_000, bytes_accessed=12_000_000, transcendentals=0),
    )(*[pltpu.with_memory_space_constraint(a, vmem) for a in held])
    return pruned, rest_t.T, hess, outs


def solution(mesh):
    return jax.shard_map(
        on_device,
        mesh=mesh,
        in_specs=(
            P("tok"),
            P("tok", "row"),
            P("row", None),
            P("row", None),
            P("row", "tok"),
            P(),
            P("row", "tok"),
        ),
        out_specs=(P("row", None), P("row", "tok"), P("tok", "row"), P(("tok", "row"), None)),
        check_vma=False,
    )
```

```python
import jax
import jax.numpy as jnp
from jax import lax
from jax.experimental import pallas as pl
from jax.experimental.pallas import tpu as pltpu
from jax.sharding import PartitionSpec as P

MESH = pl.DeviceIdType.MESH
F32, BF16 = jnp.float32, jnp.bfloat16

WIN = 256
BLOCK = 128
SUB = 8
LOCAL_ROWS = 384
LOCAL_TOKENS = 512
FEATURES = 1536
REST = 6112
HALF = 3072
N_ROW = 32
N_TOK = 8
CHIPS = 16
TOKENS = LOCAL_TOKENS * N_TOK

PHASES = 1
PHASE_COLS = HALF // PHASES
PIECE = PHASE_COLS // 2
STEP = 512

Z_UP, Z_DOWN, Z_UP_PIECE, Z_DOWN_PIECE = 0, 1, 2, 3
X_FIRST = 4
PAIR_FIRST = 20
F_MESSAGES = 20


def prune_prepare(ww, kp, fw, cur, scaled_drop, fw_t):
    factor = fw[...]
    fw_t[...] = factor.T
    row_id = lax.broadcasted_iota(jnp.int32, (WIN, WIN), 0)
    col_id = lax.broadcasted_iota(jnp.int32, (WIN, WIN), 1)
    diagonal = jnp.sum(jnp.where(row_id == col_id, factor, 0.0), axis=1, keepdims=True)
    drop = (1 - kp[...]).astype(F32).T
    scaled_drop[...] = drop * (1.0 / diagonal)
    cur[...] = ww[...].T


def prune_tile(k, cur, scaled_drop, fw_t, fw_s, err, err_blocks):
    low = k * SUB
    block_end = (low // BLOCK + 1) * BLOCK
    shape = (SUB, LOCAL_ROWS)
    tile = cur[low : low + SUB, :]
    drop = scaled_drop[low : low + SUB, :]
    place = lax.broadcasted_iota(jnp.int32, shape, 0)
    values = [jnp.broadcast_to(tile[s : s + 1, :], shape) for s in range(SUB)]
    errors = []
    tile_err = jnp.zeros(shape, F32)
    tile_out = jnp.zeros(shape, F32)
    for s in range(SUB):
        e = values[s] * jnp.broadcast_to(drop[s : s + 1, :], shape)
        for t in range(s + 1, SUB):
            values[t] = values[t] - fw_s[low + s, low + t] * e
        errors.append(e)
        tile_err = jnp.where(place == s, e, tile_err)
        tile_out = jnp.where(place == s, values[s] - fw_s[low + s, low + s] * e, tile_out)
    cur[low : low + SUB, :] = tile_out
    err[low : low + SUB, :] = tile_err
    at = ((k % 2) * CHIPS + k // 2) * SUB
    err_blocks[at : at + SUB, :] = tile_err
    start = low + SUB
    while start < block_end:
        end = min(start + 32, block_end)
        n = (end - start) // SUB
        part = cur[start:end, :].reshape(n, SUB, LOCAL_ROWS)
        for s in range(SUB):
            part = part - fw_t[start:end, low + s : low + s + 1].reshape(n, SUB, 1) * errors[s][None]
        cur[start:end, :] = part.reshape(n * SUB, LOCAL_ROWS)
        start = end
    if block_end == low + SUB and block_end < WIN:
        b = block_end - BLOCK
        cur[block_end:, :] = cur[block_end:, :] - jnp.dot(
            fw_t[block_end:, b:block_end], err[b:block_end, :],
            precision=lax.Precision.HIGHEST, preferred_element_type=F32,
        )


def compensate(rest, blocks, half, err_half):
    factor = blocks[:, half * 8 : half * 8 + 8, :].reshape(WIN, blocks.shape[2])
    change = lax.dot_general(
        factor, err_half, (((0,), (0,)), ((), ())), preferred_element_type=F32
    )
    return (rest.astype(F32) - change[: rest.shape[0]]).astype(BF16)


def kernel(
    ids_hbm, calib_hbm, keep_hbm, ww_hbm, rest_hbm, fw_hbm, fr_hbm,
    pruned_out, rest_out, hess_out, outs_out, fac, err_half,
    ids, cal, kp, ww, fw, fw_s, fr, fr_block, x_slabs, xin, x_t, cur, scaled_drop, err, err_blocks, fw_t, x_half, local_outs, z_relay, x_relay,
    gram, gram_half, relay_in, relay_out, from_left, from_right, peer_out, peer_in,
    load_sem, half_sem, f_send, f_recv, pair_recv, scat_send, scat_recv, xz_send, xz_recv, xx_send, xx_recv, xp_sem,
    o_send, o_recv, relay_recv, h_send, h_recv,
):
    tok, row = lax.axis_index("tok"), lax.axis_index("row")
    x, h, c = row // 8, (row // 2) % 4, row % 2
    l, y = tok // 4, tok % 4
    chip = x * 4 + h

    def row_of(px, ph, pc):
        return ((px + 4) % 4) * 8 + ((ph + 4) % 4) * 2 + pc

    def remote(src, dst, ssem, rsem, to_row=None, to_tok=None):
        return pltpu.make_async_remote_copy(
            src_ref=src, dst_ref=dst, send_sem=ssem, recv_sem=rsem,
            device_id=(tok if to_tok is None else to_tok, row if to_row is None else to_row),
            device_id_type=MESH,
        )

    loads = [
        pltpu.make_async_copy(s, d, load_sem.at[i])
        for i, (s, d) in enumerate(
            [(fr_hbm, fr), (calib_hbm, cal), (ww_hbm, ww), (keep_hbm, kp), (fw_hbm, fw), (ids_hbm, ids), (rest_hbm, rest_out), (fw_hbm, fw_s)]
        )
    ]
    for load in loads[:6] + loads[7:]:
        load.start()

    barrier = pltpu.get_barrier_semaphore()

    for d in range(1, N_ROW):
        pl.semaphore_signal(barrier, inc=1, device_id=(tok, (row + d) % N_ROW), device_id_type=MESH)
    up_tok, down_tok, other_tok = l * 4 + (y + 1) % 4, l * 4 + (y + 3) % 4, (1 - l) * 4 + y
    for peer in (up_tok, down_tok, other_tok):
        pl.semaphore_signal(barrier, inc=1, device_id=(peer, row), device_id_type=MESH)
    pl.semaphore_wait(barrier, N_ROW - 1 + 3)

    loads[0].wait()
    fr_block[0:8, :] = fr[:, 0:HALF]
    fr_block[8:16, HALF - 128 :] = jnp.zeros((8, 128), F32)
    fr_block[8:16, 0 : REST - HALF] = fr[:, HALF:REST]
    fac[c * CHIPS + chip] = fr_block[...].astype(BF16)

    def f_copy(p, number, slot, to_row, piece=None):
        first, size = p * PHASE_COLS, PHASE_COLS
        if piece is not None:
            first, size = first + piece * PIECE, PIECE
        ref = fac.at[c * CHIPS + slot, :, pl.ds(first, size)]
        rsem = pair_recv.at[p] if number >= PAIR_FIRST else f_recv.at[p, number]
        return remote(ref, ref, f_send.at[0], rsem, to_row=to_row)

    x_up, x_down = row_of(x + 1, h, c), row_of(x - 1, h, c)
    z_up, z_down = row_of(x, h + 1, c), row_of(x, h - 1, c)
    pair = row_of(x, h, 1 - c)
    z_slots = [h, (h + 3) % 4, (h + 1) % 4, (h + 2) % 4]
    x_slots = [x, (x + 3) % 4, (x + 1) % 4, (x + 2) % 4]

    def f_start(*args, **kw):
        f_copy(*args, **kw).start()

    def f_from_z(p, j):
        slot = x * 4 + z_slots[j]
        if j == 1:
            f_start(p, Z_UP_PIECE, slot, z_up, piece=0)
        if j == 2:
            f_start(p, Z_DOWN_PIECE, slot, z_down, piece=1)
        f_start(p, X_FIRST + 4 * j, slot, x_up)
        f_start(p, X_FIRST + 4 * j + 1, slot, x_down)
        f_start(p, PAIR_FIRST + j, slot, pair)

    def f_own(p):
        f_start(p, Z_UP, chip, z_up)
        f_start(p, Z_DOWN, chip, z_down)
        f_from_z(p, 0)

    def f_z_neighbours(p):
        f_copy(p, Z_UP, x * 4 + z_slots[1], z_up).wait_recv()
        f_from_z(p, 1)
        f_copy(p, Z_DOWN, x * 4 + z_slots[2], z_down).wait_recv()
        f_from_z(p, 2)

    def f_z_opposite(p):
        slot = x * 4 + z_slots[3]
        f_copy(p, Z_UP_PIECE, slot, z_up, piece=0).wait_recv()
        f_copy(p, Z_DOWN_PIECE, slot, z_down, piece=1).wait_recv()
        f_from_z(p, 3)

    def f_x_neighbours(p, j):
        n = X_FIRST + 4 * j
        slot = x_slots[1] * 4 + z_slots[j]
        f_copy(p, n, slot, x_up).wait_recv()
        f_start(p, n + 2, slot, x_up, piece=0)
        f_start(p, PAIR_FIRST + 4 + j, slot, pair)
        slot = x_slots[2] * 4 + z_slots[j]
        f_copy(p, n + 1, slot, x_down).wait_recv()
        f_start(p, n + 3, slot, x_down, piece=1)
        f_start(p, PAIR_FIRST + 8 + j, slot, pair)

    def f_x_opposite(p, j):
        n = X_FIRST + 4 * j
        slot = x_slots[3] * 4 + z_slots[j]
        f_copy(p, n + 2, slot, x_up, piece=0).wait_recv()
        f_copy(p, n + 3, slot, x_down, piece=1).wait_recv()
        f_start(p, PAIR_FIRST + 12 + j, slot, pair)

    def f_pair_wait(p):
        ref = fac.at[pl.ds((1 - c) * CHIPS, CHIPS), :, pl.ds(p * PHASE_COLS, PHASE_COLS)]
        remote(ref, ref, f_send.at[0], pair_recv.at[p], to_row=pair).wait_recv()

    is_source_chip = row < 2
    half_copy = remote(cal.at[pl.ds(256, 256), pl.ds(0, WIN)], x_slabs, half_sem.at[0], half_sem.at[1], to_row=pair)

    def scatter(q):
        return remote(
            x_slabs.at[pl.ds(q * 16, 16)], xin.at[c, q], scat_send.at[0], scat_recv.at[0],
            to_row=(q // 4) * 8 + (q % 4) * 2 + c,
        )

    def scatter_inputs():
        loads[1].wait()

        @pl.when(row == 0)
        def _():
            half_copy.start()
            x_slabs[...] = cal[0:256, 0:WIN]

        @pl.when(is_source_chip)
        def _():
            @pl.when(row == 1)
            def _():
                half_copy.wait_recv()

            for q in range(1, CHIPS):
                scatter(q).start()
            xin[c, 0] = x_slabs[0:16, :]

    def xz_copy(d):
        ref = xin.at[c, chip]
        return remote(ref, ref, xz_send.at[d], xz_recv.at[d], to_row=row_of(x, h + d, c))

    def xx_copy(d):
        ref = xin.at[c, pl.ds(x * 4, 4)]
        return remote(ref, ref, xx_send.at[d], xx_recv.at[d], to_row=row_of(x + d, h, c))

    xp_copy = remote(xin.at[c], xin.at[c], xp_sem.at[0], xp_sem.at[1], to_row=pair)

    def inputs_along_z():
        @pl.when(jnp.logical_not(is_source_chip))
        def _():
            ref = xin.at[c, chip]
            remote(ref, ref, scat_send.at[0], scat_recv.at[0], to_row=pair).wait_recv()

        for d in (1, 3, 2):
            xz_copy(d).start()

    def inputs_along_x():
        for d in (1, 3, 2):
            ref = xin.at[c, x * 4 + (h + 4 - d) % 4]
            remote(ref, ref, xz_send.at[d], xz_recv.at[d], to_row=row_of(x, h + d, c)).wait_recv()
        for d in (1, 3, 2):
            xx_copy(d).start()

    def inputs_to_pair():
        for d in (1, 3, 2):
            ref = xin.at[c, pl.ds(((x + 4 - d) % 4) * 4, 4)]
            remote(ref, ref, xx_send.at[d], xx_recv.at[d], to_row=row_of(x + d, h, c)).wait_recv()
        xp_copy.start()

    def inputs_complete():
        remote(xin.at[1 - c], xin.at[1 - c], xp_sem.at[0], xp_sem.at[1], to_row=pair).wait_recv()
        loads[5].wait()
        live = jnp.where(ids[...] != 1, 1.0, 0.0)
        live_t = jnp.concatenate([live, jnp.zeros((4, 128), F32)], axis=0).T
        x_parts = []
        for s in range(4):
            part = xin[s // 2, (s % 2) * 8 : (s % 2) * 8 + 8].reshape(128, WIN).astype(F32)
            x_parts.append(part * live_t[:, s : s + 1])
        x_all = jnp.concatenate(x_parts, axis=0)
        x_t[...] = x_all.T.astype(BF16)
        x_half[...] = x_all.astype(BF16)

    def h_copy(number, src, dst, to_tok):
        return remote(src, dst, h_send.at[number], h_recv.at[number], to_tok=to_tok)

    h_copies = [
        h_copy(0, gram_half.at[(y + 2) % 4], relay_in.at[0], up_tok),
        h_copy(1, gram_half.at[4 + (y + 2) % 4], relay_in.at[1], down_tok),
        h_copy(2, gram_half.at[4 + (y + 1) % 4], from_left.at[1], up_tok),
        h_copy(3, gram_half.at[(y + 3) % 4], from_right.at[0], down_tok),
        h_copy(4, relay_out.at[0], from_left.at[0], up_tok),
        h_copy(5, relay_out.at[1], from_right.at[1], down_tok),
        h_copy(6, peer_out, peer_in, other_tok),
    ]

    def hessian_begin():
        @pl.loop(0, FEATURES // 256)
        def _(i):
            cols = pl.ds(pl.multiple_of(i * 256, 256), 256)
            part = jnp.dot(x_t[...], cal[:, cols], preferred_element_type=F32).reshape(N_TOK, 32, 256)
            gram[:, :, cols] = part
            gram_half[:, :, cols] = part.astype(BF16)

        for i in range(4):
            h_copies[i].start()

    def hessian_relay():
        h_copies[0].wait_recv()
        relay_out[0] = (relay_in[0].astype(F32) + gram[(y + 1) % 4]).astype(BF16)
        h_copies[4].start()
        h_copies[1].wait_recv()
        relay_out[1] = (relay_in[1].astype(F32) + gram[4 + (y + 3) % 4]).astype(BF16)
        h_copies[5].start()

    def hessian_peer():
        for i in range(2, 6):
            h_copies[i].wait_recv()
        peer_out[...] = (
            gram[(1 - l) * 4 + y] + from_left[1 - l].astype(F32) + from_right[1 - l].astype(F32)
        ).astype(BF16)
        h_copies[6].start()

    def hessian_end():
        h_copies[6].wait_recv()
        total = gram[l * 4 + y] + from_left[l].astype(F32) + from_right[l].astype(F32) + peer_in[...].astype(F32)
        hess_out[...] = total * (2.0 / TOKENS)

    def out_cols(sender):
        return pl.ds(pl.multiple_of(sender * LOCAL_ROWS, 128), LOCAL_ROWS)

    my_cols = out_cols(row)
    relays = [
        remote(local_outs.at[:, 3, 0], z_relay.at[0], o_send.at[0], relay_recv.at[0], to_row=z_up),
        remote(local_outs.at[:, 3, 1], z_relay.at[1], o_send.at[0], relay_recv.at[1], to_row=z_down),
        remote(local_outs.at[2, pl.ds(0, 3), 0], x_relay.at[0], o_send.at[0], relay_recv.at[2], to_row=x_up),
        remote(local_outs.at[2, pl.ds(0, 3), 1], x_relay.at[1], o_send.at[0], relay_recv.at[3], to_row=x_down),
    ]

    def send_outputs():
        found = jnp.dot(
            x_half[...], cur[...].astype(BF16), preferred_element_type=F32
        ).astype(BF16).reshape(N_ROW, 16, LOCAL_ROWS)
        for r in range(N_ROW):
            local_outs[(r // 8 - x + 4) % 4, ((r // 2) % 4 - h + 5) % 4, r % 2] = found[r]
        for relay in relays:
            relay.start()
        for dx in (1, 3, 0):
            for dh in (1, -1, 0):
                for dc in (0, 1):
                    if (dx, dh, dc) != (0, 0, 0):
                        oc = (c + dc) % 2
                        remote(
                            local_outs.at[dx, dh + 1, oc], outs_out.at[:, my_cols], o_send.at[0], o_recv.at[0],
                            to_row=row_of(x + dx, h + dh, oc),
                        ).start()

    def pass_on_z(way):
        relays[way].wait_recv()
        step = 1 if way == 0 else -1
        sender = row_of(x, h - step, c)
        for dx in range(4):
            remote(
                z_relay.at[way, dx], outs_out.at[:, out_cols(sender)], o_send.at[1], o_recv.at[0],
                to_row=row_of(x + dx, h + step, way),
            ).start()

    def pass_on_x(way):
        relays[2 + way].wait_recv()
        step = 1 if way == 0 else -1
        sender = row_of(x - step, h, c)
        for dh in (-1, 0, 1):
            remote(
                x_relay.at[way, dh + 1], outs_out.at[:, out_cols(sender)], o_send.at[2], o_recv.at[0],
                to_row=row_of(x + step, h + dh, way),
            ).start()

    arrived = outs_out.at[:, pl.ds(0, (N_ROW - 1) * LOCAL_ROWS)]

    def outputs_complete():
        remote(arrived, arrived, o_send.at[0], o_recv.at[0], to_row=pair).wait_recv()

    def prune(first, last):
        for k in range(first, last):
            prune_tile(k, cur, scaled_drop, fw_t, fw_s, err, err_blocks)

    def pruned_results():
        outs_out[:, my_cols] = local_outs[0, 1, c]
        pruned_out[...] = cur[...].T
        err_half[...] = err_blocks[...].astype(BF16)

    def update(p):
        for half in range(2):

            @pl.loop(0, PHASE_COLS // STEP)
            def _(i, half=half, p=p):
                first = pl.multiple_of(p * PHASE_COLS + i * STEP, STEP)
                rows = pl.ds(pl.multiple_of(half * HALF + first, STEP), STEP)
                rest_out[rows, :] = compensate(rest_out[rows, :], fac[:, :, pl.ds(first, STEP)], half, err_half[...])

    f_own(0)
    scatter_inputs()
    loads[6].start()
    for i in (2, 3, 4, 7):
        loads[i].wait()
    prune_prepare(ww, kp, fw, cur, scaled_drop, fw_t)
    prune(0, 4)
    inputs_along_z()
    prune(4, 12)
    f_x_neighbours(0, 0)
    prune(12, 16)
    inputs_along_x()
    prune(16, 24)
    f_z_neighbours(0)
    prune(24, 28)
    inputs_to_pair()
    prune(28, 32)
    inputs_complete()
    send_outputs()
    hessian_begin()
    f_z_opposite(0)
    f_x_opposite(0, 0)
    f_x_neighbours(0, 1)
    pruned_results()
    pass_on_z(1)
    f_x_neighbours(0, 2)
    pass_on_z(0)
    hessian_relay()
    f_x_neighbours(0, 3)
    pass_on_x(1)
    pass_on_x(0)
    hessian_peer()
    f_x_opposite(0, 1)
    f_x_opposite(0, 2)
    f_x_opposite(0, 3)
    outputs_complete()
    hessian_end()
    f_pair_wait(0)
    loads[6].wait()

    remote(arrived, arrived, o_send.at[0], o_recv.at[0], to_row=pair).wait_send()
    remote(z_relay, z_relay, o_send.at[1], o_recv.at[0], to_row=pair).wait_send()
    remote(x_relay, x_relay, o_send.at[2], o_recv.at[0], to_row=pair).wait_send()

    @pl.when(row == 0)
    def _():
        half_copy.wait_send()

    @pl.when(is_source_chip)
    def _():
        sent = x_slabs.at[pl.ds(16, 240)]
        remote(sent, sent, scat_send.at[0], scat_recv.at[0], to_row=pair).wait_send()

    for d in (1, 3, 2):
        xz_copy(d).wait_send()
        xx_copy(d).wait_send()
    xp_copy.wait_send()
    for copy in h_copies:
        copy.wait_send()
    sent = fac.at[pl.ds(0, 31)]
    remote(sent, sent, f_send.at[0], pair_recv.at[0], to_row=pair).wait_send()


def finish_kernel(
    pruned, rest, hess, outs, fac, err_half,
    pruned_hbm, rest_hbm, hess_hbm, outs_hbm,
    updated, sem,
):
    copies = [
        pltpu.make_async_copy(pruned, pruned_hbm, sem.at[0]),
        pltpu.make_async_copy(hess, hess_hbm, sem.at[1]),
        pltpu.make_async_copy(outs, outs_hbm, sem.at[2]),
    ]
    last = HALF - PHASE_COLS
    if last > 0:
        for half in range(2):
            rows = pl.ds(half * HALF, last)
            copies.append(pltpu.make_async_copy(rest.at[rows], rest_hbm.at[rows], sem.at[3 + half]))
    for copy in copies:
        copy.start()
    for half in range(2):
        for i in range(PHASE_COLS // STEP):
            first = last + i * STEP
            start = half * HALF + first
            count = min(STEP, REST - start)
            part = rest[start : start + count, :]
            at = half * PHASE_COLS + i * STEP
            updated[at : at + count, :] = compensate(part, fac[:, :, first : first + STEP], half, err_half[...])
            copy = pltpu.make_async_copy(
                updated.at[pl.ds(at, count)], rest_hbm.at[pl.ds(start, count)], sem.at[5 + half * (PHASE_COLS // STEP) + i]
            )
            copy.start()
            copies.append(copy)
    for copy in copies:
        copy.wait()


def on_device(token_ids, calib_input, keep_mask, weight_window, weight_rest, factor_window, factor_rest):
    vmem, dma = pltpu.VMEM, pltpu.SemaphoreType.DMA
    slab = (32, FEATURES)
    in_hbm = [
        pltpu.with_memory_space_constraint(a, pltpu.HBM)
        for a in (
            token_ids.reshape(4, 128), calib_input, keep_mask, weight_window, weight_rest.T, factor_window, factor_rest
        )
    ]
    shapes = [
        ((LOCAL_ROWS, WIN), F32),
        ((REST, LOCAL_ROWS), BF16),
        (slab, F32),
        ((16, N_ROW * LOCAL_ROWS), BF16),
    ]
    held = pl.pallas_call(
        kernel,
        out_shape=tuple(
            vmem(*s) for s in shapes + [((2 * CHIPS, 16, HALF), BF16), ((WIN, LOCAL_ROWS), BF16)]
        ),
        in_specs=[pl.BlockSpec(memory_space=pltpu.HBM)] * 7,
        out_specs=[pl.BlockSpec(memory_space=vmem)] * 6,
        scratch_shapes=[
            vmem((4, 128), jnp.int32),
            vmem((LOCAL_TOKENS, FEATURES), BF16),
            vmem((LOCAL_ROWS, WIN), jnp.int32),
            vmem((LOCAL_ROWS, WIN), F32),
            vmem((WIN, WIN), F32),
            pltpu.SMEM((WIN, WIN), F32),
            vmem((8, REST), F32),
            vmem((16, HALF), F32),
            vmem((256, WIN), BF16),
            vmem((2, CHIPS, 16, WIN), BF16),
            vmem((WIN, LOCAL_TOKENS), BF16),
            vmem((WIN, LOCAL_ROWS), F32),
            vmem((WIN, LOCAL_ROWS), F32),
            vmem((WIN, LOCAL_ROWS), F32),
            vmem((WIN, LOCAL_ROWS), F32),
            vmem((WIN, WIN), F32),
            vmem((LOCAL_TOKENS, WIN), BF16),
            vmem((4, 4, 2, 16, LOCAL_ROWS), BF16),
            vmem((2, 4, 16, LOCAL_ROWS), BF16),
            vmem((2, 3, 16, LOCAL_ROWS), BF16),
            vmem((N_TOK,) + slab, F32),
            vmem((N_TOK,) + slab, BF16),
            vmem((2,) + slab, BF16),
            vmem((2,) + slab, BF16),
            vmem((2,) + slab, BF16),
            vmem((2,) + slab, BF16),
            vmem(slab, BF16),
            vmem(slab, BF16),
            dma((8,)),
            dma((2,)),
            dma((1,)),
            dma((PHASES, F_MESSAGES)),
            dma((PHASES,)),
            dma((1,)),
            dma((1,)),
            dma((4,)),
            dma((4,)),
            dma((4,)),
            dma((4,)),
            dma((2,)),
            dma((3,)),
            dma((1,)),
            dma((4,)),
            dma((7,)),
            dma((7,)),
        ],
        compiler_params=pltpu.CompilerParams(
            collective_id=0, has_side_effects=True, vmem_limit_bytes=32 * 1024 * 1024
        ),
        cost_estimate=pl.CostEstimate(flops=2_000_000_000, bytes_accessed=16_000_000, transcendentals=0),
    )(*in_hbm)
    pruned, rest_t, hess, outs = pl.pallas_call(
        finish_kernel,
        out_shape=tuple(jax.ShapeDtypeStruct(*s) for s in shapes),
        in_specs=[pl.BlockSpec(memory_space=vmem)] * 6,
        out_specs=[pl.BlockSpec(memory_space=pltpu.HBM)] * 4,
        scratch_shapes=[
            vmem((2 * PHASE_COLS, LOCAL_ROWS), BF16),
            dma((5 + 2 * (PHASE_COLS // STEP),)),
        ],
        compiler_params=pltpu.CompilerParams(vmem_limit_bytes=32 * 1024 * 1024),
        cost_estimate=pl.CostEstimate(flops=600_000_000, bytes_accessed=12_000_000, transcendentals=0),
    )(*[pltpu.with_memory_space_constraint(a, vmem) for a in held])
    return pruned, rest_t.T, hess, outs


def solution(mesh):
    return jax.shard_map(
        on_device,
        mesh=mesh,
        in_specs=(
            P("tok"),
            P("tok", "row"),
            P("row", None),
            P("row", None),
            P("row", "tok"),
            P(),
            P("row", "tok"),
        ),
        out_specs=(P("row", None), P("row", "tok"), P("tok", "row"), P(("tok", "row"), None)),
        check_vma=False,
    )
```

```python
import jax
import jax.numpy as jnp
from jax import lax
from jax.experimental import pallas as pl
from jax.experimental.pallas import tpu as pltpu
from jax.sharding import PartitionSpec as P

MESH = pl.DeviceIdType.MESH
F32, BF16 = jnp.float32, jnp.bfloat16

WIN = 256
BLOCK = 128
SUB = 8
LOCAL_ROWS = 384
LOCAL_TOKENS = 512
FEATURES = 1536
REST = 6112
HALF = 3072
N_ROW = 32
N_TOK = 8
CHIPS = 16
TOKENS = LOCAL_TOKENS * N_TOK

PHASES = 1
PHASE_COLS = HALF // PHASES
PIECE = PHASE_COLS // 2
STEP = 512

Z_UP, Z_DOWN, Z_UP_PIECE, Z_DOWN_PIECE = 0, 1, 2, 3
X_FIRST = 4
PAIR_FIRST = 20
F_MESSAGES = 20


def prune_prepare(ww, kp, fw, cur, scaled_drop, fw_t):
    factor = fw[...]
    fw_t[...] = factor.T
    row_id = lax.broadcasted_iota(jnp.int32, (WIN, WIN), 0)
    col_id = lax.broadcasted_iota(jnp.int32, (WIN, WIN), 1)
    diagonal = jnp.sum(jnp.where(row_id == col_id, factor, 0.0), axis=1, keepdims=True)
    drop = (1 - kp[...]).astype(F32).T
    scaled_drop[...] = drop * (1.0 / diagonal)
    cur[...] = ww[...].T


def prune_tile(k, cur, scaled_drop, fw_t, fw_s, err, err_blocks):
    low = k * SUB
    block_end = (low // BLOCK + 1) * BLOCK
    shape = (SUB, LOCAL_ROWS)
    tile = cur[low : low + SUB, :]
    drop = scaled_drop[low : low + SUB, :]
    place = lax.broadcasted_iota(jnp.int32, shape, 0)
    values = [jnp.broadcast_to(tile[s : s + 1, :], shape) for s in range(SUB)]
    errors = []
    tile_err = jnp.zeros(shape, F32)
    tile_out = jnp.zeros(shape, F32)
    for s in range(SUB):
        e = values[s] * jnp.broadcast_to(drop[s : s + 1, :], shape)
        for t in range(s + 1, SUB):
            values[t] = values[t] - fw_s[low + s, low + t] * e
        errors.append(e)
        tile_err = jnp.where(place == s, e, tile_err)
        tile_out = jnp.where(place == s, values[s] - fw_s[low + s, low + s] * e, tile_out)
    cur[low : low + SUB, :] = tile_out
    err[low : low + SUB, :] = tile_err
    at = ((k % 2) * CHIPS + k // 2) * SUB
    err_blocks[at : at + SUB, :] = tile_err
    start = low + SUB
    while start < block_end:
        end = min(start + 32, block_end)
        n = (end - start) // SUB
        part = cur[start:end, :].reshape(n, SUB, LOCAL_ROWS)
        for s in range(SUB):
            part = part - fw_t[start:end, low + s : low + s + 1].reshape(n, SUB, 1) * errors[s][None]
        cur[start:end, :] = part.reshape(n * SUB, LOCAL_ROWS)
        start = end
    if block_end == low + SUB and block_end < WIN:
        b = block_end - BLOCK
        cur[block_end:, :] = cur[block_end:, :] - jnp.dot(
            fw_t[block_end:, b:block_end], err[b:block_end, :],
            precision=lax.Precision.HIGHEST, preferred_element_type=F32,
        )


def compensate(rest, blocks, half, err_half):
    factor = blocks[:, half * 8 : half * 8 + 8, :].reshape(WIN, blocks.shape[2])
    change = lax.dot_general(
        factor, err_half, (((0,), (0,)), ((), ())), preferred_element_type=F32
    )
    return (rest.astype(F32) - change[: rest.shape[0]]).astype(BF16)


def kernel(
    ids_hbm, calib_hbm, keep_hbm, ww_hbm, rest_hbm, fw_hbm, fr_hbm,
    pruned_out, rest_out, hess_out, outs_out, fac, err_half,
    ids, cal, kp, ww, fw, fw_s, fr, fr_block, xin, x_t, cur, scaled_drop, err, err_blocks, fw_t, x_half, local_outs, z_relay,
    gram, gram_half, relay_in, relay_out, from_left, from_right, peer_out, peer_in,
    load_sem, f_send, f_recv, pair_recv, scat_send, scat_recv, xz_send, xz_recv, xx_send, xx_recv, xp_sem,
    o_send, o_recv, relay_recv, h_send, h_recv,
):
    tok, row = lax.axis_index("tok"), lax.axis_index("row")
    x, h, c = row // 8, (row // 2) % 4, row % 2
    l, y = tok // 4, tok % 4
    chip = x * 4 + h

    def row_of(px, ph, pc):
        return ((px + 4) % 4) * 8 + ((ph + 4) % 4) * 2 + pc

    def remote(src, dst, ssem, rsem, to_row=None, to_tok=None):
        return pltpu.make_async_remote_copy(
            src_ref=src, dst_ref=dst, send_sem=ssem, recv_sem=rsem,
            device_id=(tok if to_tok is None else to_tok, row if to_row is None else to_row),
            device_id_type=MESH,
        )

    loads = [
        pltpu.make_async_copy(s, d, load_sem.at[i])
        for i, (s, d) in enumerate(
            [(fr_hbm, fr), (calib_hbm, cal), (ww_hbm, ww), (keep_hbm, kp), (fw_hbm, fw), (ids_hbm, ids), (rest_hbm, rest_out), (fw_hbm, fw_s)]
        )
    ]
    for load in loads[:6] + loads[7:]:
        load.start()

    barrier = pltpu.get_barrier_semaphore()

    def greet(d, carry):
        pl.semaphore_signal(barrier, inc=1, device_id=(tok, (row + d) % N_ROW), device_id_type=MESH)
        return carry

    lax.fori_loop(1, N_ROW, greet, 0)
    up_tok, down_tok, other_tok = l * 4 + (y + 1) % 4, l * 4 + (y + 3) % 4, (1 - l) * 4 + y
    for peer in (up_tok, down_tok, other_tok):
        pl.semaphore_signal(barrier, inc=1, device_id=(peer, row), device_id_type=MESH)
    pl.semaphore_wait(barrier, N_ROW - 1 + 3)

    is_source = row == 0

    def scatter(r):
        first = pl.multiple_of((r % 2) * 256 + (r // 2) * 16, 16)
        return remote(
            cal.at[pl.ds(first, 16), pl.ds(0, WIN)], xin.at[r % 2, r // 2], scat_send.at[r], scat_recv.at[0], to_row=r
        )

    loads[0].wait()
    fr_block[0:8, :] = fr[:, 0:HALF]
    fr_block[8:16, HALF - 128 :] = jnp.zeros((8, 128), F32)
    fr_block[8:16, 0 : REST - HALF] = fr[:, HALF:REST]
    fac[c * CHIPS + chip] = fr_block[...].astype(BF16)

    def f_copy(p, number, slot, to_row, piece=None):
        first, size = p * PHASE_COLS, PHASE_COLS
        if piece is not None:
            first, size = first + piece * PIECE, PIECE
        ref = fac.at[c * CHIPS + slot, :, pl.ds(first, size)]
        rsem = pair_recv.at[p] if number >= PAIR_FIRST else f_recv.at[p, number]
        return remote(ref, ref, f_send.at[0], rsem, to_row=to_row)

    x_up, x_down = row_of(x + 1, h, c), row_of(x - 1, h, c)
    z_up, z_down = row_of(x, h + 1, c), row_of(x, h - 1, c)
    pair = row_of(x, h, 1 - c)
    z_slots = [h, (h + 3) % 4, (h + 1) % 4, (h + 2) % 4]
    x_slots = [x, (x + 3) % 4, (x + 1) % 4, (x + 2) % 4]

    def f_start(*args, **kw):
        f_copy(*args, **kw).start()

    def f_from_z(p, j):
        slot = x * 4 + z_slots[j]
        if j == 1:
            f_start(p, Z_UP_PIECE, slot, z_up, piece=0)
        if j == 2:
            f_start(p, Z_DOWN_PIECE, slot, z_down, piece=1)
        f_start(p, X_FIRST + 4 * j, slot, x_up)
        f_start(p, X_FIRST + 4 * j + 1, slot, x_down)
        f_start(p, PAIR_FIRST + j, slot, pair)

    def f_own(p):
        f_start(p, Z_UP, chip, z_up)
        f_start(p, Z_DOWN, chip, z_down)
        f_from_z(p, 0)

    def f_z_neighbours(p):
        f_copy(p, Z_UP, x * 4 + z_slots[1], z_up).wait_recv()
        f_from_z(p, 1)
        f_copy(p, Z_DOWN, x * 4 + z_slots[2], z_down).wait_recv()
        f_from_z(p, 2)

    def f_z_opposite(p):
        slot = x * 4 + z_slots[3]
        f_copy(p, Z_UP_PIECE, slot, z_up, piece=0).wait_recv()
        f_copy(p, Z_DOWN_PIECE, slot, z_down, piece=1).wait_recv()
        f_from_z(p, 3)

    def f_x_neighbours(p, j):
        n = X_FIRST + 4 * j
        slot = x_slots[1] * 4 + z_slots[j]
        f_copy(p, n, slot, x_up).wait_recv()
        f_start(p, n + 2, slot, x_up, piece=0)
        f_start(p, PAIR_FIRST + 4 + j, slot, pair)
        slot = x_slots[2] * 4 + z_slots[j]
        f_copy(p, n + 1, slot, x_down).wait_recv()
        f_start(p, n + 3, slot, x_down, piece=1)
        f_start(p, PAIR_FIRST + 8 + j, slot, pair)

    def f_x_opposite(p, j):
        n = X_FIRST + 4 * j
        slot = x_slots[3] * 4 + z_slots[j]
        f_copy(p, n + 2, slot, x_up, piece=0).wait_recv()
        f_copy(p, n + 3, slot, x_down, piece=1).wait_recv()
        f_start(p, PAIR_FIRST + 12 + j, slot, pair)

    def f_pair_wait(p):
        ref = fac.at[pl.ds((1 - c) * CHIPS, CHIPS), :, pl.ds(p * PHASE_COLS, PHASE_COLS)]
        remote(ref, ref, f_send.at[0], pair_recv.at[p], to_row=pair).wait_recv()

    def xz_copy(d):
        ref = xin.at[c, chip]
        return remote(ref, ref, xz_send.at[d], xz_recv.at[d], to_row=row_of(x, h + d, c))

    def xx_copy(d):
        ref = xin.at[c, pl.ds(x * 4, 4)]
        return remote(ref, ref, xx_send.at[d], xx_recv.at[d], to_row=row_of(x + d, h, c))

    xp_copy = remote(xin.at[c], xin.at[c], xp_sem.at[0], xp_sem.at[1], to_row=pair)

    def inputs_along_z():
        @pl.when(jnp.logical_not(is_source))
        def _():
            ref = xin.at[c, chip]
            remote(ref, ref, scat_send.at[0], scat_recv.at[0], to_row=pair).wait_recv()

        for d in (1, 3, 2):
            xz_copy(d).start()

    def inputs_along_x():
        for d in (1, 3, 2):
            ref = xin.at[c, x * 4 + (h + 4 - d) % 4]
            remote(ref, ref, xz_send.at[d], xz_recv.at[d], to_row=row_of(x, h + d, c)).wait_recv()
        for d in (1, 3, 2):
            xx_copy(d).start()

    def inputs_to_pair():
        for d in (1, 3, 2):
            ref = xin.at[c, pl.ds(((x + 4 - d) % 4) * 4, 4)]
            remote(ref, ref, xx_send.at[d], xx_recv.at[d], to_row=row_of(x + d, h, c)).wait_recv()
        xp_copy.start()

    def inputs_complete():
        remote(xin.at[1 - c], xin.at[1 - c], xp_sem.at[0], xp_sem.at[1], to_row=pair).wait_recv()
        loads[5].wait()
        live = jnp.where(ids[...] != 1, 1.0, 0.0)
        live_t = jnp.concatenate([live, jnp.zeros((4, 128), F32)], axis=0).T
        x_parts = []
        for s in range(4):
            part = xin[s // 2, (s % 2) * 8 : (s % 2) * 8 + 8].reshape(128, WIN).astype(F32)
            x_parts.append(part * live_t[:, s : s + 1])
        x_all = jnp.concatenate(x_parts, axis=0)
        x_t[...] = x_all.T.astype(BF16)
        x_half[...] = x_all.astype(BF16)

    def h_copy(number, src, dst, to_tok):
        return remote(src, dst, h_send.at[number], h_recv.at[number], to_tok=to_tok)

    h_copies = [
        h_copy(0, gram_half.at[(y + 2) % 4], relay_in.at[0], up_tok),
        h_copy(1, gram_half.at[4 + (y + 2) % 4], relay_in.at[1], down_tok),
        h_copy(2, gram_half.at[4 + (y + 1) % 4], from_left.at[1], up_tok),
        h_copy(3, gram_half.at[(y + 3) % 4], from_right.at[0], down_tok),
        h_copy(4, relay_out.at[0], from_left.at[0], up_tok),
        h_copy(5, relay_out.at[1], from_right.at[1], down_tok),
        h_copy(6, peer_out, peer_in, other_tok),
    ]

    def hessian_begin():
        @pl.loop(0, FEATURES // 256)
        def _(i):
            cols = pl.ds(pl.multiple_of(i * 256, 256), 256)
            part = jnp.dot(x_t[...], cal[:, cols], preferred_element_type=F32).reshape(N_TOK, 32, 256)
            gram[:, :, cols] = part
            gram_half[:, :, cols] = part.astype(BF16)

        for i in range(4):
            h_copies[i].start()

    def hessian_relay():
        h_copies[0].wait_recv()
        relay_out[0] = (relay_in[0].astype(F32) + gram[(y + 1) % 4]).astype(BF16)
        h_copies[4].start()
        h_copies[1].wait_recv()
        relay_out[1] = (relay_in[1].astype(F32) + gram[4 + (y + 3) % 4]).astype(BF16)
        h_copies[5].start()

    def hessian_peer():
        for i in range(2, 6):
            h_copies[i].wait_recv()
        peer_out[...] = (
            gram[(1 - l) * 4 + y] + from_left[1 - l].astype(F32) + from_right[1 - l].astype(F32)
        ).astype(BF16)
        h_copies[6].start()

    def hessian_end():
        h_copies[6].wait_recv()
        total = gram[l * 4 + y] + from_left[l].astype(F32) + from_right[l].astype(F32) + peer_in[...].astype(F32)
        hess_out[...] = total * (2.0 / TOKENS)

    def out_cols(sender):
        return pl.ds(pl.multiple_of(sender * LOCAL_ROWS, 128), LOCAL_ROWS)

    my_cols = out_cols(row)
    opposite = (h + 2) % 4
    relays = [
        remote(local_outs.at[:, opposite, 0], z_relay.at[0], o_send.at[0], relay_recv.at[0], to_row=z_up),
        remote(local_outs.at[:, opposite, 1], z_relay.at[1], o_send.at[0], relay_recv.at[1], to_row=z_down),
    ]

    def send_outputs():
        local_outs[...] = jnp.dot(
            x_half[...], cur[...].astype(BF16), preferred_element_type=F32
        ).astype(BF16).reshape(4, 4, 2, 16, LOCAL_ROWS)
        for relay in relays:
            relay.start()
        for dx in (2, 1, 3, 0):
            for dh in (1, 3, 0):
                for dc in (0, 1):
                    if (dx, dh, dc) != (0, 0, 0):
                        ox, oh, oc = (x + dx) % 4, (h + dh) % 4, (c + dc) % 2
                        remote(
                            local_outs.at[ox, oh, oc], outs_out.at[:, my_cols], o_send.at[0], o_recv.at[0],
                            to_row=row_of(ox, oh, oc),
                        ).start()

    def pass_on_z(way):
        relays[way].wait_recv()
        sender = row_of(x, h + (3 if way == 0 else 1), c)
        for px in range(4):
            remote(
                z_relay.at[way, px], outs_out.at[:, out_cols(sender)], o_send.at[1], o_recv.at[0],
                to_row=row_of(px, h + (1 if way == 0 else 3), way),
            ).start()

    arrived = outs_out.at[:, pl.ds(0, (N_ROW - 1) * LOCAL_ROWS)]

    def outputs_complete():
        remote(arrived, arrived, o_send.at[0], o_recv.at[0], to_row=pair).wait_recv()

    def prune(first, last):
        for k in range(first, last):
            prune_tile(k, cur, scaled_drop, fw_t, fw_s, err, err_blocks)

    def pruned_results():
        outs_out[:, my_cols] = local_outs[x, h, c]
        pruned_out[...] = cur[...].T
        err_half[...] = err_blocks[...].astype(BF16)

    def update(p):
        for half in range(2):

            @pl.loop(0, PHASE_COLS // STEP)
            def _(i, half=half, p=p):
                first = pl.multiple_of(p * PHASE_COLS + i * STEP, STEP)
                rows = pl.ds(pl.multiple_of(half * HALF + first, STEP), STEP)
                rest_out[rows, :] = compensate(rest_out[rows, :], fac[:, :, pl.ds(first, STEP)], half, err_half[...])

    f_own(0)
    loads[6].start()
    loads[1].wait()

    @pl.when(is_source)
    def _():
        def send(r, carry):
            scatter(r).start()
            return carry

        lax.fori_loop(1, N_ROW, send, 0)
        xin[0, 0] = cal[0:16, 0:WIN]

    for i in (2, 3, 4, 7):
        loads[i].wait()
    prune_prepare(ww, kp, fw, cur, scaled_drop, fw_t)
    prune(0, 4)
    inputs_along_z()
    prune(4, 12)
    f_x_neighbours(0, 0)
    prune(12, 16)
    inputs_along_x()
    prune(16, 24)
    f_z_neighbours(0)
    prune(24, 28)
    inputs_to_pair()
    prune(28, 32)
    inputs_complete()
    send_outputs()
    hessian_begin()
    f_z_opposite(0)
    f_x_neighbours(0, 2)
    f_x_neighbours(0, 1)
    hessian_relay()
    pass_on_z(1)
    pass_on_z(0)
    f_x_neighbours(0, 3)
    f_x_opposite(0, 0)
    pruned_results()
    hessian_peer()
    f_x_opposite(0, 2)
    f_x_opposite(0, 1)
    f_x_opposite(0, 3)
    loads[6].wait()
    outputs_complete()
    hessian_end()
    f_pair_wait(0)

    remote(arrived, arrived, o_send.at[0], o_recv.at[0], to_row=pair).wait_send()
    remote(z_relay, z_relay, o_send.at[1], o_recv.at[0], to_row=pair).wait_send()

    @pl.when(is_source)
    def _():
        def left(r, carry):
            scatter(r).wait_send()
            return carry

        lax.fori_loop(1, N_ROW, left, 0)

    for d in (1, 3, 2):
        xz_copy(d).wait_send()
        xx_copy(d).wait_send()
    xp_copy.wait_send()
    for copy in h_copies:
        copy.wait_send()
    sent = fac.at[pl.ds(0, 31)]
    remote(sent, sent, f_send.at[0], pair_recv.at[0], to_row=pair).wait_send()


def finish_kernel(
    pruned, rest, hess, outs, fac, err_half,
    pruned_hbm, rest_hbm, hess_hbm, outs_hbm,
    updated, sem,
):
    copies = [
        pltpu.make_async_copy(pruned, pruned_hbm, sem.at[0]),
        pltpu.make_async_copy(hess, hess_hbm, sem.at[1]),
        pltpu.make_async_copy(outs, outs_hbm, sem.at[2]),
    ]
    last = HALF - PHASE_COLS
    if last > 0:
        for half in range(2):
            rows = pl.ds(half * HALF, last)
            copies.append(pltpu.make_async_copy(rest.at[rows], rest_hbm.at[rows], sem.at[3 + half]))
    for copy in copies:
        copy.start()
    for half in range(2):
        for i in range(PHASE_COLS // STEP):
            first = last + i * STEP
            start = half * HALF + first
            count = min(STEP, REST - start)
            part = rest[start : start + count, :]
            at = half * PHASE_COLS + i * STEP
            updated[at : at + count, :] = compensate(part, fac[:, :, first : first + STEP], half, err_half[...])
            copy = pltpu.make_async_copy(
                updated.at[pl.ds(at, count)], rest_hbm.at[pl.ds(start, count)], sem.at[5 + half * (PHASE_COLS // STEP) + i]
            )
            copy.start()
            copies.append(copy)
    for copy in copies:
        copy.wait()


def on_device(token_ids, calib_input, keep_mask, weight_window, weight_rest, factor_window, factor_rest):
    vmem, dma = pltpu.VMEM, pltpu.SemaphoreType.DMA
    slab = (32, FEATURES)
    in_hbm = [
        pltpu.with_memory_space_constraint(a, pltpu.HBM)
        for a in (
            token_ids.reshape(4, 128), calib_input, keep_mask, weight_window, weight_rest.T, factor_window, factor_rest
        )
    ]
    shapes = [
        ((LOCAL_ROWS, WIN), F32),
        ((REST, LOCAL_ROWS), BF16),
        (slab, F32),
        ((16, N_ROW * LOCAL_ROWS), BF16),
    ]
    held = pl.pallas_call(
        kernel,
        out_shape=tuple(
            vmem(*s) for s in shapes + [((2 * CHIPS, 16, HALF), BF16), ((WIN, LOCAL_ROWS), BF16)]
        ),
        in_specs=[pl.BlockSpec(memory_space=pltpu.HBM)] * 7,
        out_specs=[pl.BlockSpec(memory_space=vmem)] * 6,
        scratch_shapes=[
            vmem((4, 128), jnp.int32),
            vmem((LOCAL_TOKENS, FEATURES), BF16),
            vmem((LOCAL_ROWS, WIN), jnp.int32),
            vmem((LOCAL_ROWS, WIN), F32),
            vmem((WIN, WIN), F32),
            pltpu.SMEM((WIN, WIN), F32),
            vmem((8, REST), F32),
            vmem((16, HALF), F32),
            vmem((2, CHIPS, 16, WIN), BF16),
            vmem((WIN, LOCAL_TOKENS), BF16),
            vmem((WIN, LOCAL_ROWS), F32),
            vmem((WIN, LOCAL_ROWS), F32),
            vmem((WIN, LOCAL_ROWS), F32),
            vmem((WIN, LOCAL_ROWS), F32),
            vmem((WIN, WIN), F32),
            vmem((LOCAL_TOKENS, WIN), BF16),
            vmem((4, 4, 2, 16, LOCAL_ROWS), BF16),
            vmem((2, 4, 16, LOCAL_ROWS), BF16),
            vmem((N_TOK,) + slab, F32),
            vmem((N_TOK,) + slab, BF16),
            vmem((2,) + slab, BF16),
            vmem((2,) + slab, BF16),
            vmem((2,) + slab, BF16),
            vmem((2,) + slab, BF16),
            vmem(slab, BF16),
            vmem(slab, BF16),
            dma((8,)),
            dma((1,)),
            dma((PHASES, F_MESSAGES)),
            dma((PHASES,)),
            dma((N_ROW,)),
            dma((1,)),
            dma((4,)),
            dma((4,)),
            dma((4,)),
            dma((4,)),
            dma((2,)),
            dma((2,)),
            dma((1,)),
            dma((2,)),
            dma((7,)),
            dma((7,)),
        ],
        compiler_params=pltpu.CompilerParams(
            collective_id=0, has_side_effects=True, vmem_limit_bytes=32 * 1024 * 1024
        ),
        cost_estimate=pl.CostEstimate(flops=2_000_000_000, bytes_accessed=16_000_000, transcendentals=0),
    )(*in_hbm)
    pruned, rest_t, hess, outs = pl.pallas_call(
        finish_kernel,
        out_shape=tuple(jax.ShapeDtypeStruct(*s) for s in shapes),
        in_specs=[pl.BlockSpec(memory_space=vmem)] * 6,
        out_specs=[pl.BlockSpec(memory_space=pltpu.HBM)] * 4,
        scratch_shapes=[
            vmem((2 * PHASE_COLS, LOCAL_ROWS), BF16),
            dma((5 + 2 * (PHASE_COLS // STEP),)),
        ],
        compiler_params=pltpu.CompilerParams(vmem_limit_bytes=32 * 1024 * 1024),
        cost_estimate=pl.CostEstimate(flops=600_000_000, bytes_accessed=12_000_000, transcendentals=0),
    )(*[pltpu.with_memory_space_constraint(a, vmem) for a in held])
    return pruned, rest_t.T, hess, outs


def solution(mesh):
    return jax.shard_map(
        on_device,
        mesh=mesh,
        in_specs=(
            P("tok"),
            P("tok", "row"),
            P("row", None),
            P("row", None),
            P("row", "tok"),
            P(),
            P("row", "tok"),
        ),
        out_specs=(P("row", None), P("row", "tok"), P("tok", "row"), P(("tok", "row"), None)),
        check_vma=False,
    )
```

```python
import jax
import jax.numpy as jnp
from jax import lax
from jax.experimental import pallas as pl
from jax.experimental.pallas import tpu as pltpu
from jax.sharding import PartitionSpec as P

MESH = pl.DeviceIdType.MESH
F32, BF16 = jnp.float32, jnp.bfloat16

WIN = 256
BLOCK = 128
SUB = 8
LOCAL_ROWS = 384
LOCAL_TOKENS = 512
FEATURES = 1536
REST = 6112
HALF = 3072
N_ROW = 32
N_TOK = 8
CHIPS = 16
TOKENS = LOCAL_TOKENS * N_TOK

PHASES = 1
PHASE_COLS = HALF // PHASES
PIECE = PHASE_COLS // 2
STEP = 512

Z_UP, Z_DOWN, Z_UP_PIECE, Z_DOWN_PIECE = 0, 1, 2, 3
X_FIRST = 4
PAIR_FIRST = 20
F_MESSAGES = 20


def prune_prepare(ww, kp, fw, cur, scaled_drop, fw_t):
    factor = fw[...]
    fw_t[...] = factor.T
    row_id = lax.broadcasted_iota(jnp.int32, (WIN, WIN), 0)
    col_id = lax.broadcasted_iota(jnp.int32, (WIN, WIN), 1)
    diagonal = jnp.sum(jnp.where(row_id == col_id, factor, 0.0), axis=1, keepdims=True)
    drop = (1 - kp[...]).astype(F32).T
    scaled_drop[...] = drop * (1.0 / diagonal)
    cur[...] = ww[...].T


def prune_tile(k, cur, scaled_drop, fw_t, fw_s, err, err_blocks):
    low = k * SUB
    block_end = (low // BLOCK + 1) * BLOCK
    shape = (SUB, LOCAL_ROWS)
    tile = cur[low : low + SUB, :]
    drop = scaled_drop[low : low + SUB, :]
    place = lax.broadcasted_iota(jnp.int32, shape, 0)
    values = [jnp.broadcast_to(tile[s : s + 1, :], shape) for s in range(SUB)]
    errors = []
    tile_err = jnp.zeros(shape, F32)
    tile_out = jnp.zeros(shape, F32)
    for s in range(SUB):
        e = values[s] * jnp.broadcast_to(drop[s : s + 1, :], shape)
        for t in range(s + 1, SUB):
            values[t] = values[t] - fw_s[low + s, low + t] * e
        errors.append(e)
        tile_err = jnp.where(place == s, e, tile_err)
        tile_out = jnp.where(place == s, values[s] - fw_s[low + s, low + s] * e, tile_out)
    cur[low : low + SUB, :] = tile_out
    err[low : low + SUB, :] = tile_err
    at = ((k % 2) * CHIPS + k // 2) * SUB
    err_blocks[at : at + SUB, :] = tile_err
    start = low + SUB
    while start < block_end:
        end = min(start + 32, block_end)
        n = (end - start) // SUB
        part = cur[start:end, :].reshape(n, SUB, LOCAL_ROWS)
        for s in range(SUB):
            part = part - fw_t[start:end, low + s : low + s + 1].reshape(n, SUB, 1) * errors[s][None]
        cur[start:end, :] = part.reshape(n * SUB, LOCAL_ROWS)
        start = end
    if block_end == low + SUB and block_end < WIN:
        b = block_end - BLOCK
        cur[block_end:, :] = cur[block_end:, :] - jnp.dot(
            fw_t[block_end:, b:block_end], err[b:block_end, :],
            precision=lax.Precision.HIGHEST, preferred_element_type=F32,
        )


def compensate(rest, blocks, half, err_half):
    factor = blocks[:, half * 8 : half * 8 + 8, :].reshape(WIN, blocks.shape[2])
    change = lax.dot_general(
        factor, err_half, (((0,), (0,)), ((), ())), preferred_element_type=F32
    )
    return (rest.astype(F32) - change[: rest.shape[0]]).astype(BF16)


def kernel(
    ids_hbm, calib_hbm, keep_hbm, ww_hbm, rest_hbm, fw_hbm, fr_hbm,
    pruned_out, rest_out, hess_out, outs_out, fac, err_half,
    ids, cal, kp, ww, fw, fw_s, fr, fr_block, xin, x_t, cur, scaled_drop, err, err_blocks, fw_t, x_half, local_outs, z_relay, x_relay,
    gram, gram_half, relay_in, relay_out, from_left, from_right, peer_out, peer_in,
    load_sem, f_send, f_recv, pair_recv, scat_send, scat_recv, xz_send, xz_recv, xx_send, xx_recv, xp_sem,
    o_send, o_recv, relay_recv, h_send, h_recv,
):
    tok, row = lax.axis_index("tok"), lax.axis_index("row")
    x, h, c = row // 8, (row // 2) % 4, row % 2
    l, y = tok // 4, tok % 4
    chip = x * 4 + h

    def row_of(px, ph, pc):
        return ((px + 4) % 4) * 8 + ((ph + 4) % 4) * 2 + pc

    def remote(src, dst, ssem, rsem, to_row=None, to_tok=None):
        return pltpu.make_async_remote_copy(
            src_ref=src, dst_ref=dst, send_sem=ssem, recv_sem=rsem,
            device_id=(tok if to_tok is None else to_tok, row if to_row is None else to_row),
            device_id_type=MESH,
        )

    loads = [
        pltpu.make_async_copy(s, d, load_sem.at[i])
        for i, (s, d) in enumerate(
            [(fr_hbm, fr), (calib_hbm, cal), (ww_hbm, ww), (keep_hbm, kp), (fw_hbm, fw), (ids_hbm, ids), (rest_hbm, rest_out), (fw_hbm, fw_s)]
        )
    ]
    for load in loads[:6] + loads[7:]:
        load.start()

    barrier = pltpu.get_barrier_semaphore()

    def greet(d, carry):
        pl.semaphore_signal(barrier, inc=1, device_id=(tok, (row + d) % N_ROW), device_id_type=MESH)
        return carry

    lax.fori_loop(1, N_ROW, greet, 0)
    up_tok, down_tok, other_tok = l * 4 + (y + 1) % 4, l * 4 + (y + 3) % 4, (1 - l) * 4 + y
    for peer in (up_tok, down_tok, other_tok):
        pl.semaphore_signal(barrier, inc=1, device_id=(peer, row), device_id_type=MESH)
    pl.semaphore_wait(barrier, N_ROW - 1 + 3)

    is_source = row == 0

    def scatter(r):
        first = pl.multiple_of((r % 2) * 256 + (r // 2) * 16, 16)
        return remote(
            cal.at[pl.ds(first, 16), pl.ds(0, WIN)], xin.at[r % 2, r // 2], scat_send.at[r], scat_recv.at[0], to_row=r
        )

    loads[0].wait()
    fr_block[0:8, :] = fr[:, 0:HALF]
    fr_block[8:16, HALF - 128 :] = jnp.zeros((8, 128), F32)
    fr_block[8:16, 0 : REST - HALF] = fr[:, HALF:REST]
    fac[c * CHIPS + chip] = fr_block[...].astype(BF16)

    def f_copy(p, number, slot, to_row, piece=None):
        first, size = p * PHASE_COLS, PHASE_COLS
        if piece is not None:
            first, size = first + piece * PIECE, PIECE
        ref = fac.at[c * CHIPS + slot, :, pl.ds(first, size)]
        rsem = pair_recv.at[p] if number >= PAIR_FIRST else f_recv.at[p, number]
        return remote(ref, ref, f_send.at[0], rsem, to_row=to_row)

    x_up, x_down = row_of(x + 1, h, c), row_of(x - 1, h, c)
    z_up, z_down = row_of(x, h + 1, c), row_of(x, h - 1, c)
    pair = row_of(x, h, 1 - c)
    z_slots = [h, (h + 3) % 4, (h + 1) % 4, (h + 2) % 4]
    x_slots = [x, (x + 3) % 4, (x + 1) % 4, (x + 2) % 4]

    def f_start(*args, **kw):
        f_copy(*args, **kw).start()

    def f_from_z(p, j):
        slot = x * 4 + z_slots[j]
        if j == 1:
            f_start(p, Z_UP_PIECE, slot, z_up, piece=0)
        if j == 2:
            f_start(p, Z_DOWN_PIECE, slot, z_down, piece=1)
        f_start(p, X_FIRST + 4 * j, slot, x_up)
        f_start(p, X_FIRST + 4 * j + 1, slot, x_down)
        f_start(p, PAIR_FIRST + j, slot, pair)

    def f_own_along_z(p):
        f_start(p, Z_UP, chip, z_up)
        f_start(p, Z_DOWN, chip, z_down)

    def f_z_neighbours(p):
        f_copy(p, Z_UP, x * 4 + z_slots[1], z_up).wait_recv()
        f_from_z(p, 1)
        f_copy(p, Z_DOWN, x * 4 + z_slots[2], z_down).wait_recv()
        f_from_z(p, 2)

    def f_z_opposite(p):
        slot = x * 4 + z_slots[3]
        f_copy(p, Z_UP_PIECE, slot, z_up, piece=0).wait_recv()
        f_copy(p, Z_DOWN_PIECE, slot, z_down, piece=1).wait_recv()
        f_from_z(p, 3)

    def f_x_neighbours(p, j):
        n = X_FIRST + 4 * j
        slot = x_slots[1] * 4 + z_slots[j]
        f_copy(p, n, slot, x_up).wait_recv()
        f_start(p, n + 2, slot, x_up, piece=0)
        f_start(p, PAIR_FIRST + 4 + j, slot, pair)
        slot = x_slots[2] * 4 + z_slots[j]
        f_copy(p, n + 1, slot, x_down).wait_recv()
        f_start(p, n + 3, slot, x_down, piece=1)
        f_start(p, PAIR_FIRST + 8 + j, slot, pair)

    def f_x_opposite(p, j):
        n = X_FIRST + 4 * j
        slot = x_slots[3] * 4 + z_slots[j]
        f_copy(p, n + 2, slot, x_up, piece=0).wait_recv()
        f_copy(p, n + 3, slot, x_down, piece=1).wait_recv()
        f_start(p, PAIR_FIRST + 12 + j, slot, pair)

    def f_pair_wait(p):
        ref = fac.at[pl.ds((1 - c) * CHIPS, CHIPS), :, pl.ds(p * PHASE_COLS, PHASE_COLS)]
        remote(ref, ref, f_send.at[0], pair_recv.at[p], to_row=pair).wait_recv()

    loads[1].wait()

    @pl.when(is_source)
    def _():
        def send(r, carry):
            scatter(r).start()
            return carry

        lax.fori_loop(1, N_ROW, send, 0)
        xin[0, 0] = cal[0:16, 0:WIN]

    def xz_copy(d):
        ref = xin.at[c, chip]
        return remote(ref, ref, xz_send.at[d], xz_recv.at[d], to_row=row_of(x, h + d, c))

    def xx_copy(d):
        ref = xin.at[c, pl.ds(x * 4, 4)]
        return remote(ref, ref, xx_send.at[d], xx_recv.at[d], to_row=row_of(x + d, h, c))

    xp_copy = remote(xin.at[c], xin.at[c], xp_sem.at[0], xp_sem.at[1], to_row=pair)

    def inputs_along_z():
        @pl.when(jnp.logical_not(is_source))
        def _():
            ref = xin.at[c, chip]
            remote(ref, ref, scat_send.at[0], scat_recv.at[0], to_row=pair).wait_recv()

        for d in (1, 3, 2):
            xz_copy(d).start()

    def inputs_along_x():
        for d in (1, 3, 2):
            ref = xin.at[c, x * 4 + (h + 4 - d) % 4]
            remote(ref, ref, xz_send.at[d], xz_recv.at[d], to_row=row_of(x, h + d, c)).wait_recv()
        for d in (1, 3, 2):
            xx_copy(d).start()

    def inputs_to_pair():
        for d in (1, 3, 2):
            ref = xin.at[c, pl.ds(((x + 4 - d) % 4) * 4, 4)]
            remote(ref, ref, xx_send.at[d], xx_recv.at[d], to_row=row_of(x + d, h, c)).wait_recv()
        xp_copy.start()

    def inputs_complete():
        remote(xin.at[1 - c], xin.at[1 - c], xp_sem.at[0], xp_sem.at[1], to_row=pair).wait_recv()
        loads[5].wait()
        live = jnp.where(ids[...] != 1, 1.0, 0.0)
        live_t = jnp.concatenate([live, jnp.zeros((4, 128), F32)], axis=0).T
        x_parts = []
        for s in range(4):
            part = xin[s // 2, (s % 2) * 8 : (s % 2) * 8 + 8].reshape(128, WIN).astype(F32)
            x_parts.append(part * live_t[:, s : s + 1])
        x_all = jnp.concatenate(x_parts, axis=0)
        x_t[...] = x_all.T.astype(BF16)
        x_half[...] = x_all.astype(BF16)

    def h_copy(number, src, dst, to_tok):
        return remote(src, dst, h_send.at[number], h_recv.at[number], to_tok=to_tok)

    h_copies = [
        h_copy(0, gram_half.at[(y + 2) % 4], relay_in.at[0], up_tok),
        h_copy(1, gram_half.at[4 + (y + 2) % 4], relay_in.at[1], down_tok),
        h_copy(2, gram_half.at[4 + (y + 1) % 4], from_left.at[1], up_tok),
        h_copy(3, gram_half.at[(y + 3) % 4], from_right.at[0], down_tok),
        h_copy(4, relay_out.at[0], from_left.at[0], up_tok),
        h_copy(5, relay_out.at[1], from_right.at[1], down_tok),
        h_copy(6, peer_out, peer_in, other_tok),
    ]

    def hessian_begin():
        @pl.loop(0, FEATURES // 256)
        def _(i):
            cols = pl.ds(pl.multiple_of(i * 256, 256), 256)
            part = jnp.dot(x_t[...], cal[:, cols], preferred_element_type=F32).reshape(N_TOK, 32, 256)
            gram[:, :, cols] = part
            gram_half[:, :, cols] = part.astype(BF16)

        for i in range(4):
            h_copies[i].start()

    def hessian_relay():
        h_copies[0].wait_recv()
        relay_out[0] = (relay_in[0].astype(F32) + gram[(y + 1) % 4]).astype(BF16)
        h_copies[4].start()
        h_copies[1].wait_recv()
        relay_out[1] = (relay_in[1].astype(F32) + gram[4 + (y + 3) % 4]).astype(BF16)
        h_copies[5].start()

    def hessian_peer():
        for i in range(2, 6):
            h_copies[i].wait_recv()
        peer_out[...] = (
            gram[(1 - l) * 4 + y] + from_left[1 - l].astype(F32) + from_right[1 - l].astype(F32)
        ).astype(BF16)
        h_copies[6].start()

    def hessian_end():
        h_copies[6].wait_recv()
        total = gram[l * 4 + y] + from_left[l].astype(F32) + from_right[l].astype(F32) + peer_in[...].astype(F32)
        hess_out[...] = total * (2.0 / TOKENS)

    def out_cols(sender):
        return pl.ds(pl.multiple_of(sender * LOCAL_ROWS, 128), LOCAL_ROWS)

    my_cols = out_cols(row)
    relays = [
        remote(local_outs.at[:, 3, 0], z_relay.at[0], o_send.at[0], relay_recv.at[0], to_row=z_up),
        remote(local_outs.at[:, 3, 1], z_relay.at[1], o_send.at[0], relay_recv.at[1], to_row=z_down),
        remote(local_outs.at[2, pl.ds(0, 3), 0], x_relay.at[0], o_send.at[0], relay_recv.at[2], to_row=x_up),
        remote(local_outs.at[2, pl.ds(0, 3), 1], x_relay.at[1], o_send.at[0], relay_recv.at[3], to_row=x_down),
    ]

    def send_outputs():
        found = jnp.dot(
            x_half[...], cur[...].astype(BF16), preferred_element_type=F32
        ).astype(BF16).reshape(N_ROW, 16, LOCAL_ROWS)
        for r in range(N_ROW):
            local_outs[(r // 8 - x + 4) % 4, ((r // 2) % 4 - h + 5) % 4, r % 2] = found[r]
        for relay in relays:
            relay.start()
        for dx in (1, 3, 0):
            for dh in (1, -1, 0):
                for dc in (0, 1):
                    if (dx, dh, dc) != (0, 0, 0):
                        oc = (c + dc) % 2
                        remote(
                            local_outs.at[dx, dh + 1, oc], outs_out.at[:, my_cols], o_send.at[0], o_recv.at[0],
                            to_row=row_of(x + dx, h + dh, oc),
                        ).start()

    def pass_on_z(way):
        relays[way].wait_recv()
        step = 1 if way == 0 else -1
        sender = row_of(x, h - step, c)
        for dx in range(4):
            remote(
                z_relay.at[way, dx], outs_out.at[:, out_cols(sender)], o_send.at[1], o_recv.at[0],
                to_row=row_of(x + dx, h + step, way),
            ).start()

    def pass_on_x(way):
        relays[2 + way].wait_recv()
        step = 1 if way == 0 else -1
        sender = row_of(x - step, h, c)
        for dh in (-1, 0, 1):
            remote(
                x_relay.at[way, dh + 1], outs_out.at[:, out_cols(sender)], o_send.at[2], o_recv.at[0],
                to_row=row_of(x + step, h + dh, way),
            ).start()

    arrived = outs_out.at[:, pl.ds(0, (N_ROW - 1) * LOCAL_ROWS)]

    def outputs_complete():
        remote(arrived, arrived, o_send.at[0], o_recv.at[0], to_row=pair).wait_recv()

    def prune(first, last):
        for k in range(first, last):
            prune_tile(k, cur, scaled_drop, fw_t, fw_s, err, err_blocks)

    def pruned_results():
        outs_out[:, my_cols] = local_outs[0, 1, c]
        pruned_out[...] = cur[...].T
        err_half[...] = err_blocks[...].astype(BF16)

    def update(p):
        for half in range(2):

            @pl.loop(0, PHASE_COLS // STEP)
            def _(i, half=half, p=p):
                first = pl.multiple_of(p * PHASE_COLS + i * STEP, STEP)
                rows = pl.ds(pl.multiple_of(half * HALF + first, STEP), STEP)
                rest_out[rows, :] = compensate(rest_out[rows, :], fac[:, :, pl.ds(first, STEP)], half, err_half[...])

    f_from_z(0, 0)
    loads[6].start()
    for i in (2, 3, 4, 7):
        loads[i].wait()
    prune_prepare(ww, kp, fw, cur, scaled_drop, fw_t)
    prune(0, 4)
    inputs_along_z()
    f_own_along_z(0)
    prune(4, 12)
    inputs_along_x()
    f_x_neighbours(0, 0)
    prune(12, 24)
    inputs_to_pair()
    prune(24, 32)
    f_z_neighbours(0)
    inputs_complete()
    send_outputs()
    hessian_begin()
    f_z_opposite(0)
    f_x_opposite(0, 0)
    f_x_neighbours(0, 1)
    pruned_results()
    pass_on_z(1)
    f_x_neighbours(0, 2)
    pass_on_z(0)
    hessian_relay()
    f_x_neighbours(0, 3)
    pass_on_x(1)
    pass_on_x(0)
    hessian_peer()
    f_x_opposite(0, 1)
    f_x_opposite(0, 2)
    f_x_opposite(0, 3)
    outputs_complete()
    hessian_end()
    f_pair_wait(0)
    loads[6].wait()

    remote(arrived, arrived, o_send.at[0], o_recv.at[0], to_row=pair).wait_send()
    remote(z_relay, z_relay, o_send.at[1], o_recv.at[0], to_row=pair).wait_send()
    remote(x_relay, x_relay, o_send.at[2], o_recv.at[0], to_row=pair).wait_send()

    @pl.when(is_source)
    def _():
        def left(r, carry):
            scatter(r).wait_send()
            return carry

        lax.fori_loop(1, N_ROW, left, 0)

    for d in (1, 3, 2):
        xz_copy(d).wait_send()
        xx_copy(d).wait_send()
    xp_copy.wait_send()
    for copy in h_copies:
        copy.wait_send()
    sent = fac.at[pl.ds(0, 31)]
    remote(sent, sent, f_send.at[0], pair_recv.at[0], to_row=pair).wait_send()


def finish_kernel(
    pruned, rest, hess, outs, fac, err_half,
    pruned_hbm, rest_hbm, hess_hbm, outs_hbm,
    updated, sem,
):
    copies = [
        pltpu.make_async_copy(pruned, pruned_hbm, sem.at[0]),
        pltpu.make_async_copy(hess, hess_hbm, sem.at[1]),
        pltpu.make_async_copy(outs, outs_hbm, sem.at[2]),
    ]
    last = HALF - PHASE_COLS
    if last > 0:
        for half in range(2):
            rows = pl.ds(half * HALF, last)
            copies.append(pltpu.make_async_copy(rest.at[rows], rest_hbm.at[rows], sem.at[3 + half]))
    for copy in copies:
        copy.start()
    for half in range(2):
        for i in range(PHASE_COLS // STEP):
            first = last + i * STEP
            start = half * HALF + first
            count = min(STEP, REST - start)
            part = rest[start : start + count, :]
            at = half * PHASE_COLS + i * STEP
            updated[at : at + count, :] = compensate(part, fac[:, :, first : first + STEP], half, err_half[...])
            copy = pltpu.make_async_copy(
                updated.at[pl.ds(at, count)], rest_hbm.at[pl.ds(start, count)], sem.at[5 + half * (PHASE_COLS // STEP) + i]
            )
            copy.start()
            copies.append(copy)
    for copy in copies:
        copy.wait()


def on_device(token_ids, calib_input, keep_mask, weight_window, weight_rest, factor_window, factor_rest):
    vmem, dma = pltpu.VMEM, pltpu.SemaphoreType.DMA
    slab = (32, FEATURES)
    in_hbm = [
        pltpu.with_memory_space_constraint(a, pltpu.HBM)
        for a in (
            token_ids.reshape(4, 128), calib_input, keep_mask, weight_window, weight_rest.T, factor_window, factor_rest
        )
    ]
    shapes = [
        ((LOCAL_ROWS, WIN), F32),
        ((REST, LOCAL_ROWS), BF16),
        (slab, F32),
        ((16, N_ROW * LOCAL_ROWS), BF16),
    ]
    held = pl.pallas_call(
        kernel,
        out_shape=tuple(
            vmem(*s) for s in shapes + [((2 * CHIPS, 16, HALF), BF16), ((WIN, LOCAL_ROWS), BF16)]
        ),
        in_specs=[pl.BlockSpec(memory_space=pltpu.HBM)] * 7,
        out_specs=[pl.BlockSpec(memory_space=vmem)] * 6,
        scratch_shapes=[
            vmem((4, 128), jnp.int32),
            vmem((LOCAL_TOKENS, FEATURES), BF16),
            vmem((LOCAL_ROWS, WIN), jnp.int32),
            vmem((LOCAL_ROWS, WIN), F32),
            vmem((WIN, WIN), F32),
            pltpu.SMEM((WIN, WIN), F32),
            vmem((8, REST), F32),
            vmem((16, HALF), F32),
            vmem((2, CHIPS, 16, WIN), BF16),
            vmem((WIN, LOCAL_TOKENS), BF16),
            vmem((WIN, LOCAL_ROWS), F32),
            vmem((WIN, LOCAL_ROWS), F32),
            vmem((WIN, LOCAL_ROWS), F32),
            vmem((WIN, LOCAL_ROWS), F32),
            vmem((WIN, WIN), F32),
            vmem((LOCAL_TOKENS, WIN), BF16),
            vmem((4, 4, 2, 16, LOCAL_ROWS), BF16),
            vmem((2, 4, 16, LOCAL_ROWS), BF16),
            vmem((2, 3, 16, LOCAL_ROWS), BF16),
            vmem((N_TOK,) + slab, F32),
            vmem((N_TOK,) + slab, BF16),
            vmem((2,) + slab, BF16),
            vmem((2,) + slab, BF16),
            vmem((2,) + slab, BF16),
            vmem((2,) + slab, BF16),
            vmem(slab, BF16),
            vmem(slab, BF16),
            dma((8,)),
            dma((1,)),
            dma((PHASES, F_MESSAGES)),
            dma((PHASES,)),
            dma((N_ROW,)),
            dma((1,)),
            dma((4,)),
            dma((4,)),
            dma((4,)),
            dma((4,)),
            dma((2,)),
            dma((3,)),
            dma((1,)),
            dma((4,)),
            dma((7,)),
            dma((7,)),
        ],
        compiler_params=pltpu.CompilerParams(
            collective_id=0, has_side_effects=True, vmem_limit_bytes=32 * 1024 * 1024
        ),
        cost_estimate=pl.CostEstimate(flops=2_000_000_000, bytes_accessed=16_000_000, transcendentals=0),
    )(*in_hbm)
    pruned, rest_t, hess, outs = pl.pallas_call(
        finish_kernel,
        out_shape=tuple(jax.ShapeDtypeStruct(*s) for s in shapes),
        in_specs=[pl.BlockSpec(memory_space=vmem)] * 6,
        out_specs=[pl.BlockSpec(memory_space=pltpu.HBM)] * 4,
        scratch_shapes=[
            vmem((2 * PHASE_COLS, LOCAL_ROWS), BF16),
            dma((5 + 2 * (PHASE_COLS // STEP),)),
        ],
        compiler_params=pltpu.CompilerParams(vmem_limit_bytes=32 * 1024 * 1024),
        cost_estimate=pl.CostEstimate(flops=600_000_000, bytes_accessed=12_000_000, transcendentals=0),
    )(*[pltpu.with_memory_space_constraint(a, vmem) for a in held])
    return pruned, rest_t.T, hess, outs


def solution(mesh):
    return jax.shard_map(
        on_device,
        mesh=mesh,
        in_specs=(
            P("tok"),
            P("tok", "row"),
            P("row", None),
            P("row", None),
            P("row", "tok"),
            P(),
            P("row", "tok"),
        ),
        out_specs=(P("row", None), P("row", "tok"), P("tok", "row"), P(("tok", "row"), None)),
        check_vma=False,
    )
```

```python
import jax
import jax.numpy as jnp
from jax import lax
from jax.experimental import pallas as pl
from jax.experimental.pallas import tpu as pltpu
from jax.sharding import PartitionSpec as P

MESH = pl.DeviceIdType.MESH
F32, BF16 = jnp.float32, jnp.bfloat16

WIN = 256
BLOCK = 128
SUB = 8
LOCAL_ROWS = 384
LOCAL_TOKENS = 512
FEATURES = 1536
REST = 6112
HALF = 3072
N_ROW = 32
N_TOK = 8
CHIPS = 16
TOKENS = LOCAL_TOKENS * N_TOK

PHASES = 1
PHASE_COLS = HALF // PHASES
PIECE = PHASE_COLS // 2
STEP = 512

Z_UP, Z_DOWN, Z_UP_PIECE, Z_DOWN_PIECE = 0, 1, 2, 3
X_FIRST = 4
PAIR_FIRST = 20
F_MESSAGES = 20


def prune_prepare(ww, kp, fw, cur, scaled_drop, fw_t):
    factor = fw[...]
    fw_t[...] = factor.T
    row_id = lax.broadcasted_iota(jnp.int32, (WIN, WIN), 0)
    col_id = lax.broadcasted_iota(jnp.int32, (WIN, WIN), 1)
    diagonal = jnp.sum(jnp.where(row_id == col_id, factor, 0.0), axis=1, keepdims=True)
    drop = (1 - kp[...]).astype(F32).T
    scaled_drop[...] = drop * (1.0 / diagonal)
    cur[...] = ww[...].T


def prune_tile(k, cur, scaled_drop, fw_t, fw_s, err, err_blocks):
    low = k * SUB
    block_end = (low // BLOCK + 1) * BLOCK
    shape = (SUB, LOCAL_ROWS)
    tile = cur[low : low + SUB, :]
    drop = scaled_drop[low : low + SUB, :]
    place = lax.broadcasted_iota(jnp.int32, shape, 0)
    values = [jnp.broadcast_to(tile[s : s + 1, :], shape) for s in range(SUB)]
    errors = []
    tile_err = jnp.zeros(shape, F32)
    tile_out = jnp.zeros(shape, F32)
    for s in range(SUB):
        e = values[s] * jnp.broadcast_to(drop[s : s + 1, :], shape)
        for t in range(s + 1, SUB):
            values[t] = values[t] - fw_s[low + s, low + t] * e
        errors.append(e)
        tile_err = jnp.where(place == s, e, tile_err)
        tile_out = jnp.where(place == s, values[s] - fw_s[low + s, low + s] * e, tile_out)
    cur[low : low + SUB, :] = tile_out
    err[low : low + SUB, :] = tile_err
    at = ((k % 2) * CHIPS + k // 2) * SUB
    err_blocks[at : at + SUB, :] = tile_err
    start = low + SUB
    while start < block_end:
        end = min(start + 32, block_end)
        n = (end - start) // SUB
        part = cur[start:end, :].reshape(n, SUB, LOCAL_ROWS)
        for s in range(SUB):
            part = part - fw_t[start:end, low + s : low + s + 1].reshape(n, SUB, 1) * errors[s][None]
        cur[start:end, :] = part.reshape(n * SUB, LOCAL_ROWS)
        start = end
    if block_end == low + SUB and block_end < WIN:
        b = block_end - BLOCK
        cur[block_end:, :] = cur[block_end:, :] - jnp.dot(
            fw_t[block_end:, b:block_end], err[b:block_end, :],
            precision=lax.Precision.HIGHEST, preferred_element_type=F32,
        )


def compensate(rest, blocks, half, err_half):
    factor = blocks[:, half * 8 : half * 8 + 8, :].reshape(WIN, blocks.shape[2])
    change = lax.dot_general(
        factor, err_half, (((0,), (0,)), ((), ())), preferred_element_type=F32
    )
    return (rest.astype(F32) - change[: rest.shape[0]]).astype(BF16)


def kernel(
    ids_hbm, calib_hbm, keep_hbm, ww_hbm, rest_hbm, fw_hbm, fr_hbm,
    pruned_out, rest_out, hess_out, outs_out, fac, err_half,
    ids, cal, kp, ww, fw, fw_s, fr, fr_block, xin, x_t, cur, scaled_drop, err, err_blocks, fw_t, x_half, local_outs, z_relay, x_relay,
    gram, gram_half, relay_in, relay_out, from_left, from_right, peer_out, peer_in,
    load_sem, f_send, f_recv, pair_recv, scat_send, scat_recv, xz_send, xz_recv, xx_send, xx_recv, xp_sem,
    o_send, o_recv, relay_recv, h_send, h_recv,
):
    tok, row = lax.axis_index("tok"), lax.axis_index("row")
    x, h, c = row // 8, (row // 2) % 4, row % 2
    l, y = tok // 4, tok % 4
    chip = x * 4 + h

    def row_of(px, ph, pc):
        return ((px + 4) % 4) * 8 + ((ph + 4) % 4) * 2 + pc

    def remote(src, dst, ssem, rsem, to_row=None, to_tok=None):
        return pltpu.make_async_remote_copy(
            src_ref=src, dst_ref=dst, send_sem=ssem, recv_sem=rsem,
            device_id=(tok if to_tok is None else to_tok, row if to_row is None else to_row),
            device_id_type=MESH,
        )

    loads = [
        pltpu.make_async_copy(s, d, load_sem.at[i])
        for i, (s, d) in enumerate(
            [(fr_hbm, fr), (calib_hbm, cal), (ww_hbm, ww), (keep_hbm, kp), (fw_hbm, fw), (ids_hbm, ids), (rest_hbm, rest_out), (fw_hbm, fw_s)]
        )
    ]
    for load in loads[:6] + loads[7:]:
        load.start()

    barrier = pltpu.get_barrier_semaphore()

    def greet(d, carry):
        pl.semaphore_signal(barrier, inc=1, device_id=(tok, (row + d) % N_ROW), device_id_type=MESH)
        return carry

    lax.fori_loop(1, N_ROW, greet, 0)
    up_tok, down_tok, other_tok = l * 4 + (y + 1) % 4, l * 4 + (y + 3) % 4, (1 - l) * 4 + y
    for peer in (up_tok, down_tok, other_tok):
        pl.semaphore_signal(barrier, inc=1, device_id=(peer, row), device_id_type=MESH)
    pl.semaphore_wait(barrier, N_ROW - 1 + 3)

    is_source = row == 0

    def scatter(r):
        first = pl.multiple_of((r % 2) * 256 + (r // 2) * 16, 16)
        return remote(
            cal.at[pl.ds(first, 16), pl.ds(0, WIN)], xin.at[r % 2, r // 2], scat_send.at[r], scat_recv.at[0], to_row=r
        )

    loads[0].wait()
    fr_block[0:8, :] = fr[:, 0:HALF]
    fr_block[8:16, HALF - 128 :] = jnp.zeros((8, 128), F32)
    fr_block[8:16, 0 : REST - HALF] = fr[:, HALF:REST]
    fac[c * CHIPS + chip] = fr_block[...].astype(BF16)

    def f_copy(p, number, slot, to_row, piece=None):
        first, size = p * PHASE_COLS, PHASE_COLS
        if piece is not None:
            first, size = first + piece * PIECE, PIECE
        ref = fac.at[c * CHIPS + slot, :, pl.ds(first, size)]
        rsem = pair_recv.at[p] if number >= PAIR_FIRST else f_recv.at[p, number]
        return remote(ref, ref, f_send.at[0], rsem, to_row=to_row)

    x_up, x_down = row_of(x + 1, h, c), row_of(x - 1, h, c)
    z_up, z_down = row_of(x, h + 1, c), row_of(x, h - 1, c)
    pair = row_of(x, h, 1 - c)
    z_slots = [h, (h + 3) % 4, (h + 1) % 4, (h + 2) % 4]
    x_slots = [x, (x + 3) % 4, (x + 1) % 4, (x + 2) % 4]

    def f_start(*args, **kw):
        f_copy(*args, **kw).start()

    def f_from_z(p, j):
        slot = x * 4 + z_slots[j]
        if j == 1:
            f_start(p, Z_UP_PIECE, slot, z_up, piece=0)
        if j == 2:
            f_start(p, Z_DOWN_PIECE, slot, z_down, piece=1)
        f_start(p, X_FIRST + 4 * j, slot, x_up)
        f_start(p, X_FIRST + 4 * j + 1, slot, x_down)
        f_start(p, PAIR_FIRST + j, slot, pair)

    def f_own_along_z(p):
        f_start(p, Z_UP, chip, z_up)
        f_start(p, Z_DOWN, chip, z_down)

    def f_z_neighbours(p):
        f_copy(p, Z_UP, x * 4 + z_slots[1], z_up).wait_recv()
        f_from_z(p, 1)
        f_copy(p, Z_DOWN, x * 4 + z_slots[2], z_down).wait_recv()
        f_from_z(p, 2)

    def f_z_opposite(p):
        slot = x * 4 + z_slots[3]
        f_copy(p, Z_UP_PIECE, slot, z_up, piece=0).wait_recv()
        f_copy(p, Z_DOWN_PIECE, slot, z_down, piece=1).wait_recv()
        f_from_z(p, 3)

    def f_x_neighbours(p, j):
        n = X_FIRST + 4 * j
        slot = x_slots[1] * 4 + z_slots[j]
        f_copy(p, n, slot, x_up).wait_recv()
        f_start(p, n + 2, slot, x_up, piece=0)
        f_start(p, PAIR_FIRST + 4 + j, slot, pair)
        slot = x_slots[2] * 4 + z_slots[j]
        f_copy(p, n + 1, slot, x_down).wait_recv()
        f_start(p, n + 3, slot, x_down, piece=1)
        f_start(p, PAIR_FIRST + 8 + j, slot, pair)

    def f_x_opposite(p, j):
        n = X_FIRST + 4 * j
        slot = x_slots[3] * 4 + z_slots[j]
        f_copy(p, n + 2, slot, x_up, piece=0).wait_recv()
        f_copy(p, n + 3, slot, x_down, piece=1).wait_recv()
        f_start(p, PAIR_FIRST + 12 + j, slot, pair)

    def f_pair_wait(p):
        ref = fac.at[pl.ds((1 - c) * CHIPS, CHIPS), :, pl.ds(p * PHASE_COLS, PHASE_COLS)]
        remote(ref, ref, f_send.at[0], pair_recv.at[p], to_row=pair).wait_recv()

    loads[1].wait()

    @pl.when(is_source)
    def _():
        def send(r, carry):
            scatter(r).start()
            return carry

        lax.fori_loop(1, N_ROW, send, 0)
        xin[0, 0] = cal[0:16, 0:WIN]

    def xz_copy(d):
        ref = xin.at[c, chip]
        return remote(ref, ref, xz_send.at[d], xz_recv.at[d], to_row=row_of(x, h + d, c))

    def xx_copy(d):
        ref = xin.at[c, pl.ds(x * 4, 4)]
        return remote(ref, ref, xx_send.at[d], xx_recv.at[d], to_row=row_of(x + d, h, c))

    xp_copy = remote(xin.at[c], xin.at[c], xp_sem.at[0], xp_sem.at[1], to_row=pair)

    def inputs_along_z():
        @pl.when(jnp.logical_not(is_source))
        def _():
            ref = xin.at[c, chip]
            remote(ref, ref, scat_send.at[0], scat_recv.at[0], to_row=pair).wait_recv()

        for d in (1, 3, 2):
            xz_copy(d).start()

    def inputs_along_x():
        for d in (1, 3, 2):
            ref = xin.at[c, x * 4 + (h + 4 - d) % 4]
            remote(ref, ref, xz_send.at[d], xz_recv.at[d], to_row=row_of(x, h + d, c)).wait_recv()
        for d in (1, 3, 2):
            xx_copy(d).start()

    def inputs_to_pair():
        for d in (1, 3, 2):
            ref = xin.at[c, pl.ds(((x + 4 - d) % 4) * 4, 4)]
            remote(ref, ref, xx_send.at[d], xx_recv.at[d], to_row=row_of(x + d, h, c)).wait_recv()
        xp_copy.start()

    def inputs_complete():
        remote(xin.at[1 - c], xin.at[1 - c], xp_sem.at[0], xp_sem.at[1], to_row=pair).wait_recv()
        loads[5].wait()
        live = jnp.where(ids[...] != 1, 1.0, 0.0)
        live_t = jnp.concatenate([live, jnp.zeros((4, 128), F32)], axis=0).T
        x_parts = []
        for s in range(4):
            part = xin[s // 2, (s % 2) * 8 : (s % 2) * 8 + 8].reshape(128, WIN).astype(F32)
            x_parts.append(part * live_t[:, s : s + 1])
        x_all = jnp.concatenate(x_parts, axis=0)
        x_t[...] = x_all.T.astype(BF16)
        x_half[...] = x_all.astype(BF16)

    def h_copy(number, src, dst, to_tok):
        return remote(src, dst, h_send.at[number], h_recv.at[number], to_tok=to_tok)

    h_copies = [
        h_copy(0, gram_half.at[(y + 2) % 4], relay_in.at[0], up_tok),
        h_copy(1, gram_half.at[4 + (y + 2) % 4], relay_in.at[1], down_tok),
        h_copy(2, gram_half.at[4 + (y + 1) % 4], from_left.at[1], up_tok),
        h_copy(3, gram_half.at[(y + 3) % 4], from_right.at[0], down_tok),
        h_copy(4, relay_out.at[0], from_left.at[0], up_tok),
        h_copy(5, relay_out.at[1], from_right.at[1], down_tok),
        h_copy(6, peer_out, peer_in, other_tok),
    ]

    def hessian_begin():
        @pl.loop(0, FEATURES // 256)
        def _(i):
            cols = pl.ds(pl.multiple_of(i * 256, 256), 256)
            part = jnp.dot(x_t[...], cal[:, cols], preferred_element_type=F32).reshape(N_TOK, 32, 256)
            gram[:, :, cols] = part
            gram_half[:, :, cols] = part.astype(BF16)

        for i in range(4):
            h_copies[i].start()

    def hessian_relay():
        h_copies[0].wait_recv()
        relay_out[0] = (relay_in[0].astype(F32) + gram[(y + 1) % 4]).astype(BF16)
        h_copies[4].start()
        h_copies[1].wait_recv()
        relay_out[1] = (relay_in[1].astype(F32) + gram[4 + (y + 3) % 4]).astype(BF16)
        h_copies[5].start()

    def hessian_peer():
        for i in range(2, 6):
            h_copies[i].wait_recv()
        peer_out[...] = (
            gram[(1 - l) * 4 + y] + from_left[1 - l].astype(F32) + from_right[1 - l].astype(F32)
        ).astype(BF16)
        h_copies[6].start()

    def hessian_end():
        h_copies[6].wait_recv()
        total = gram[l * 4 + y] + from_left[l].astype(F32) + from_right[l].astype(F32) + peer_in[...].astype(F32)
        hess_out[...] = total * (2.0 / TOKENS)

    def out_cols(sender):
        return pl.ds(pl.multiple_of(sender * LOCAL_ROWS, 128), LOCAL_ROWS)

    my_cols = out_cols(row)
    relays = [
        remote(local_outs.at[:, 3, 0], z_relay.at[0], o_send.at[0], relay_recv.at[0], to_row=z_up),
        remote(local_outs.at[:, 3, 1], z_relay.at[1], o_send.at[0], relay_recv.at[1], to_row=z_down),
        remote(local_outs.at[2, pl.ds(0, 3), 0], x_relay.at[0], o_send.at[0], relay_recv.at[2], to_row=x_up),
        remote(local_outs.at[2, pl.ds(0, 3), 1], x_relay.at[1], o_send.at[0], relay_recv.at[3], to_row=x_down),
    ]

    def send_outputs():
        found = jnp.dot(
            x_half[...], cur[...].astype(BF16), preferred_element_type=F32
        ).astype(BF16).reshape(N_ROW, 16, LOCAL_ROWS)
        for r in range(N_ROW):
            local_outs[(r // 8 - x + 4) % 4, ((r // 2) % 4 - h + 5) % 4, r % 2] = found[r]
        for relay in relays:
            relay.start()
        for dx in (1, 3, 0):
            for dh in (1, -1, 0):
                for dc in (0, 1):
                    if (dx, dh, dc) != (0, 0, 0):
                        oc = (c + dc) % 2
                        remote(
                            local_outs.at[dx, dh + 1, oc], outs_out.at[:, my_cols], o_send.at[0], o_recv.at[0],
                            to_row=row_of(x + dx, h + dh, oc),
                        ).start()

    def pass_on_z(way):
        relays[way].wait_recv()
        step = 1 if way == 0 else -1
        sender = row_of(x, h - step, c)
        for dx in range(4):
            remote(
                z_relay.at[way, dx], outs_out.at[:, out_cols(sender)], o_send.at[1], o_recv.at[0],
                to_row=row_of(x + dx, h + step, way),
            ).start()

    def pass_on_x(way):
        relays[2 + way].wait_recv()
        step = 1 if way == 0 else -1
        sender = row_of(x - step, h, c)
        for dh in (-1, 0, 1):
            remote(
                x_relay.at[way, dh + 1], outs_out.at[:, out_cols(sender)], o_send.at[2], o_recv.at[0],
                to_row=row_of(x + step, h + dh, way),
            ).start()

    arrived = outs_out.at[:, pl.ds(0, (N_ROW - 1) * LOCAL_ROWS)]

    def outputs_complete():
        remote(arrived, arrived, o_send.at[0], o_recv.at[0], to_row=pair).wait_recv()

    def prune(first, last):
        for k in range(first, last):
            prune_tile(k, cur, scaled_drop, fw_t, fw_s, err, err_blocks)

    def pruned_results():
        outs_out[:, my_cols] = local_outs[0, 1, c]
        pruned_out[...] = cur[...].T
        err_half[...] = err_blocks[...].astype(BF16)

    def update(p):
        for half in range(2):

            @pl.loop(0, PHASE_COLS // STEP)
            def _(i, half=half, p=p):
                first = pl.multiple_of(p * PHASE_COLS + i * STEP, STEP)
                rows = pl.ds(pl.multiple_of(half * HALF + first, STEP), STEP)
                rest_out[rows, :] = compensate(rest_out[rows, :], fac[:, :, pl.ds(first, STEP)], half, err_half[...])

    f_from_z(0, 0)
    loads[6].start()
    for i in (2, 3, 4, 7):
        loads[i].wait()
    prune_prepare(ww, kp, fw, cur, scaled_drop, fw_t)
    inputs_along_z()
    f_own_along_z(0)
    prune(0, 10)
    inputs_along_x()
    f_x_neighbours(0, 0)
    prune(10, 22)
    inputs_to_pair()
    prune(22, 32)
    f_z_neighbours(0)
    inputs_complete()
    send_outputs()
    hessian_begin()
    f_z_opposite(0)
    f_x_opposite(0, 0)
    f_x_neighbours(0, 1)
    pruned_results()
    pass_on_z(1)
    f_x_neighbours(0, 2)
    pass_on_z(0)
    hessian_relay()
    f_x_neighbours(0, 3)
    pass_on_x(1)
    pass_on_x(0)
    hessian_peer()
    f_x_opposite(0, 1)
    f_x_opposite(0, 2)
    f_x_opposite(0, 3)
    outputs_complete()
    hessian_end()
    f_pair_wait(0)
    loads[6].wait()

    remote(arrived, arrived, o_send.at[0], o_recv.at[0], to_row=pair).wait_send()
    remote(z_relay, z_relay, o_send.at[1], o_recv.at[0], to_row=pair).wait_send()
    remote(x_relay, x_relay, o_send.at[2], o_recv.at[0], to_row=pair).wait_send()

    @pl.when(is_source)
    def _():
        def left(r, carry):
            scatter(r).wait_send()
            return carry

        lax.fori_loop(1, N_ROW, left, 0)

    for d in (1, 3, 2):
        xz_copy(d).wait_send()
        xx_copy(d).wait_send()
    xp_copy.wait_send()
    for copy in h_copies:
        copy.wait_send()
    sent = fac.at[pl.ds(0, 31)]
    remote(sent, sent, f_send.at[0], pair_recv.at[0], to_row=pair).wait_send()


def finish_kernel(
    pruned, rest, hess, outs, fac, err_half,
    pruned_hbm, rest_hbm, hess_hbm, outs_hbm,
    updated, sem,
):
    copies = [
        pltpu.make_async_copy(pruned, pruned_hbm, sem.at[0]),
        pltpu.make_async_copy(hess, hess_hbm, sem.at[1]),
        pltpu.make_async_copy(outs, outs_hbm, sem.at[2]),
    ]
    last = HALF - PHASE_COLS
    if last > 0:
        for half in range(2):
            rows = pl.ds(half * HALF, last)
            copies.append(pltpu.make_async_copy(rest.at[rows], rest_hbm.at[rows], sem.at[3 + half]))
    for copy in copies:
        copy.start()
    for half in range(2):
        for i in range(PHASE_COLS // STEP):
            first = last + i * STEP
            start = half * HALF + first
            count = min(STEP, REST - start)
            part = rest[start : start + count, :]
            at = half * PHASE_COLS + i * STEP
            updated[at : at + count, :] = compensate(part, fac[:, :, first : first + STEP], half, err_half[...])
            copy = pltpu.make_async_copy(
                updated.at[pl.ds(at, count)], rest_hbm.at[pl.ds(start, count)], sem.at[5 + half * (PHASE_COLS // STEP) + i]
            )
            copy.start()
            copies.append(copy)
    for copy in copies:
        copy.wait()


def on_device(token_ids, calib_input, keep_mask, weight_window, weight_rest, factor_window, factor_rest):
    vmem, dma = pltpu.VMEM, pltpu.SemaphoreType.DMA
    slab = (32, FEATURES)
    in_hbm = [
        pltpu.with_memory_space_constraint(a, pltpu.HBM)
        for a in (
            token_ids.reshape(4, 128), calib_input, keep_mask, weight_window, weight_rest.T, factor_window, factor_rest
        )
    ]
    shapes = [
        ((LOCAL_ROWS, WIN), F32),
        ((REST, LOCAL_ROWS), BF16),
        (slab, F32),
        ((16, N_ROW * LOCAL_ROWS), BF16),
    ]
    held = pl.pallas_call(
        kernel,
        out_shape=tuple(
            vmem(*s) for s in shapes + [((2 * CHIPS, 16, HALF), BF16), ((WIN, LOCAL_ROWS), BF16)]
        ),
        in_specs=[pl.BlockSpec(memory_space=pltpu.HBM)] * 7,
        out_specs=[pl.BlockSpec(memory_space=vmem)] * 6,
        scratch_shapes=[
            vmem((4, 128), jnp.int32),
            vmem((LOCAL_TOKENS, FEATURES), BF16),
            vmem((LOCAL_ROWS, WIN), jnp.int32),
            vmem((LOCAL_ROWS, WIN), F32),
            vmem((WIN, WIN), F32),
            pltpu.SMEM((WIN, WIN), F32),
            vmem((8, REST), F32),
            vmem((16, HALF), F32),
            vmem((2, CHIPS, 16, WIN), BF16),
            vmem((WIN, LOCAL_TOKENS), BF16),
            vmem((WIN, LOCAL_ROWS), F32),
            vmem((WIN, LOCAL_ROWS), F32),
            vmem((WIN, LOCAL_ROWS), F32),
            vmem((WIN, LOCAL_ROWS), F32),
            vmem((WIN, WIN), F32),
            vmem((LOCAL_TOKENS, WIN), BF16),
            vmem((4, 4, 2, 16, LOCAL_ROWS), BF16),
            vmem((2, 4, 16, LOCAL_ROWS), BF16),
            vmem((2, 3, 16, LOCAL_ROWS), BF16),
            vmem((N_TOK,) + slab, F32),
            vmem((N_TOK,) + slab, BF16),
            vmem((2,) + slab, BF16),
            vmem((2,) + slab, BF16),
            vmem((2,) + slab, BF16),
            vmem((2,) + slab, BF16),
            vmem(slab, BF16),
            vmem(slab, BF16),
            dma((8,)),
            dma((1,)),
            dma((PHASES, F_MESSAGES)),
            dma((PHASES,)),
            dma((N_ROW,)),
            dma((1,)),
            dma((4,)),
            dma((4,)),
            dma((4,)),
            dma((4,)),
            dma((2,)),
            dma((3,)),
            dma((1,)),
            dma((4,)),
            dma((7,)),
            dma((7,)),
        ],
        compiler_params=pltpu.CompilerParams(
            collective_id=0, has_side_effects=True, vmem_limit_bytes=32 * 1024 * 1024
        ),
        cost_estimate=pl.CostEstimate(flops=2_000_000_000, bytes_accessed=16_000_000, transcendentals=0),
    )(*in_hbm)
    pruned, rest_t, hess, outs = pl.pallas_call(
        finish_kernel,
        out_shape=tuple(jax.ShapeDtypeStruct(*s) for s in shapes),
        in_specs=[pl.BlockSpec(memory_space=vmem)] * 6,
        out_specs=[pl.BlockSpec(memory_space=pltpu.HBM)] * 4,
        scratch_shapes=[
            vmem((2 * PHASE_COLS, LOCAL_ROWS), BF16),
            dma((5 + 2 * (PHASE_COLS // STEP),)),
        ],
        compiler_params=pltpu.CompilerParams(vmem_limit_bytes=32 * 1024 * 1024),
        cost_estimate=pl.CostEstimate(flops=600_000_000, bytes_accessed=12_000_000, transcendentals=0),
    )(*[pltpu.with_memory_space_constraint(a, vmem) for a in held])
    return pruned, rest_t.T, hess, outs


def solution(mesh):
    return jax.shard_map(
        on_device,
        mesh=mesh,
        in_specs=(
            P("tok"),
            P("tok", "row"),
            P("row", None),
            P("row", None),
            P("row", "tok"),
            P(),
            P("row", "tok"),
        ),
        out_specs=(P("row", None), P("row", "tok"), P("tok", "row"), P(("tok", "row"), None)),
        check_vma=False,
    )
```
